32 devices in a mesh: row: 4 (over x, core), col: 8 (over z, y).
Axes of the slice: x: 2, y: 2, z: 4, core: 2. Of those that a mesh axis runs over, the one named last changes fastest.
Arguments:
- left_tiles: bfloat16 [4, 8, 6, 128, 128], P('row', 'col'), may hold values from -6 to 6
- left_index: int32 [4, 8, 6], replicated, may hold values from 0 to 16, as said below
- right_tiles: bfloat16 [4, 8, 2, 3, 128, 128], P('row', 'col'), may hold values from -0.125 to 0.125
- right_index: int32 [4, 8, 2, 3], replicated, may hold values from 0 to 8, as said below
Outputs:
- product: bfloat16 [1024, 1024], P('row', 'col')
The draws below stay inside these ranges and needn't reach their ends.
Inputs may be any that keep to these rules, and one draw needn't show every extreme that they name: `left_index`: in each block r, c the used slots come first and name distinct positions i * 8 + k; unused slots hold 16. Every block uses at least a third of its 6 slots, some block uses all of them and some block leaves slots unused. `right_index`: in each half block r, c, h the used slots come first and name distinct positions k + j; unused slots hold 8. Every half block uses at least a third of its 3 slots, some uses all of them and some leaves slots unused.
All inputs are finite; a program needn't handle non-finite values.
Results may differ from the reference program's by a relative error of at most 0.001.
Values may be sent and summed in bfloat16 or wider, within the bound.
No kernel may reach another device: no remote copies, remote signals or barrier semaphores. Data moves between devices by JAX's collectives and lax.ppermute only.
A program may use at most 64 MiB of HBM per device.

```python
import jax
import jax.numpy as jnp
from jax import lax

TILE = 128
KT = 8
RT = 2
CT = 1
LCAP = 6
RCAP = 3
N_ROW = 4
N_COL = 8


def occupancy(key, blocks, positions, capacity):
    lowest = max(1, capacity // 3)
    keys = jax.random.split(key, 4)
    counts = jax.random.randint(keys[0], (blocks,), lowest, capacity + 1)
    fullest = jax.random.randint(keys[1], (), 0, blocks)
    sparsest = (fullest + 1 + jax.random.randint(keys[2], (), 0, blocks - 1)) % blocks
    block_ids = jnp.arange(blocks)
    counts = jnp.where(block_ids == fullest, capacity, counts)
    counts = jnp.where(block_ids == sparsest, lowest, counts)
    orders = jax.vmap(lambda one_key: jax.random.permutation(one_key, positions))(jax.random.split(keys[3], blocks))
    orders = orders[:, :capacity]
    slot_ids = jnp.arange(capacity)
    return jnp.where(slot_ids[None, :] < counts[:, None], orders, positions).astype(jnp.int32)


def draw_left_index(key, part):
    key = jax.random.fold_in(key, 17)
    return occupancy(key, N_ROW * N_COL, RT * KT, LCAP).reshape(N_ROW, N_COL, LCAP)


def draw_right_index(key, part):
    key = jax.random.fold_in(key, 29)
    return occupancy(key, N_ROW * N_COL * 2, KT * CT, RCAP).reshape(N_ROW, N_COL, 2, RCAP)


def shard_levels(stream_key, shape, cuts, smallest, high):
    factor_of = 1.0
    for axis_at, blocks in cuts:
        steps = jax.random.uniform(jax.random.fold_in(jax.random.fold_in(stream_key, 6), axis_at), (blocks,), jnp.float32, smallest / len(cuts), high / len(cuts))
        factor_of = factor_of * jnp.repeat(jnp.exp(steps), shape[axis_at] // blocks).reshape((-1,) + (1,) * (len(shape) - 1 - axis_at))
    return factor_of


def scatter_about(rng, extent, spread, bound, cuts=(), kind=jnp.bfloat16):
    entries = spread * jax.random.normal(rng, extent, jnp.float32)
    if cuts:
        entries = entries * shard_levels(rng, extent, cuts, -0.22, 0.18)
    return jnp.clip(entries, -bound, bound).astype(kind)


def setup_inputs(seed: int = 0) -> dict:
    splits = jax.random.split(jax.random.key(seed), 5)
    return {
        "left_tiles": scatter_about(splits[0], (N_ROW, N_COL, LCAP, TILE, TILE), 1.0, 6.0, ((0, 4), (1, 8))),
        "left_index": draw_left_index(jax.random.fold_in(splits[4], 71), 0),
        "right_tiles": scatter_about(splits[2], (N_ROW, N_COL, 2, RCAP, TILE, TILE), (16 * TILE) ** -0.5, 0.125, ((0, 4), (1, 8))),
        "right_index": draw_right_index(jax.random.fold_in(splits[4], 71), 0),
    }


def partial_product(left_cur, left_slots, right_cur, right_slots):
    tile = left_cur.shape[-1]
    right_onehot = (right_slots[:, None] == jnp.arange(KT * CT, dtype=jnp.int32)[None, :]).astype(jnp.float32)
    right_dense = jnp.einsum("sp,sab->pab", right_onehot, right_cur)
    right_strips = right_dense.reshape(KT, CT, tile, tile).transpose(0, 2, 1, 3).reshape(KT, tile, CT * tile)
    inner_onehot = ((left_slots % KT)[:, None] == jnp.arange(KT, dtype=jnp.int32)[None, :]).astype(jnp.float32)
    chosen = jnp.einsum("sk,kbc->sbc", inner_onehot, right_strips)
    products = jnp.einsum("sab,sbc->sac", left_cur, chosen)
    row_onehot = ((left_slots // KT)[:, None] == jnp.arange(RT, dtype=jnp.int32)[None, :]).astype(jnp.float32)
    return jnp.einsum("si,sac->iac", row_onehot, products)


def reference(left_tiles, left_index, right_tiles, right_index):
    tile = left_tiles.shape[-1]

    def out_block(flat_index):
        row_pos = flat_index // N_COL
        col_pos = flat_index % N_COL

        def accumulate(inner_piece, total):
            left_cur = left_tiles[row_pos, inner_piece].astype(jnp.float32)
            left_slots = left_index[row_pos, inner_piece]
            right_cur = right_tiles[inner_piece // 2, col_pos, inner_piece % 2].astype(jnp.float32)
            right_slots = right_index[inner_piece // 2, col_pos, inner_piece % 2]
            return total + partial_product(left_cur, left_slots, right_cur, right_slots)

        start = jnp.zeros((RT, tile, CT * tile), jnp.float32)
        total = lax.fori_loop(0, N_COL, accumulate, start)
        return total.reshape(RT * tile, CT * tile)

    blocks = lax.map(out_block, jnp.arange(N_ROW * N_COL, dtype=jnp.int32))
    whole = blocks.reshape(N_ROW, N_COL, RT * tile, CT * tile).transpose(0, 2, 1, 3)
    return whole.reshape(N_ROW * RT * tile, N_COL * CT * tile).astype(jnp.bfloat16)
```

```python
import jax
import jax.numpy as jnp
from jax import lax
from jax.experimental import pallas as pl
from jax.experimental.pallas import tpu as pltpu
from jax.sharding import PartitionSpec as P

KT = 8
RT = 2


def multiply(row, col, left_index, right_index, left, right):
    pieces, left_slots, tile, _ = left.shape
    right_slots = right.shape[1]

    def kernel(row_ref, col_ref, li_ref, ri_ref, left_ref, right_ref, out_ref, total):
        r = row_ref[0]
        c = col_ref[0]
        total[...] = jnp.zeros_like(total)

        @pl.loop(0, pieces)
        def _(p):
            for s in range(left_slots):
                place = li_ref[r, p, s]
                k = place % KT
                found = jnp.int32(right_slots)
                for t in range(right_slots):
                    found = jnp.where(ri_ref[p // 2, c, p % 2, t] == k, t, found)

                @pl.when(jnp.logical_and(place < RT * KT, found < right_slots))
                def _():
                    i = place // KT
                    total[i] += jnp.dot(
                        left_ref[p, s], right_ref[p, found], preferred_element_type=jnp.float32
                    )

        out_ref[...] = total[...].reshape(RT * tile, tile).astype(out_ref.dtype)

    smem = pl.BlockSpec(memory_space=pltpu.SMEM)
    vmem = pl.BlockSpec(memory_space=pltpu.VMEM)
    return pl.pallas_call(
        kernel,
        out_shape=jax.ShapeDtypeStruct((RT * tile, tile), jnp.bfloat16),
        in_specs=[smem, smem, smem, smem, vmem, vmem],
        out_specs=vmem,
        scratch_shapes=[pltpu.VMEM((RT, tile, tile), jnp.float32)],
        compiler_params=pltpu.CompilerParams(vmem_limit_bytes=32 * 1024 * 1024),
    )(row, col, left_index, right_index, left, right)


def shards(left_tiles, left_index, right_tiles, right_index):
    row = lax.axis_index("row").reshape(1)
    col = lax.axis_index("col").reshape(1)
    left = lax.all_gather(left_tiles[0], "col", axis=0, tiled=True)
    right = lax.all_gather(right_tiles[0, 0], "row", axis=0, tiled=True)
    return multiply(row, col, left_index, right_index, left, right)


def solution(mesh):
    return jax.shard_map(
        shards,
        mesh=mesh,
        in_specs=(
            P("row", "col", None, None, None),
            P(),
            P("row", "col", None, None, None, None),
            P(),
        ),
        out_specs=P("row", "col"),
        check_vma=False,
    )
```

```python
import jax
import jax.numpy as jnp
from jax import lax
from jax.experimental import pallas as pl
from jax.experimental.pallas import tpu as pltpu
from jax.sharding import PartitionSpec as P

KT = 8
RT = 2


def partial_products(place, left_index, right_index, lefts, rights):
    slots, tile, _ = lefts[0].shape
    pairs, right_slots = rights[0].shape[:2]
    inner = len(lefts)

    def kernel(place_ref, li_ref, ri_ref, *refs):
        left_refs, right_refs = refs[:inner], refs[inner : 2 * inner]
        mine_ref, other_ref, total, held = refs[2 * inner :]
        row, z, y = place_ref[0], place_ref[1], place_ref[2]
        total[...] = jnp.zeros_like(total)
        for t in range(inner):
            held[lax.rem(row - t + inner, inner)] = right_refs[t][...]

        for s in range(inner):
            zp = lax.rem(z - s + inner, inner)

            @pl.loop(0, slots)
            def _(slot):
                at = li_ref[row, 2 * zp + y, slot]
                k = lax.rem(at, KT)
                i = lax.div(at, KT)
                for j in range(pairs):
                    c = 2 * z + (y if j == 0 else 1 - y)
                    found = jnp.int32(right_slots)
                    for t in range(right_slots):
                        found = jnp.where(ri_ref[zp, c, y, t] == k, t, found)

                    @pl.when(jnp.logical_and(at < RT * KT, found < right_slots))
                    def _():
                        total[j, i] += jnp.dot(
                            left_refs[s][slot],
                            held[zp, j, found],
                            preferred_element_type=jnp.float32,
                        )

        mine_ref[...] = total[0].reshape(RT * tile, tile)
        other_ref[...] = total[1].reshape(RT * tile, tile)

    smem = pl.BlockSpec(memory_space=pltpu.SMEM)
    vmem = pl.BlockSpec(memory_space=pltpu.VMEM)
    return pl.pallas_call(
        kernel,
        out_shape=[jax.ShapeDtypeStruct((RT * tile, tile), jnp.float32)] * 2,
        in_specs=[smem] * 3 + [vmem] * (2 * inner),
        out_specs=[vmem] * 2,
        scratch_shapes=[
            pltpu.VMEM((pairs, RT, tile, tile), jnp.float32),
            pltpu.VMEM((inner, pairs, right_slots, tile, tile), jnp.bfloat16),
        ],
        compiler_params=pltpu.CompilerParams(vmem_limit_bytes=32 * 1024 * 1024),
    )(place, left_index, right_index, *lefts, *rights)


def shards(left_tiles, left_index, right_tiles, right_index):
    row_count = lax.axis_size("row")
    col_count = lax.axis_size("col")
    row = lax.axis_index("row")
    col = lax.axis_index("col")
    z, y = col // 2, col % 2
    left = left_tiles[0, 0]
    right = right_tiles[0, 0]

    swap = [(c, c ^ 1) for c in range(col_count)]
    given = lax.dynamic_index_in_dim(right, 1 - y, 0, keepdims=True)
    kept = lax.dynamic_index_in_dim(right, y, 0, keepdims=True)
    taken = lax.ppermute(given, "col", swap)

    lefts = [left]
    for s in range(1, col_count // 2):
        route = [(c, (c + 2 * s) % col_count) for c in range(col_count)]
        lefts.append(lax.ppermute(left, "col", route))

    halves = jnp.concatenate([kept, taken])
    rights = [halves]
    for t in range(1, row_count):
        route = [(r, (r + t) % row_count) for r in range(row_count)]
        rights.append(lax.ppermute(halves, "row", route))

    place = jnp.stack([row, z, y])
    mine, other = partial_products(place, left_index, right_index, lefts, rights)
    return (mine + lax.ppermute(other, "col", swap)).astype(jnp.bfloat16)


def solution(mesh):
    return jax.shard_map(
        shards,
        mesh=mesh,
        in_specs=(
            P("row", "col", None, None, None),
            P(),
            P("row", "col", None, None, None, None),
            P(),
        ),
        out_specs=P("row", "col"),
        check_vma=False,
    )
```

```python
import jax
import jax.numpy as jnp
from jax import lax
from jax.experimental import pallas as pl
from jax.experimental.pallas import tpu as pltpu
from jax.sharding import PartitionSpec as P

KT = 8
RT = 2
SMEM = pl.BlockSpec(memory_space=pltpu.SMEM)
VMEM = pl.BlockSpec(memory_space=pltpu.VMEM)


def add_block(li_ref, ri_ref, row, zp, y, column, left_ref, right_at, total_ref):
    slots, tile, _ = left_ref.shape
    right_slots = ri_ref.shape[-1]

    @pl.loop(0, slots)
    def _(slot):
        at = li_ref[row, 2 * zp + y, slot]
        k = lax.rem(at, KT)
        i = lax.div(at, KT)
        found = jnp.int32(right_slots)
        for t in range(right_slots):
            found = jnp.where(ri_ref[zp, column, y, t] == k, t, found)

        @pl.when(jnp.logical_and(at < RT * KT, found < right_slots))
        def _():
            rows = pl.ds(pl.multiple_of(i * tile, tile), tile)
            total_ref[rows, :] += jnp.dot(
                left_ref[slot], right_at(found), preferred_element_type=jnp.float32
            )


def first_products(place, left_index, right_index, lefts, kept, taken):
    slots, tile, _ = lefts[0].shape
    count = len(lefts)
    inner = len(kept)
    right_slots = kept[0].shape[1]

    def kernel(place_ref, li_ref, ri_ref, *refs):
        left_refs = refs[:count]
        sides = refs[count : count + inner], refs[count + inner : count + 2 * inner]
        totals = refs[count + 2 * inner : count + 2 * inner + 2]
        lasts = refs[count + 2 * inner + 2 : count + 2 * inner + 4]
        held = refs[-1]
        row, z, y = place_ref[0], place_ref[1], place_ref[2]
        for side in range(2):
            column = 2 * z + (y if side == 0 else 1 - y)
            totals[side][...] = jnp.zeros_like(totals[side])
            for t in range(inner):
                held[side, row ^ t] = sides[side][t][0]
            for s in range(count):
                zp = z ^ s
                add_block(
                    li_ref, ri_ref, row, zp, y, column, left_refs[s],
                    lambda found, side=side, zp=zp: held[side, zp, found], totals[side],
                )
            lasts[side][...] = held[side, z ^ (inner - 1)]

    return pl.pallas_call(
        kernel,
        out_shape=[jax.ShapeDtypeStruct((RT * tile, tile), jnp.float32)] * 2
        + [jax.ShapeDtypeStruct((right_slots, tile, tile), jnp.bfloat16)] * 2,
        in_specs=[SMEM] * 3 + [VMEM] * (count + 2 * inner),
        out_specs=[VMEM] * 4,
        scratch_shapes=[pltpu.VMEM((2, inner, right_slots, tile, tile), jnp.bfloat16)],
        compiler_params=pltpu.CompilerParams(vmem_limit_bytes=32 * 1024 * 1024),
        cost_estimate=pl.CostEstimate(
            flops=4 * count * slots * tile**3, bytes_accessed=2 * count * slots * tile**2, transcendentals=0
        ),
    )(place, left_index, right_index, *lefts, *kept, *taken)


def last_products(place, left_index, right_index, left, right, total, side, inner):
    slots, tile, _ = left.shape

    def kernel(place_ref, li_ref, ri_ref, left_ref, right_ref, total_ref, out_ref):
        row, z, y = place_ref[0], place_ref[1], place_ref[2]
        column = 2 * z + (y if side == 0 else 1 - y)
        out_ref[...] = total_ref[...]
        add_block(
            li_ref, ri_ref, row, z ^ (inner - 1), y, column, left_ref,
            lambda found: right_ref[found], out_ref,
        )

    return pl.pallas_call(
        kernel,
        out_shape=jax.ShapeDtypeStruct(total.shape, total.dtype),
        in_specs=[SMEM] * 3 + [VMEM] * 3,
        out_specs=VMEM,
        compiler_params=pltpu.CompilerParams(vmem_limit_bytes=16 * 1024 * 1024),
        cost_estimate=pl.CostEstimate(
            flops=2 * slots * tile**3, bytes_accessed=2 * slots * tile**2, transcendentals=0
        ),
    )(place, left_index, right_index, left, right, total)


def shards(left_tiles, left_index, right_tiles, right_index):
    row_count = lax.axis_size("row")
    col_count = lax.axis_size("col")
    inner = col_count // 2
    row = lax.axis_index("row")
    col = lax.axis_index("col")
    z, y = col >> 1, col & 1
    right = right_tiles[0, 0]

    def across(block, axis, mask):
        route = [(i, i ^ mask) for i in range(lax.axis_size(axis))]
        return lax.ppermute(block, axis, route)

    lefts = {0: left_tiles[0, 0]}
    distance = inner // 2
    while distance:
        for s in sorted(lefts):
            lefts[s ^ distance] = across(lefts[s], "col", 2 * distance)
        distance //= 2

    given = lax.dynamic_index_in_dim(right, 1 - y, 0, keepdims=True)
    own = lax.dynamic_index_in_dim(right, y, 0, keepdims=True)
    swapped = across(given, "col", 1)
    kept = [own] + [across(own, "row", t) for t in range(1, row_count)]
    taken = [swapped] + [across(swapped, "row", t) for t in range(1, row_count)]

    place = jnp.stack([row, z, y])
    where = (place, left_index, right_index)
    early = [lefts[s] for s in range(inner - 1)]
    mine, other, mine_last, other_last = first_products(*where, early, kept, taken)
    final = lefts[inner - 1]
    other = last_products(*where, final, other_last, other, 1, inner)
    coming = across(other, "col", 1)
    mine = last_products(*where, final, mine_last, mine, 0, inner)
    return (mine + coming).astype(jnp.bfloat16)


def solution(mesh):
    return jax.shard_map(
        shards,
        mesh=mesh,
        in_specs=(
            P("row", "col", None, None, None),
            P(),
            P("row", "col", None, None, None, None),
            P(),
        ),
        out_specs=P("row", "col"),
        check_vma=False,
    )
```

```python
import jax
import jax.numpy as jnp
from jax import lax
from jax.experimental import pallas as pl
from jax.experimental.pallas import tpu as pltpu
from jax.sharding import PartitionSpec as P

KT = 8
RT = 2
SMEM = pl.BlockSpec(memory_space=pltpu.SMEM)
VMEM = pl.BlockSpec(memory_space=pltpu.VMEM)


def match(li_ref, ri_ref, row, zp, y, column, slot):
    right_slots = ri_ref.shape[-1]
    at = li_ref[row, 2 * zp + y, slot]
    k = lax.rem(at, KT)
    code = jnp.int32(0)
    for t in range(right_slots):
        code = jnp.where(ri_ref[zp, column, y, t] == k, 1 + lax.div(at, KT) * right_slots + t, code)
    return jnp.where(at < RT * KT, code, 0)


def add_tile(code, left_tile, right_at, right_slots, total_ref):
    tile = total_ref.shape[1]

    @pl.when(code > 0)
    def _():
        i = lax.div(code - 1, right_slots)
        rows = pl.ds(pl.multiple_of(i * tile, tile), tile)
        total_ref[rows, :] += jnp.dot(
            left_tile(), right_at(lax.rem(code - 1, right_slots)), preferred_element_type=jnp.float32
        )


def first_products(place, left_index, right_index, lefts, rights):
    slots, tile, _ = lefts[0].shape
    count = len(lefts)
    inner = len(rights)
    right_slots = rights[0].shape[1]

    def kernel(place_ref, li_ref, ri_ref, *refs):
        left_refs, right_refs = refs[:count], refs[count : count + inner]
        totals = refs[count + inner : count + inner + 2]
        last_ref, codes_ref, held = refs[count + inner + 2 :]
        row, z, y = place_ref[0], place_ref[1], place_ref[2]
        for t in range(inner):
            held[row ^ t] = right_refs[t][...]
        zl = z ^ (inner - 1)
        last_ref[...] = held[zl]
        for side in range(2):
            column = 2 * z + (y if side == 0 else 1 - y)
            totals[side][...] = jnp.zeros_like(totals[side])
            for slot in range(slots):
                codes_ref[side * slots + slot] = match(li_ref, ri_ref, row, zl, y, column, slot)
            for s in range(count):
                zp = z ^ s

                @pl.loop(0, slots)
                def _(slot):
                    add_tile(
                        match(li_ref, ri_ref, row, zp, y, column, slot),
                        lambda: left_refs[s][slot],
                        lambda found: held[zp, side, found],
                        right_slots,
                        totals[side],
                    )

    return pl.pallas_call(
        kernel,
        out_shape=[jax.ShapeDtypeStruct((RT * tile, tile), jnp.float32)] * 2
        + [
            jax.ShapeDtypeStruct((2, right_slots, tile, tile), jnp.bfloat16),
            jax.ShapeDtypeStruct((2 * slots,), jnp.int32),
        ],
        in_specs=[SMEM] * 3 + [VMEM] * (count + inner),
        out_specs=[VMEM] * 3 + [SMEM],
        scratch_shapes=[pltpu.VMEM((inner, 2, right_slots, tile, tile), jnp.bfloat16)],
        compiler_params=pltpu.CompilerParams(vmem_limit_bytes=32 * 1024 * 1024),
        cost_estimate=pl.CostEstimate(
            flops=4 * count * slots * tile**3, bytes_accessed=2 * count * slots * tile**2, transcendentals=0
        ),
    )(place, left_index, right_index, *lefts, *rights)


def last_products(codes, left, right, total, side):
    slots, tile, _ = left.shape
    right_slots = right.shape[1]

    def kernel(codes_ref, left_ref, right_ref, total_ref, out_ref):
        out_ref[...] = total_ref[...]
        for slot in range(slots):
            add_tile(
                codes_ref[side * slots + slot],
                lambda: left_ref[slot],
                lambda found: right_ref[side, found],
                right_slots,
                out_ref,
            )

    return pl.pallas_call(
        kernel,
        out_shape=jax.ShapeDtypeStruct(total.shape, total.dtype),
        in_specs=[SMEM] + [VMEM] * 3,
        out_specs=VMEM,
        compiler_params=pltpu.CompilerParams(vmem_limit_bytes=16 * 1024 * 1024),
        cost_estimate=pl.CostEstimate(
            flops=2 * slots * tile**3, bytes_accessed=2 * slots * tile**2, transcendentals=0
        ),
    )(codes, left, right, total)


def across(block, axis, mask):
    route = [(i, i ^ mask) for i in range(lax.axis_size(axis))]
    return lax.ppermute(block, axis, route)


def gather(block, axis, unit):
    blocks = {0: block}
    distance = lax.axis_size(axis) // unit // 2
    while distance:
        for s in sorted(blocks):
            blocks[s ^ distance] = across(blocks[s], axis, unit * distance)
        distance //= 2
    return [blocks[s] for s in range(len(blocks))]


def shards(left_tiles, left_index, right_tiles, right_index):
    row = lax.axis_index("row")
    col = lax.axis_index("col")
    z, y = col >> 1, col & 1
    right = right_tiles[0, 0]

    lefts = gather(left_tiles[0, 0], "col", 2)
    given = lax.dynamic_index_in_dim(right, 1 - y, 0, keepdims=True)
    own = lax.dynamic_index_in_dim(right, y, 0, keepdims=True)
    halves = jnp.concatenate([own, across(given, "col", 1)])
    rights = gather(halves, "row", 1)

    place = jnp.stack([row, z, y])
    mine, other, right_last, codes = first_products(place, left_index, right_index, lefts[:-1], rights)
    other = last_products(codes, lefts[-1], right_last, other, 1)
    coming = across(other, "col", 1)
    mine = last_products(codes, lefts[-1], right_last, mine, 0)
    return (mine + coming).astype(jnp.bfloat16)


def solution(mesh):
    return jax.shard_map(
        shards,
        mesh=mesh,
        in_specs=(
            P("row", "col", None, None, None),
            P(),
            P("row", "col", None, None, None, None),
            P(),
        ),
        out_specs=P("row", "col"),
        check_vma=False,
    )
```

```python
import jax
import jax.numpy as jnp
from jax import lax
from jax.experimental import pallas as pl
from jax.experimental.pallas import tpu as pltpu
from jax.sharding import PartitionSpec as P

KT = 8
RT = 2
SMEM = pl.BlockSpec(memory_space=pltpu.SMEM)
VMEM = pl.BlockSpec(memory_space=pltpu.VMEM)


def match(li_ref, ri_ref, row, zp, y, column, slot):
    right_slots = ri_ref.shape[-1]
    at = li_ref[row, 2 * zp + y, slot]
    k = lax.rem(at, KT)
    code = jnp.int32(0)
    for t in range(right_slots):
        code = jnp.where(ri_ref[zp, column, y, t] == k, 1 + lax.div(at, KT) * right_slots + t, code)
    return jnp.where(at < RT * KT, code, 0)


def add_tile(code, left_tile, right_at, right_slots, total_ref):
    tile = total_ref.shape[1]

    @pl.when(code > 0)
    def _():
        i = lax.div(code - 1, right_slots)
        rows = pl.ds(pl.multiple_of(i * tile, tile), tile)
        total_ref[rows, :] += jnp.dot(
            left_tile(), right_at(lax.rem(code - 1, right_slots)), preferred_element_type=jnp.float32
        )


def first_products(place, left_index, right_index, lefts, rights):
    slots, tile, _ = lefts[0].shape
    count = len(lefts)
    inner = rights[0].shape[0]
    right_slots = rights[0].shape[1]

    def kernel(place_ref, li_ref, ri_ref, *refs):
        left_refs, right_refs = refs[:count], refs[count : count + 2]
        totals = refs[count + 2 : count + 4]
        last_ref, codes_ref, held = refs[count + 4 :]
        row, z, y = place_ref[0], place_ref[1], place_ref[2]
        for t in range(inner):
            for side in range(2):
                held[row ^ t, side] = right_refs[t % 2][t - t % 2 + side]
        zl = lax.rem(z + 1, inner)
        last_ref[...] = held[zl]
        for side in range(2):
            column = 2 * z + (y if side == 0 else 1 - y)
            totals[side][...] = jnp.zeros_like(totals[side])
            for slot in range(slots):
                codes_ref[side * slots + slot] = match(li_ref, ri_ref, row, zl, y, column, slot)
            for s in range(count):
                zp = lax.rem(z - s + inner, inner)

                @pl.loop(0, slots)
                def _(slot):
                    add_tile(
                        match(li_ref, ri_ref, row, zp, y, column, slot),
                        lambda: left_refs[s][slot],
                        lambda found: held[zp, side, found],
                        right_slots,
                        totals[side],
                    )

    return pl.pallas_call(
        kernel,
        out_shape=[jax.ShapeDtypeStruct((RT * tile, tile), jnp.float32)] * 2
        + [
            jax.ShapeDtypeStruct((2, right_slots, tile, tile), jnp.bfloat16),
            jax.ShapeDtypeStruct((2 * slots,), jnp.int32),
        ],
        in_specs=[SMEM] * 3 + [VMEM] * (count + 2),
        out_specs=[VMEM] * 3 + [SMEM],
        scratch_shapes=[pltpu.VMEM((inner, 2, right_slots, tile, tile), jnp.bfloat16)],
        compiler_params=pltpu.CompilerParams(vmem_limit_bytes=32 * 1024 * 1024),
        cost_estimate=pl.CostEstimate(
            flops=4 * count * slots * tile**3, bytes_accessed=2 * count * slots * tile**2, transcendentals=0
        ),
    )(place, left_index, right_index, *lefts, *rights)


def last_products(codes, left, right, total, side):
    slots, tile, _ = left.shape
    right_slots = right.shape[1]

    def kernel(codes_ref, left_ref, right_ref, total_ref, out_ref):
        out_ref[...] = total_ref[...]
        for slot in range(slots):
            add_tile(
                codes_ref[side * slots + slot],
                lambda: left_ref[slot],
                lambda found: right_ref[side, found],
                right_slots,
                out_ref,
            )

    return pl.pallas_call(
        kernel,
        out_shape=jax.ShapeDtypeStruct(total.shape, total.dtype),
        in_specs=[SMEM] + [VMEM] * 3,
        out_specs=VMEM,
        compiler_params=pltpu.CompilerParams(vmem_limit_bytes=16 * 1024 * 1024),
        cost_estimate=pl.CostEstimate(
            flops=2 * slots * tile**3, bytes_accessed=2 * slots * tile**2, transcendentals=0
        ),
    )(codes, left, right, total)


def across(block, axis, mask):
    route = [(i, i ^ mask) for i in range(lax.axis_size(axis))]
    return lax.ppermute(block, axis, route)


def crossed(block, mask):
    rows, cols = lax.axis_size("row"), lax.axis_size("col")
    route = [(r * cols + c, (r ^ mask) * cols + (c ^ 1)) for r in range(rows) for c in range(cols)]
    return lax.ppermute(block, ("row", "col"), route)


def around(block):
    cols = lax.axis_size("col")
    route = [(c, (c + 2) % cols) for c in range(cols)]
    blocks = [block]
    for _ in range(cols // 2 - 1):
        blocks.append(lax.ppermute(blocks[-1], "col", route))
    return blocks


def shards(left_tiles, left_index, right_tiles, right_index):
    row = lax.axis_index("row")
    col = lax.axis_index("col")
    z, y = col >> 1, col & 1
    right = right_tiles[0, 0]

    lefts = around(left_tiles[0, 0])
    given = lax.dynamic_index_in_dim(right, 1 - y, 0, keepdims=True)
    own = lax.dynamic_index_in_dim(right, y, 0, keepdims=True)
    chips = []
    for t in range(0, lax.axis_size("row"), 2):
        chips.append(across(own, "row", t) if t else own)
        chips.append(crossed(given, t))
    chips = jnp.concatenate(chips)
    rights = [chips, across(chips, "row", 1)]

    place = jnp.stack([row, z, y])
    mine, other, right_last, codes = first_products(place, left_index, right_index, lefts[:-1], rights)
    other = last_products(codes, lefts[-1], right_last, other, 1)
    coming = across(other, "col", 1)
    mine = last_products(codes, lefts[-1], right_last, mine, 0)
    return (mine + coming).astype(jnp.bfloat16)


def solution(mesh):
    return jax.shard_map(
        shards,
        mesh=mesh,
        in_specs=(
            P("row", "col", None, None, None),
            P(),
            P("row", "col", None, None, None, None),
            P(),
        ),
        out_specs=P("row", "col"),
        check_vma=False,
    )
```

```python
import jax
import jax.numpy as jnp
from jax import lax
from jax.experimental import pallas as pl
from jax.experimental.pallas import tpu as pltpu
from jax.sharding import PartitionSpec as P

KT = 8
RT = 2
CUT = 4
SMEM = pl.BlockSpec(memory_space=pltpu.SMEM)
VMEM = pl.BlockSpec(memory_space=pltpu.VMEM)


def find_matches(place, left_index, right_index):
    slots = left_index.shape[-1]
    inner, _, _, right_slots = right_index.shape

    def kernel(place_ref, li_ref, ri_ref, codes_ref):
        row, z, y = place_ref[0], place_ref[1], place_ref[2]

        @pl.loop(0, inner)
        def _(s):
            zp = z ^ s
            for side in range(2):
                column = 2 * z + (y if side == 0 else 1 - y)
                have = [ri_ref[zp, column, y, t] for t in range(right_slots)]
                for slot in range(slots):
                    at = li_ref[row, 2 * zp + y, slot]
                    k = lax.rem(at, KT)
                    first = 1 + lax.div(at, KT) * right_slots
                    code = jnp.int32(0)
                    for t in range(right_slots):
                        code = jnp.where(have[t] == k, first + t, code)
                    codes_ref[(s * 2 + side) * slots + slot] = jnp.where(at < RT * KT, code, 0)

    return pl.pallas_call(
        kernel,
        out_shape=jax.ShapeDtypeStruct((inner * 2 * slots,), jnp.int32),
        in_specs=[SMEM] * 3,
        out_specs=SMEM,
    )(place, left_index, right_index)


def add_part(codes_ref, s, side, start, slots, left_ref, right_at, right_slots, total_ref):
    tile = total_ref.shape[1]

    @pl.loop(0, left_ref.shape[0])
    def _(slot):
        code = codes_ref[(s * 2 + side) * slots + start + slot]

        @pl.when(code > 0)
        def _():
            i = lax.div(code - 1, right_slots)
            rows = pl.ds(pl.multiple_of(i * tile, tile), tile)
            total_ref[rows, :] += jnp.dot(
                left_ref[slot],
                right_at(lax.rem(code - 1, right_slots)),
                preferred_element_type=jnp.float32,
            )


def first_products(place, codes, lefts, rights, slots):
    parts = [(s, part) for s, block in lefts for part in block]
    count = len(parts)
    inner = len(rights)
    _, right_slots, tile, _ = rights[0].shape

    def kernel(place_ref, codes_ref, *refs):
        right_refs = refs[count : count + inner]
        totals = refs[count + inner : count + inner + 2]
        last_ref, held = refs[count + inner + 2 :]
        row, z = place_ref[0], place_ref[1]
        for t in range(inner):
            held[row ^ t] = right_refs[t][...]
        last_ref[...] = held[z ^ (inner - 1)]
        for side in range(2):
            totals[side][...] = jnp.zeros_like(totals[side])
            start, before = 0, None
            for (s, _), left_ref in zip(parts, refs):
                start = start if s == before else 0
                add_part(
                    codes_ref, s, side, start, slots, left_ref,
                    lambda found, s=s: held[z ^ s, side, found], right_slots, totals[side],
                )
                start, before = start + left_ref.shape[0], s

    return pl.pallas_call(
        kernel,
        out_shape=[jax.ShapeDtypeStruct((RT * tile, tile), jnp.float32)] * 2
        + [jax.ShapeDtypeStruct((2, right_slots, tile, tile), jnp.bfloat16)],
        in_specs=[SMEM] * 2 + [VMEM] * (count + inner),
        out_specs=[VMEM] * 3,
        scratch_shapes=[pltpu.VMEM((inner, 2, right_slots, tile, tile), jnp.bfloat16)],
        compiler_params=pltpu.CompilerParams(vmem_limit_bytes=32 * 1024 * 1024),
        cost_estimate=pl.CostEstimate(
            flops=4 * inner * slots * tile**3, bytes_accessed=2 * inner * slots * tile**2, transcendentals=0
        ),
    )(place, codes, *[part for _, part in parts], *rights)


def last_products(codes, s, parts, right, total, side, slots):
    count = len(parts)
    right_slots = right.shape[1]

    def kernel(codes_ref, *refs):
        right_ref, total_ref, out_ref = refs[count:]
        out_ref[...] = total_ref[...]
        start = 0
        for left_ref in refs[:count]:
            add_part(
                codes_ref, s, side, start, slots, left_ref,
                lambda found: right_ref[side, found], right_slots, out_ref,
            )
            start += left_ref.shape[0]

    return pl.pallas_call(
        kernel,
        out_shape=jax.ShapeDtypeStruct(total.shape, total.dtype),
        in_specs=[SMEM] + [VMEM] * (count + 2),
        out_specs=VMEM,
        compiler_params=pltpu.CompilerParams(vmem_limit_bytes=16 * 1024 * 1024),
        cost_estimate=pl.CostEstimate(
            flops=2 * slots * 128**3, bytes_accessed=2 * slots * 128**2, transcendentals=0
        ),
    )(codes, *parts, right, total)


def across(block, axis, mask):
    route = [(i, i ^ mask) for i in range(lax.axis_size(axis))]
    return lax.ppermute(block, axis, route)


def crossed(block, mask):
    rows, cols = lax.axis_size("row"), lax.axis_size("col")
    route = [(r * cols + c, (r ^ mask) * cols + (c ^ 1)) for r in range(rows) for c in range(cols)]
    return lax.ppermute(block, ("row", "col"), route)


def gather(block, cut):
    distance = lax.axis_size("col") // 4
    far_head = across(block[:cut], "col", 2 * distance)
    tail, _ = lax.optimization_barrier((block[cut:], far_head))
    far_tail = across(tail, "col", 2 * distance)
    blocks = {0: (block,), distance: (far_head, far_tail)}
    near = distance // 2
    while near:
        for s in sorted(blocks):
            blocks[s ^ near] = tuple(across(part, "col", 2 * near) for part in blocks[s])
        near //= 2
    return sorted(blocks.items())


def shards(left_tiles, left_index, right_tiles, right_index):
    row = lax.axis_index("row")
    col = lax.axis_index("col")
    z, y = col >> 1, col & 1
    left = left_tiles[0, 0]
    right = right_tiles[0, 0]
    slots = left.shape[0]

    lefts = gather(left, CUT)
    given = lax.dynamic_index_in_dim(right, 1 - y, 0, keepdims=True)
    own = lax.dynamic_index_in_dim(right, y, 0, keepdims=True)
    rights = []
    for t in range(0, lax.axis_size("row"), 2):
        pair = jnp.concatenate([across(own, "row", t) if t else own, crossed(given, t)])
        rights += [pair, across(pair, "row", 1)]

    place = jnp.stack([row, z, y])
    codes = find_matches(place, left_index, right_index)
    mine, other, right_last = first_products(place, codes, lefts[:-1], rights, slots)
    far, final = lefts[-1]
    other = last_products(codes, far, final, right_last, other, 1, slots)
    coming = across(other, "col", 1)
    mine = last_products(codes, far, final, right_last, mine, 0, slots)
    return (mine + coming).astype(jnp.bfloat16)


def solution(mesh):
    return jax.shard_map(
        shards,
        mesh=mesh,
        in_specs=(
            P("row", "col", None, None, None),
            P(),
            P("row", "col", None, None, None, None),
            P(),
        ),
        out_specs=P("row", "col"),
        check_vma=False,
    )
```

```python
import jax
import jax.numpy as jnp
from jax import lax
from jax.experimental import pallas as pl
from jax.experimental.pallas import tpu as pltpu
from jax.sharding import PartitionSpec as P

KT = 8
RT = 2
SMEM = pl.BlockSpec(memory_space=pltpu.SMEM)
VMEM = pl.BlockSpec(memory_space=pltpu.VMEM)


def match(li_ref, ri_ref, row, zp, y, column, slot):
    right_slots = ri_ref.shape[-1]
    at = li_ref[row, 2 * zp + y, slot]
    k = lax.rem(at, KT)
    code = jnp.int32(0)
    for t in range(right_slots):
        code = jnp.where(ri_ref[zp, column, y, t] == k, 1 + lax.div(at, KT) * right_slots + t, code)
    return jnp.where(at < RT * KT, code, 0)


def add_tile(code, left_tile, right_at, right_slots, total_ref):
    tile = total_ref.shape[1]

    @pl.when(code > 0)
    def _():
        i = lax.div(code - 1, right_slots)
        rows = pl.ds(pl.multiple_of(i * tile, tile), tile)
        total_ref[rows, :] += jnp.dot(
            left_tile(), right_at(lax.rem(code - 1, right_slots)), preferred_element_type=jnp.float32
        )


def first_products(place, left_index, right_index, lefts, rights):
    slots, tile, _ = lefts[0].shape
    count = len(lefts)
    inner = len(rights) // 2
    right_slots = rights[0].shape[0]

    def kernel(place_ref, li_ref, ri_ref, *refs):
        left_refs, right_refs = refs[:count], refs[count : count + 2 * inner]
        totals = refs[count + 2 * inner : count + 2 * inner + 2]
        last_ref, codes_ref, held = refs[count + 2 * inner + 2 :]
        row, z, y = place_ref[0], place_ref[1], place_ref[2]
        for t in range(inner):
            for side in range(2):
                held[row ^ t, side] = right_refs[2 * t + side][...]
        zl = z ^ (inner - 1)
        last_ref[...] = held[zl]
        for side in range(2):
            column = 2 * z + (y if side == 0 else 1 - y)
            totals[side][...] = jnp.zeros_like(totals[side])
            for slot in range(slots):
                codes_ref[side * slots + slot] = match(li_ref, ri_ref, row, zl, y, column, slot)
            for s in range(count):
                zp = z ^ s

                @pl.loop(0, slots)
                def _(slot):
                    add_tile(
                        match(li_ref, ri_ref, row, zp, y, column, slot),
                        lambda: left_refs[s][slot],
                        lambda found: held[zp, side, found],
                        right_slots,
                        totals[side],
                    )

    return pl.pallas_call(
        kernel,
        out_shape=[jax.ShapeDtypeStruct((RT * tile, tile), jnp.float32)] * 2
        + [
            jax.ShapeDtypeStruct((2, right_slots, tile, tile), jnp.bfloat16),
            jax.ShapeDtypeStruct((2 * slots,), jnp.int32),
        ],
        in_specs=[SMEM] * 3 + [VMEM] * (count + 2 * inner),
        out_specs=[VMEM] * 3 + [SMEM],
        scratch_shapes=[pltpu.VMEM((inner, 2, right_slots, tile, tile), jnp.bfloat16)],
        compiler_params=pltpu.CompilerParams(vmem_limit_bytes=32 * 1024 * 1024),
        cost_estimate=pl.CostEstimate(
            flops=4 * count * slots * tile**3, bytes_accessed=2 * count * slots * tile**2, transcendentals=0
        ),
    )(place, left_index, right_index, *lefts, *rights)


def last_products(codes, left, right, total, side):
    slots, tile, _ = left.shape
    right_slots = right.shape[1]

    def kernel(codes_ref, left_ref, right_ref, total_ref, out_ref):
        out_ref[...] = total_ref[...]
        for slot in range(slots):
            add_tile(
                codes_ref[side * slots + slot],
                lambda: left_ref[slot],
                lambda found: right_ref[side, found],
                right_slots,
                out_ref,
            )

    return pl.pallas_call(
        kernel,
        out_shape=jax.ShapeDtypeStruct(total.shape, total.dtype),
        in_specs=[SMEM] + [VMEM] * 3,
        out_specs=VMEM,
        compiler_params=pltpu.CompilerParams(vmem_limit_bytes=16 * 1024 * 1024),
        cost_estimate=pl.CostEstimate(
            flops=2 * slots * tile**3, bytes_accessed=2 * slots * tile**2, transcendentals=0
        ),
    )(codes, left, right, total)


def across(block, axis, mask):
    route = [(i, i ^ mask) for i in range(lax.axis_size(axis))]
    return lax.ppermute(block, axis, route)


def crossed(block, mask):
    rows, cols = lax.axis_size("row"), lax.axis_size("col")
    route = [(r * cols + c, (r ^ mask) * cols + (c ^ 1)) for r in range(rows) for c in range(cols)]
    return lax.ppermute(block, ("row", "col"), route)


def gather(block):
    distance = lax.axis_size("col") // 4
    near = [distance // 2**n for n in range(distance.bit_length())]
    blocks = {0: block}
    for distance in near:
        blocks[distance] = across(block, "col", 2 * distance)
    held = lax.optimization_barrier([blocks[d] for d in near])
    blocks.update(zip(near, held))
    for n, distance in enumerate(near):
        for s in sorted(blocks):
            if s ^ distance not in blocks and s & (distance - 1) == 0:
                blocks[s ^ distance] = across(blocks[s], "col", 2 * distance)
    return [blocks[s] for s in range(len(blocks))]


def shards(left_tiles, left_index, right_tiles, right_index):
    row = lax.axis_index("row")
    col = lax.axis_index("col")
    z, y = col >> 1, col & 1
    right = right_tiles[0, 0]

    lefts = gather(left_tiles[0, 0])
    given = lax.dynamic_index_in_dim(right, 1 - y, 0, keepdims=False)
    own = lax.dynamic_index_in_dim(right, y, 0, keepdims=False)
    rights = []
    for t in range(lax.axis_size("row")):
        rights += [across(own, "row", t) if t else own, crossed(given, t)]

    place = jnp.stack([row, z, y])
    mine, other, right_last, codes = first_products(place, left_index, right_index, lefts[:-1], rights)
    other = last_products(codes, lefts[-1], right_last, other, 1)
    coming = across(other, "col", 1)
    mine = last_products(codes, lefts[-1], right_last, mine, 0)
    return (mine + coming).astype(jnp.bfloat16)


def solution(mesh):
    return jax.shard_map(
        shards,
        mesh=mesh,
        in_specs=(
            P("row", "col", None, None, None),
            P(),
            P("row", "col", None, None, None, None),
            P(),
        ),
        out_specs=P("row", "col"),
        check_vma=False,
    )
```

```python
import jax
import jax.numpy as jnp
from jax import lax
from jax.experimental import pallas as pl
from jax.experimental.pallas import tpu as pltpu
from jax.sharding import PartitionSpec as P

KT = 8
RT = 2
SMEM = pl.BlockSpec(memory_space=pltpu.SMEM)
VMEM = pl.BlockSpec(memory_space=pltpu.VMEM)


def match(li_ref, ri_ref, row, zp, there, y, column, slot):
    right_slots = ri_ref.shape[-1]
    at = li_ref[row, 2 * zp + y, slot]
    k = lax.rem(at, KT)
    code = jnp.int32(0)
    for t in range(right_slots):
        code = jnp.where(ri_ref[zp, column, y, t] == k, 1 + lax.div(at, KT) * right_slots + t, code)
    return jnp.where(jnp.logical_and(there, at < RT * KT), code, 0)


def add_tile(code, left_tile, right_at, right_slots, total_ref):
    tile = total_ref.shape[1]

    @pl.when(code > 0)
    def _():
        i = lax.div(code - 1, right_slots)
        rows = pl.ds(pl.multiple_of(i * tile, tile), tile)
        total_ref[rows, :] += jnp.dot(
            left_tile(), right_at(lax.rem(code - 1, right_slots)), preferred_element_type=jnp.float32
        )


def first_products(place, left_index, right_index, names, lefts, last, rights):
    slots, tile, _ = lefts[0].shape
    count = len(lefts)
    inner = len(rights)
    right_slots = rights[0].shape[1]

    def kernel(place_ref, li_ref, ri_ref, *refs):
        left_refs, right_refs = refs[:count], refs[count : count + inner]
        totals = refs[count + inner : count + inner + 2]
        last_ref, codes_ref, held = refs[count + inner + 2 :]
        row, z, y = place_ref[0], place_ref[1], place_ref[2]
        for t in range(inner):
            held[row ^ t] = right_refs[t][...]
        zl, there = origin(z, *last, inner)
        last_ref[...] = held[zl]
        for side in range(2):
            column = 2 * z + (y if side == 0 else 1 - y)
            totals[side][...] = jnp.zeros_like(totals[side])
            for slot in range(slots):
                codes_ref[side * slots + slot] = match(li_ref, ri_ref, row, zl, there, y, column, slot)
            for n, name in enumerate(names):
                zp, there_n = origin(z, *name, inner)

                @pl.when(there_n)
                def _():
                    @pl.loop(0, slots)
                    def _(slot):
                        add_tile(
                            match(li_ref, ri_ref, row, zp, True, y, column, slot),
                            lambda: left_refs[n][slot],
                            lambda found: held[zp, side, found],
                            right_slots,
                            totals[side],
                        )

    return pl.pallas_call(
        kernel,
        out_shape=[jax.ShapeDtypeStruct((RT * tile, tile), jnp.float32)] * 2
        + [
            jax.ShapeDtypeStruct((2, right_slots, tile, tile), jnp.bfloat16),
            jax.ShapeDtypeStruct((2 * slots,), jnp.int32),
        ],
        in_specs=[SMEM] * 3 + [VMEM] * (count + inner),
        out_specs=[VMEM] * 3 + [SMEM],
        scratch_shapes=[pltpu.VMEM((inner, 2, right_slots, tile, tile), jnp.bfloat16)],
        compiler_params=pltpu.CompilerParams(vmem_limit_bytes=32 * 1024 * 1024),
        cost_estimate=pl.CostEstimate(
            flops=4 * count * slots * tile**3, bytes_accessed=2 * count * slots * tile**2, transcendentals=0
        ),
    )(place, left_index, right_index, *lefts, *rights)


def last_products(codes, left, right, total, side):
    slots, tile, _ = left.shape
    right_slots = right.shape[1]

    def kernel(codes_ref, left_ref, right_ref, total_ref, out_ref):
        out_ref[...] = total_ref[...]
        for slot in range(slots):
            add_tile(
                codes_ref[side * slots + slot],
                lambda: left_ref[slot],
                lambda found: right_ref[side, found],
                right_slots,
                out_ref,
            )

    return pl.pallas_call(
        kernel,
        out_shape=jax.ShapeDtypeStruct(total.shape, total.dtype),
        in_specs=[SMEM] + [VMEM] * 3,
        out_specs=VMEM,
        compiler_params=pltpu.CompilerParams(vmem_limit_bytes=16 * 1024 * 1024),
        cost_estimate=pl.CostEstimate(
            flops=2 * slots * tile**3, bytes_accessed=2 * slots * tile**2, transcendentals=0
        ),
    )(codes, left, right, total)


def across(block, axis, mask):
    route = [(i, i ^ mask) for i in range(lax.axis_size(axis))]
    return lax.ppermute(block, axis, route)


def crossed(block, mask):
    rows, cols = lax.axis_size("row"), lax.axis_size("col")
    route = [(r * cols + c, (r ^ mask) * cols + (c ^ 1)) for r in range(rows) for c in range(cols)]
    return lax.ppermute(block, ("row", "col"), route)


def spread(block):
    places = lax.axis_size("col") // 2
    found = [(0, 0, block)]
    held = {0: block, 1: block}
    for step in range(1, places):
        came = {}
        for edge in range(2):
            route = []
            for i in range(places):
                j = i + 1 - 2 * ((i + edge) % 2)
                if 0 <= j < places and 0 <= i - (j - i) * (step - 1) < places:
                    route += [(2 * i + y, 2 * j + y) for y in range(2)]
            if route:
                came[edge] = lax.ppermute(held[1 - edge], "col", route)
                found.append((edge, step, came[edge]))
        held = came
    return found


def origin(z, edge, step, places):
    zp = z + step * (1 - 2 * lax.rem(z + edge, 2))
    there = jnp.logical_and(zp >= 0, zp < places)
    return jnp.where(there, zp, z), there


def shards(left_tiles, left_index, right_tiles, right_index):
    row = lax.axis_index("row")
    col = lax.axis_index("col")
    z, y = col >> 1, col & 1
    right = right_tiles[0, 0]

    *early, (*last, final) = spread(left_tiles[0, 0])
    names = [(edge, step) for edge, step, _ in early]
    lefts = [block for _, _, block in early]
    given = lax.dynamic_index_in_dim(right, 1 - y, 0, keepdims=False)
    own = lax.dynamic_index_in_dim(right, y, 0, keepdims=False)
    rights = []
    for t in range(0, lax.axis_size("row"), 2):
        pair = jnp.stack([across(own, "row", t) if t else own, crossed(given, t)])
        rights += [pair, across(pair, "row", 1)]

    place = jnp.stack([row, z, y])
    mine, other, right_last, codes = first_products(
        place, left_index, right_index, names, lefts, last, rights
    )
    other = last_products(codes, final, right_last, other, 1)
    coming = across(other, "col", 1)
    mine = last_products(codes, final, right_last, mine, 0)
    return (mine + coming).astype(jnp.bfloat16)


def solution(mesh):
    return jax.shard_map(
        shards,
        mesh=mesh,
        in_specs=(
            P("row", "col", None, None, None),
            P(),
            P("row", "col", None, None, None, None),
            P(),
        ),
        out_specs=P("row", "col"),
        check_vma=False,
    )
```

```python
import jax
import jax.numpy as jnp
from jax import lax
from jax.experimental import pallas as pl
from jax.experimental.pallas import tpu as pltpu
from jax.sharding import PartitionSpec as P

KT = 8
RT = 2
SMEM = pl.BlockSpec(memory_space=pltpu.SMEM)
VMEM = pl.BlockSpec(memory_space=pltpu.VMEM)


def find_matches(place, left_index, right_index):
    slots = left_index.shape[-1]
    inner, _, _, right_slots = right_index.shape

    def kernel(place_ref, li_ref, ri_ref, codes_ref):
        row, z, y = place_ref[0], place_ref[1], place_ref[2]

        @pl.loop(0, inner)
        def _(s):
            zp = z ^ s
            for side in range(2):
                column = 2 * z + (y if side == 0 else 1 - y)
                have = [ri_ref[zp, column, y, t] for t in range(right_slots)]
                for slot in range(slots):
                    at = li_ref[row, 2 * zp + y, slot]
                    k = lax.rem(at, KT)
                    first = 1 + lax.div(at, KT) * right_slots
                    code = jnp.int32(0)
                    for t in range(right_slots):
                        code = jnp.where(have[t] == k, first + t, code)
                    codes_ref[(s * 2 + side) * slots + slot] = jnp.where(at < RT * KT, code, 0)

    return pl.pallas_call(
        kernel,
        out_shape=jax.ShapeDtypeStruct((inner * 2 * slots,), jnp.int32),
        in_specs=[SMEM] * 3,
        out_specs=SMEM,
    )(place, left_index, right_index)


def add_part(codes_ref, s, side, start, slots, left_ref, right_at, right_slots, total_ref):
    tile = total_ref.shape[1]

    @pl.loop(0, left_ref.shape[0])
    def _(slot):
        code = codes_ref[(s * 2 + side) * slots + start + slot]

        @pl.when(code > 0)
        def _():
            i = lax.div(code - 1, right_slots)
            rows = pl.ds(pl.multiple_of(i * tile, tile), tile)
            total_ref[rows, :] += jnp.dot(
                left_ref[slot],
                right_at(lax.rem(code - 1, right_slots)),
                preferred_element_type=jnp.float32,
            )


def first_products(place, codes, lefts, rights, slots):
    parts = [(s, part) for s, block in lefts for part in block]
    count = len(parts)
    inner = len(rights)
    _, right_slots, tile, _ = rights[0].shape

    def kernel(place_ref, codes_ref, *refs):
        right_refs = refs[count : count + inner]
        totals = refs[count + inner : count + inner + 2]
        last_ref, held = refs[count + inner + 2 :]
        row, z = place_ref[0], place_ref[1]
        for t in range(inner):
            held[row ^ t] = right_refs[t][...]
        last_ref[...] = held[z ^ (inner - 1)]
        for side in range(2):
            totals[side][...] = jnp.zeros_like(totals[side])
            start, before = 0, None
            for (s, _), left_ref in zip(parts, refs):
                start = start if s == before else 0
                add_part(
                    codes_ref, s, side, start, slots, left_ref,
                    lambda found, s=s: held[z ^ s, side, found], right_slots, totals[side],
                )
                start, before = start + left_ref.shape[0], s

    return pl.pallas_call(
        kernel,
        out_shape=[jax.ShapeDtypeStruct((RT * tile, tile), jnp.float32)] * 2
        + [jax.ShapeDtypeStruct((2, right_slots, tile, tile), jnp.bfloat16)],
        in_specs=[SMEM] * 2 + [VMEM] * (count + inner),
        out_specs=[VMEM] * 3,
        scratch_shapes=[pltpu.VMEM((inner, 2, right_slots, tile, tile), jnp.bfloat16)],
        compiler_params=pltpu.CompilerParams(vmem_limit_bytes=32 * 1024 * 1024),
        cost_estimate=pl.CostEstimate(
            flops=4 * inner * slots * tile**3, bytes_accessed=2 * inner * slots * tile**2, transcendentals=0
        ),
    )(place, codes, *[part for _, part in parts], *rights)


def last_products(codes, s, parts, right, total, side, slots):
    count = len(parts)
    right_slots = right.shape[1]

    def kernel(codes_ref, *refs):
        right_ref, total_ref, out_ref = refs[count:]
        out_ref[...] = total_ref[...]
        start = 0
        for left_ref in refs[:count]:
            add_part(
                codes_ref, s, side, start, slots, left_ref,
                lambda found: right_ref[side, found], right_slots, out_ref,
            )
            start += left_ref.shape[0]

    return pl.pallas_call(
        kernel,
        out_shape=jax.ShapeDtypeStruct(total.shape, total.dtype),
        in_specs=[SMEM] + [VMEM] * (count + 2),
        out_specs=VMEM,
        compiler_params=pltpu.CompilerParams(vmem_limit_bytes=16 * 1024 * 1024),
        cost_estimate=pl.CostEstimate(
            flops=2 * slots * 128**3, bytes_accessed=2 * slots * 128**2, transcendentals=0
        ),
    )(codes, *parts, right, total)


def across(block, axis, mask):
    route = [(i, i ^ mask) for i in range(lax.axis_size(axis))]
    return lax.ppermute(block, axis, route)


def row_gather(right, y):
    given = lax.dynamic_index_in_dim(right, 1 - y, 0, keepdims=False)
    own = lax.dynamic_index_in_dim(right, y, 0, keepdims=False)
    blocks = {0: jnp.stack([own, across(given, "col", 1)])}
    distance = lax.axis_size("row") // 2
    while distance:
        for t in sorted(blocks):
            blocks[t ^ distance] = across(blocks[t], "row", distance)
        distance //= 2
    return [blocks[t] for t in range(len(blocks))]


def shards(left_tiles, left_index, right_tiles, right_index):
    row = lax.axis_index("row")
    col = lax.axis_index("col")
    z, y = col >> 1, col & 1
    left = left_tiles[0, 0]
    right = right_tiles[0, 0]
    slots = left.shape[0]
    rows = lax.axis_size("row")

    lefts = [(s, (across(left, "col", 2 * s) if s else left,)) for s in range(rows)]
    place = jnp.stack([row, z, y])

    def right_side():
        return find_matches(place, left_index, right_index), row_gather(right, y)

    def nothing():
        return jnp.zeros((rows * 2 * slots,), jnp.int32), [jnp.zeros_like(right)] * rows

    codes, rights = lax.cond(row < rows, right_side, nothing)
    mine, other, right_last = first_products(place, codes, lefts[:-1], rights, slots)
    far, final = lefts[-1]
    other = last_products(codes, far, final, right_last, other, 1, slots)
    coming = across(other, "col", 1)
    mine = last_products(codes, far, final, right_last, mine, 0, slots)
    return (mine + coming).astype(jnp.bfloat16)


def solution(mesh):
    return jax.shard_map(
        shards,
        mesh=mesh,
        in_specs=(
            P("row", "col", None, None, None),
            P(),
            P("row", "col", None, None, None, None),
            P(),
        ),
        out_specs=P("row", "col"),
        check_vma=False,
    )
```

```python
import jax
import jax.numpy as jnp
from jax import lax
from jax.experimental import pallas as pl
from jax.experimental.pallas import tpu as pltpu
from jax.sharding import PartitionSpec as P

KT = 8
RT = 2
SMEM = pl.BlockSpec(memory_space=pltpu.SMEM)
VMEM = pl.BlockSpec(memory_space=pltpu.VMEM)


def find_matches(place, left_index, right_index):
    slots = left_index.shape[-1]
    inner, _, _, right_slots = right_index.shape

    def kernel(place_ref, li_ref, ri_ref, codes_ref):
        row, z, y = place_ref[0], place_ref[1], place_ref[2]

        @pl.loop(0, inner)
        def _(s):
            zp = z ^ s
            for side in range(2):
                column = 2 * z + (y if side == 0 else 1 - y)
                have = [ri_ref[zp, column, y, t] for t in range(right_slots)]
                for slot in range(slots):
                    at = li_ref[row, 2 * zp + y, slot]
                    k = lax.rem(at, KT)
                    first = 1 + lax.div(at, KT) * right_slots
                    code = jnp.int32(0)
                    for t in range(right_slots):
                        code = jnp.where(have[t] == k, first + t, code)
                    codes_ref[(s * 2 + side) * slots + slot] = jnp.where(at < RT * KT, code, 0)

    return pl.pallas_call(
        kernel,
        out_shape=jax.ShapeDtypeStruct((inner * 2 * slots,), jnp.int32),
        in_specs=[SMEM] * 3,
        out_specs=SMEM,
    )(place, left_index, right_index)


def add_part(codes_ref, s, side, start, slots, left_ref, right_at, right_slots, total_ref):
    tile = total_ref.shape[1]

    @pl.loop(0, left_ref.shape[0])
    def _(slot):
        code = codes_ref[(s * 2 + side) * slots + start + slot]

        @pl.when(code > 0)
        def _():
            i = lax.div(code - 1, right_slots)
            rows = pl.ds(pl.multiple_of(i * tile, tile), tile)
            total_ref[rows, :] += jnp.dot(
                left_ref[slot],
                right_at(lax.rem(code - 1, right_slots)),
                preferred_element_type=jnp.float32,
            )


def first_products(place, codes, lefts, rights, slots):
    parts = [(s, part) for s, block in lefts for part in block]
    count = len(parts)
    inner = len(rights)
    _, right_slots, tile, _ = rights[0].shape

    def kernel(place_ref, codes_ref, *refs):
        right_refs = refs[count : count + inner]
        totals = refs[count + inner : count + inner + 2]
        last_ref, held = refs[count + inner + 2 :]
        row, z = place_ref[0], place_ref[1]
        for t in range(inner):
            held[row ^ t] = right_refs[t][...]
        last_ref[...] = held[z ^ (inner - 1)]
        for side in range(2):
            totals[side][...] = jnp.zeros_like(totals[side])
            start, before = 0, None
            for (s, _), left_ref in zip(parts, refs):
                start = start if s == before else 0
                add_part(
                    codes_ref, s, side, start, slots, left_ref,
                    lambda found, s=s: held[z ^ s, side, found], right_slots, totals[side],
                )
                start, before = start + left_ref.shape[0], s

    return pl.pallas_call(
        kernel,
        out_shape=[jax.ShapeDtypeStruct((RT * tile, tile), jnp.float32)] * 2
        + [jax.ShapeDtypeStruct((2, right_slots, tile, tile), jnp.bfloat16)],
        in_specs=[SMEM] * 2 + [VMEM] * (count + inner),
        out_specs=[VMEM] * 3,
        scratch_shapes=[pltpu.VMEM((inner, 2, right_slots, tile, tile), jnp.bfloat16)],
        compiler_params=pltpu.CompilerParams(vmem_limit_bytes=32 * 1024 * 1024),
        cost_estimate=pl.CostEstimate(
            flops=4 * inner * slots * tile**3, bytes_accessed=2 * inner * slots * tile**2, transcendentals=0
        ),
    )(place, codes, *[part for _, part in parts], *rights)


def last_products(codes, s, parts, right, total, side, slots):
    count = len(parts)
    right_slots = right.shape[1]

    def kernel(codes_ref, *refs):
        right_ref, total_ref, out_ref = refs[count:]
        out_ref[...] = total_ref[...]
        start = 0
        for left_ref in refs[:count]:
            add_part(
                codes_ref, s, side, start, slots, left_ref,
                lambda found: right_ref[side, found], right_slots, out_ref,
            )
            start += left_ref.shape[0]

    return pl.pallas_call(
        kernel,
        out_shape=jax.ShapeDtypeStruct(total.shape, total.dtype),
        in_specs=[SMEM] + [VMEM] * (count + 2),
        out_specs=VMEM,
        compiler_params=pltpu.CompilerParams(vmem_limit_bytes=16 * 1024 * 1024),
        cost_estimate=pl.CostEstimate(
            flops=2 * slots * 128**3, bytes_accessed=2 * slots * 128**2, transcendentals=0
        ),
    )(codes, *parts, right, total)


def across(block, axis, mask):
    route = [(i, i ^ mask) for i in range(lax.axis_size(axis))]
    return lax.ppermute(block, axis, route)


def crossed(block, mask):
    rows, cols = lax.axis_size("row"), lax.axis_size("col")
    route = [(r * cols + c, (r ^ mask) * cols + (c ^ 1)) for r in range(rows) for c in range(cols)]
    return lax.ppermute(block, ("row", "col"), route)


def gather(block, beside):
    distance = lax.axis_size("col") // 4
    steps = [distance >> n for n in range(distance.bit_length())]
    came = [across(block, "col", 2 * d) for d in steps]
    came, results = lax.optimization_barrier((came, beside()))
    blocks = {0: block, **dict(zip(steps, came))}
    for d in steps:
        for s in sorted(blocks):
            if s ^ d not in blocks and s & (d - 1) == 0:
                blocks[s ^ d] = across(blocks[s], "col", 2 * d)
    return [(s, (blocks[s],)) for s in range(len(blocks))], results


def right_side(place, left_index, right_index, right, y):
    codes = find_matches(place, left_index, right_index)
    given = lax.dynamic_index_in_dim(right, 1 - y, 0, keepdims=False)
    own = lax.dynamic_index_in_dim(right, y, 0, keepdims=False)
    pairs = []
    for t in range(0, lax.axis_size("row"), 2):
        pairs.append(jnp.stack([across(own, "row", t) if t else own, crossed(given, t)]))
    codes, pairs = lax.optimization_barrier((codes, pairs))
    rights = []
    for pair in pairs:
        rights += [pair, across(pair, "row", 1)]
    return codes, rights


def shards(left_tiles, left_index, right_tiles, right_index):
    row = lax.axis_index("row")
    col = lax.axis_index("col")
    z, y = col >> 1, col & 1
    left = left_tiles[0, 0]
    right = right_tiles[0, 0]
    slots = left.shape[0]
    rows = lax.axis_size("row")

    place = jnp.stack([row, z, y])

    def right_branch():
        return lax.cond(
            row < rows,
            lambda: right_side(place, left_index, right_index, right, y),
            lambda: (jnp.zeros((rows * 2 * slots,), jnp.int32), [jnp.zeros_like(right)] * rows),
        )

    lefts, (codes, rights) = gather(left, right_branch)
    mine, other, right_last = first_products(place, codes, lefts[:-1], rights, slots)
    far, final = lefts[-1]
    other = last_products(codes, far, final, right_last, other, 1, slots)
    coming = across(other, "col", 1)
    mine = last_products(codes, far, final, right_last, mine, 0, slots)
    return (mine + coming).astype(jnp.bfloat16)


def solution(mesh):
    return jax.shard_map(
        shards,
        mesh=mesh,
        in_specs=(
            P("row", "col", None, None, None),
            P(),
            P("row", "col", None, None, None, None),
            P(),
        ),
        out_specs=P("row", "col"),
        check_vma=False,
    )
```

```python
import jax
import jax.numpy as jnp
from jax import lax
from jax.experimental import pallas as pl
from jax.experimental.pallas import tpu as pltpu
from jax.sharding import PartitionSpec as P

KT = 8
RT = 2
SMEM = pl.BlockSpec(memory_space=pltpu.SMEM)
VMEM = pl.BlockSpec(memory_space=pltpu.VMEM)


def find_matches(place, left_index, right_index):
    slots = left_index.shape[-1]
    inner, _, _, right_slots = right_index.shape
    left_index = left_index.transpose(2, 0, 1)
    right_index = right_index.transpose(0, 3, 2, 1)

    def kernel(place_ref, li_ref, ri_ref, codes_ref):
        row, z, y = place_ref[0], place_ref[1], place_ref[2]

        @pl.loop(0, inner)
        def _(s):
            zp = z ^ s
            for side in range(2):
                column = 2 * z + (y if side == 0 else 1 - y)
                have = [ri_ref[zp, t, y, column] for t in range(right_slots)]
                for slot in range(slots):
                    at = li_ref[slot, row, 2 * zp + y]
                    k = lax.rem(at, KT)
                    first = 1 + lax.div(at, KT) * right_slots
                    code = jnp.int32(0)
                    for t in range(right_slots):
                        code = jnp.where(have[t] == k, first + t, code)
                    codes_ref[(s * 2 + side) * slots + slot] = jnp.where(at < RT * KT, code, 0)

    return pl.pallas_call(
        kernel,
        out_shape=jax.ShapeDtypeStruct((inner * 2 * slots,), jnp.int32),
        in_specs=[SMEM] * 3,
        out_specs=SMEM,
    )(place, left_index, right_index)


def add_part(codes_ref, s, side, start, slots, left_ref, right_at, right_slots, total_ref):
    tile = total_ref.shape[1]

    @pl.loop(0, left_ref.shape[0])
    def _(slot):
        code = codes_ref[(s * 2 + side) * slots + start + slot]

        @pl.when(code > 0)
        def _():
            i = lax.div(code - 1, right_slots)
            rows = pl.ds(pl.multiple_of(i * tile, tile), tile)
            total_ref[rows, :] += jnp.dot(
                left_ref[slot],
                right_at(lax.rem(code - 1, right_slots)),
                preferred_element_type=jnp.float32,
            )


def first_products(place, codes, lefts, rights, slots):
    parts = [(s, part) for s, block in lefts for part in block]
    count = len(parts)
    inner = len(rights) // 2
    right_slots, tile, _ = rights[0].shape

    def kernel(place_ref, codes_ref, *refs):
        right_refs = refs[count : count + 2 * inner]
        totals = refs[count + 2 * inner : count + 2 * inner + 2]
        last_ref, held = refs[count + 2 * inner + 2 :]
        row, z = place_ref[0], place_ref[1]
        for t in range(inner):
            for side in range(2):
                held[row ^ t, side] = right_refs[2 * t + side][...]
        last_ref[...] = held[z ^ (inner - 1)]
        for side in range(2):
            totals[side][...] = jnp.zeros_like(totals[side])
            start, before = 0, None
            for (s, _), left_ref in zip(parts, refs):
                start = start if s == before else 0
                add_part(
                    codes_ref, s, side, start, slots, left_ref,
                    lambda found, s=s: held[z ^ s, side, found], right_slots, totals[side],
                )
                start, before = start + left_ref.shape[0], s

    return pl.pallas_call(
        kernel,
        out_shape=[jax.ShapeDtypeStruct((RT * tile, tile), jnp.float32)] * 2
        + [jax.ShapeDtypeStruct((2, right_slots, tile, tile), jnp.bfloat16)],
        in_specs=[SMEM] * 2 + [VMEM] * (count + 2 * inner),
        out_specs=[VMEM] * 3,
        scratch_shapes=[pltpu.VMEM((inner, 2, right_slots, tile, tile), jnp.bfloat16)],
        compiler_params=pltpu.CompilerParams(vmem_limit_bytes=32 * 1024 * 1024),
        cost_estimate=pl.CostEstimate(
            flops=4 * inner * slots * tile**3, bytes_accessed=2 * inner * slots * tile**2, transcendentals=0
        ),
    )(place, codes, *[part for _, part in parts], *rights)


def last_products(codes, s, parts, right, total, side, slots):
    count = len(parts)
    right_slots = right.shape[1]

    def kernel(codes_ref, *refs):
        right_ref, total_ref, out_ref = refs[count:]
        out_ref[...] = total_ref[...]
        start = 0
        for left_ref in refs[:count]:
            add_part(
                codes_ref, s, side, start, slots, left_ref,
                lambda found: right_ref[side, found], right_slots, out_ref,
            )
            start += left_ref.shape[0]

    return pl.pallas_call(
        kernel,
        out_shape=jax.ShapeDtypeStruct(total.shape, total.dtype),
        in_specs=[SMEM] + [VMEM] * (count + 2),
        out_specs=VMEM,
        compiler_params=pltpu.CompilerParams(vmem_limit_bytes=16 * 1024 * 1024),
        cost_estimate=pl.CostEstimate(
            flops=2 * slots * 128**3, bytes_accessed=2 * slots * 128**2, transcendentals=0
        ),
    )(codes, *parts, right, total)


def across(block, axis, mask):
    route = [(i, i ^ mask) for i in range(lax.axis_size(axis))]
    return lax.ppermute(block, axis, route)


def crossed(block, mask):
    rows, cols = lax.axis_size("row"), lax.axis_size("col")
    route = [(r * cols + c, (r ^ mask) * cols + (c ^ 1)) for r in range(rows) for c in range(cols)]
    return lax.ppermute(block, ("row", "col"), route)


def gather(block, beside):
    distance = lax.axis_size("col") // 4
    steps = [distance >> n for n in range(distance.bit_length())]
    came = [across(block, "col", 2 * d) for d in steps]
    came, beside = lax.optimization_barrier((came, beside))
    blocks = {0: block, **dict(zip(steps, came))}
    for d in steps:
        for s in sorted(blocks):
            if s ^ d not in blocks and s & (d - 1) == 0:
                blocks[s ^ d] = across(blocks[s], "col", 2 * d)
    return [(s, (blocks[s],)) for s in range(len(blocks))], beside


def shards(left_tiles, left_index, right_tiles, right_index):
    row = lax.axis_index("row")
    col = lax.axis_index("col")
    z, y = col >> 1, col & 1
    left = left_tiles[0, 0]
    right = right_tiles[0, 0]
    slots = left.shape[0]

    place = jnp.stack([row, z, y])
    codes = find_matches(place, left_index, right_index)
    lefts, codes = gather(left, codes)
    given = lax.dynamic_index_in_dim(right, 1 - y, 0, keepdims=False)
    own = lax.dynamic_index_in_dim(right, y, 0, keepdims=False)
    rights = []
    for t in range(0, lax.axis_size("row"), 2):
        pair = [across(own, "row", t) if t else own, crossed(given, t)]
        rights += pair + [across(half, "row", 1) for half in pair]

    mine, other, right_last = first_products(place, codes, lefts[:-1], rights, slots)
    far, final = lefts[-1]
    other = last_products(codes, far, final, right_last, other, 1, slots)
    coming = across(other, "col", 1)
    mine = last_products(codes, far, final, right_last, mine, 0, slots)
    return (mine + coming).astype(jnp.bfloat16)


def solution(mesh):
    return jax.shard_map(
        shards,
        mesh=mesh,
        in_specs=(
            P("row", "col", None, None, None),
            P(),
            P("row", "col", None, None, None, None),
            P(),
        ),
        out_specs=P("row", "col"),
        check_vma=False,
    )
```

```python
import jax
import jax.numpy as jnp
from jax import lax
from jax.experimental import pallas as pl
from jax.experimental.pallas import tpu as pltpu
from jax.sharding import PartitionSpec as P

KT = 8
RT = 2
SMEM = pl.BlockSpec(memory_space=pltpu.SMEM)
VMEM = pl.BlockSpec(memory_space=pltpu.VMEM)


def find_matches(place, left_index, right_index):
    slots = left_index.shape[-1]
    inner, _, _, right_slots = right_index.shape
    left_index = left_index.transpose(2, 0, 1)
    right_index = right_index.transpose(0, 3, 2, 1)

    def kernel(place_ref, li_ref, ri_ref, codes_ref):
        row, z, y = place_ref[0], place_ref[1], place_ref[2]

        @pl.loop(0, inner)
        def _(s):
            zp = z ^ s
            for side in range(2):
                column = 2 * z + (y if side == 0 else 1 - y)
                have = [ri_ref[zp, t, y, column] for t in range(right_slots)]
                for slot in range(slots):
                    at = li_ref[slot, row, 2 * zp + y]
                    k = lax.rem(at, KT)
                    first = 1 + lax.div(at, KT) * right_slots
                    code = jnp.int32(0)
                    for t in range(right_slots):
                        code = jnp.where(have[t] == k, first + t, code)
                    codes_ref[(s * 2 + side) * slots + slot] = jnp.where(at < RT * KT, code, 0)

    return pl.pallas_call(
        kernel,
        out_shape=jax.ShapeDtypeStruct((inner * 2 * slots,), jnp.int32),
        in_specs=[SMEM] * 3,
        out_specs=SMEM,
    )(place, left_index, right_index)


def add_part(codes_ref, s, side, start, slots, left_ref, right_at, right_slots, total_ref):
    tile = total_ref.shape[1]

    @pl.loop(0, left_ref.shape[0])
    def _(slot):
        code = codes_ref[(s * 2 + side) * slots + start + slot]

        @pl.when(code > 0)
        def _():
            i = lax.div(code - 1, right_slots)
            rows = pl.ds(pl.multiple_of(i * tile, tile), tile)
            total_ref[rows, :] += jnp.dot(
                left_ref[slot],
                right_at(lax.rem(code - 1, right_slots)),
                preferred_element_type=jnp.float32,
            )


def first_products(place, codes, lefts, rights, slots):
    parts = [(s, part) for s, block in lefts for part in block]
    count = len(parts)
    inner = len(rights) // 2
    right_slots, tile, _ = rights[0].shape

    def kernel(place_ref, codes_ref, *refs):
        right_refs = refs[count : count + 2 * inner]
        totals = refs[count + 2 * inner : count + 2 * inner + 2]
        last_ref, held = refs[count + 2 * inner + 2 :]
        row, z = place_ref[0], place_ref[1]
        for t in range(inner):
            for side in range(2):
                held[row ^ t, side] = right_refs[2 * t + side][...]
        last_ref[...] = held[z ^ (inner - 1)]
        for side in range(2):
            totals[side][...] = jnp.zeros_like(totals[side])
            start, before = 0, None
            for (s, _), left_ref in zip(parts, refs):
                start = start if s == before else 0
                add_part(
                    codes_ref, s, side, start, slots, left_ref,
                    lambda found, s=s: held[z ^ s, side, found], right_slots, totals[side],
                )
                start, before = start + left_ref.shape[0], s

    return pl.pallas_call(
        kernel,
        out_shape=[jax.ShapeDtypeStruct((RT * tile, tile), jnp.float32)] * 2
        + [jax.ShapeDtypeStruct((2, right_slots, tile, tile), jnp.bfloat16)],
        in_specs=[SMEM] * 2 + [VMEM] * (count + 2 * inner),
        out_specs=[VMEM] * 3,
        scratch_shapes=[pltpu.VMEM((inner, 2, right_slots, tile, tile), jnp.bfloat16)],
        compiler_params=pltpu.CompilerParams(vmem_limit_bytes=32 * 1024 * 1024),
        cost_estimate=pl.CostEstimate(
            flops=4 * inner * slots * tile**3, bytes_accessed=2 * inner * slots * tile**2, transcendentals=0
        ),
    )(place, codes, *[part for _, part in parts], *rights)


def last_products(codes, s, parts, right, total, side, slots):
    count = len(parts)
    right_slots = right.shape[1]

    def kernel(codes_ref, *refs):
        right_ref, total_ref, out_ref = refs[count:]
        out_ref[...] = total_ref[...]
        start = 0
        for left_ref in refs[:count]:
            add_part(
                codes_ref, s, side, start, slots, left_ref,
                lambda found: right_ref[side, found], right_slots, out_ref,
            )
            start += left_ref.shape[0]

    return pl.pallas_call(
        kernel,
        out_shape=jax.ShapeDtypeStruct(total.shape, total.dtype),
        in_specs=[SMEM] + [VMEM] * (count + 2),
        out_specs=VMEM,
        compiler_params=pltpu.CompilerParams(vmem_limit_bytes=16 * 1024 * 1024),
        cost_estimate=pl.CostEstimate(
            flops=2 * slots * 128**3, bytes_accessed=2 * slots * 128**2, transcendentals=0
        ),
    )(codes, *parts, right, total)


def across(block, axis, mask):
    route = [(i, i ^ mask) for i in range(lax.axis_size(axis))]
    return lax.ppermute(block, axis, route)


def crossed(block, mask):
    rows, cols = lax.axis_size("row"), lax.axis_size("col")
    route = [(r * cols + c, (r ^ mask) * cols + (c ^ 1)) for r in range(rows) for c in range(cols)]
    return lax.ppermute(block, ("row", "col"), route)


def gather(block, beside, ahead):
    distance = lax.axis_size("col") // 4
    steps = [distance >> n for n in range(distance.bit_length())]
    later, ahead = lax.optimization_barrier((block, ahead))
    came = [across(later if d == 1 else block, "col", 2 * d) for d in steps]
    came[:-1], beside = lax.optimization_barrier((came[:-1], beside))
    blocks = {0: block, **dict(zip(steps, came))}
    for d in steps:
        for s in sorted(blocks):
            if s ^ d not in blocks and s & (d - 1) == 0:
                blocks[s ^ d] = across(blocks[s], "col", 2 * d)
    return [(s, (blocks[s],)) for s in range(len(blocks))], beside, ahead


def shards(left_tiles, left_index, right_tiles, right_index):
    row = lax.axis_index("row")
    col = lax.axis_index("col")
    z, y = col >> 1, col & 1
    left = left_tiles[0, 0]
    right = right_tiles[0, 0]
    slots = left.shape[0]

    place = jnp.stack([row, z, y])
    codes = find_matches(place, left_index, right_index)
    given = lax.dynamic_index_in_dim(right, 1 - y, 0, keepdims=False)
    own = lax.dynamic_index_in_dim(right, y, 0, keepdims=False)
    lefts, codes, (own, given) = gather(left, codes, (own, given))
    rights = []
    for t in range(0, lax.axis_size("row"), 2):
        pair = [across(own, "row", t) if t else own, crossed(given, t)]
        if not t:
            pair[0], near = lax.optimization_barrier((pair[0], lefts[1][1]))
            lefts[1] = (1, near)
        rights += pair + [across(half, "row", 1) for half in pair]

    mine, other, right_last = first_products(place, codes, lefts[:-1], rights, slots)
    far, final = lefts[-1]
    other = last_products(codes, far, final, right_last, other, 1, slots)
    coming = across(other, "col", 1)
    mine = last_products(codes, far, final, right_last, mine, 0, slots)
    return (mine + coming).astype(jnp.bfloat16)


def solution(mesh):
    return jax.shard_map(
        shards,
        mesh=mesh,
        in_specs=(
            P("row", "col", None, None, None),
            P(),
            P("row", "col", None, None, None, None),
            P(),
        ),
        out_specs=P("row", "col"),
        check_vma=False,
    )
```

```python
import jax
import jax.numpy as jnp
from jax import lax
from jax.experimental import pallas as pl
from jax.experimental.pallas import tpu as pltpu
from jax.sharding import PartitionSpec as P

KT = 8
RT = 2
BITS = 15
LEAST = 100
PAD = 16
SMEM = pl.BlockSpec(memory_space=pltpu.SMEM)
VMEM = pl.BlockSpec(memory_space=pltpu.VMEM)


def position():
    col = lax.axis_index("col")
    return lax.axis_index("row"), col >> 1, col & 1


def find_matches(left_index, right_index):
    slots = left_index.shape[-1]
    inner, _, _, right_slots = right_index.shape
    left_index = left_index.transpose(2, 0, 1)
    right_index = right_index.transpose(0, 3, 2, 1)

    def kernel(li_ref, ri_ref, codes_ref):
        row, z, y = position()

        @pl.loop(0, inner)
        def _(s):
            zp = z ^ s
            for side in range(2):
                column = 2 * z + (y if side == 0 else 1 - y)
                have = [ri_ref[zp, t, y, column] for t in range(right_slots)]
                for slot in range(slots):
                    at = li_ref[slot, row, 2 * zp + y]
                    k = lax.rem(at, KT)
                    first = 1 + lax.div(at, KT) * right_slots
                    code = jnp.int32(0)
                    for t in range(right_slots):
                        code = jnp.where(have[t] == k, first + t, code)
                    codes_ref[(s * 2 + side) * slots + slot] = jnp.where(at < RT * KT, code, 0)

    return pl.pallas_call(
        kernel,
        out_shape=jax.ShapeDtypeStruct((inner * 2 * slots,), jnp.int32),
        in_specs=[SMEM] * 2,
        out_specs=SMEM,
    )(left_index, right_index)


def add_part(codes_ref, s, side, start, slots, left_ref, right_at, right_slots, total_ref):
    tile = total_ref.shape[1]

    @pl.loop(0, left_ref.shape[0])
    def _(slot):
        code = codes_ref[(s * 2 + side) * slots + start + slot]

        @pl.when(code > 0)
        def _():
            i = lax.div(code - 1, right_slots)
            rows = pl.ds(pl.multiple_of(i * tile, tile), tile)
            total_ref[rows, :] += jnp.dot(
                left_ref[slot],
                right_at(lax.rem(code - 1, right_slots)),
                preferred_element_type=jnp.float32,
            )


def first_products(codes, lefts, rights, slots):
    parts = [(s, part) for s, block in lefts for part in block]
    count = len(parts)
    inner = len(rights) // 2
    right_slots, tile, _ = rights[0].shape

    def kernel(codes_ref, *refs):
        right_refs = refs[count : count + 2 * inner]
        totals = refs[count + 2 * inner : count + 2 * inner + 2]
        last_ref, held = refs[count + 2 * inner + 2 :]
        row, z, _ = position()
        for t in range(inner):
            for side in range(2):
                held[row ^ t, side] = right_refs[2 * t + side][...]
        last_ref[...] = held[z ^ (inner - 1)]
        for side in range(2):
            totals[side][...] = jnp.zeros_like(totals[side])
            start, before = 0, None
            for (s, _), left_ref in zip(parts, refs):
                start = start if s == before else 0
                add_part(
                    codes_ref, s, side, start, slots, left_ref,
                    lambda found, s=s: held[z ^ s, side, found], right_slots, totals[side],
                )
                start, before = start + left_ref.shape[0], s

    return pl.pallas_call(
        kernel,
        out_shape=[jax.ShapeDtypeStruct((RT * tile, tile), jnp.float32)] * 2
        + [jax.ShapeDtypeStruct((2, right_slots, tile, tile), jnp.bfloat16)],
        in_specs=[SMEM] + [VMEM] * (count + 2 * inner),
        out_specs=[VMEM] * 3,
        scratch_shapes=[pltpu.VMEM((inner, 2, right_slots, tile, tile), jnp.bfloat16)],
        compiler_params=pltpu.CompilerParams(vmem_limit_bytes=32 * 1024 * 1024),
        cost_estimate=pl.CostEstimate(
            flops=4 * inner * slots * tile**3, bytes_accessed=2 * inner * slots * tile**2, transcendentals=0
        ),
    )(codes, *[part for _, part in parts], *rights)


def last_products(codes, s, parts, right, total, side, slots, finish, out_shape):
    count = len(parts)
    right_slots = right.shape[1]

    def kernel(codes_ref, *refs):
        right_ref, total_ref, out_ref, sum_ref = refs[count:]
        sum_ref[...] = total_ref[...]
        start = 0
        for left_ref in refs[:count]:
            add_part(
                codes_ref, s, side, start, slots, left_ref,
                lambda found: right_ref[side, found], right_slots, sum_ref,
            )
            start += left_ref.shape[0]
        finish(sum_ref, out_ref)

    return pl.pallas_call(
        kernel,
        out_shape=out_shape,
        in_specs=[SMEM] + [VMEM] * (count + 2),
        out_specs=VMEM,
        scratch_shapes=[pltpu.VMEM(total.shape, total.dtype)],
        compiler_params=pltpu.CompilerParams(vmem_limit_bytes=16 * 1024 * 1024),
        cost_estimate=pl.CostEstimate(
            flops=2 * slots * 128**3, bytes_accessed=2 * slots * 128**2, transcendentals=0
        ),
    )(codes, *parts, right, total)


def write_sum(sum_ref, out_ref):
    out_ref[...] = sum_ref[...]


def write_coded(sum_ref, out_ref):
    tile = sum_ref.shape[1]
    exponents = jnp.zeros((PAD, tile), jnp.float32)
    for i in range(RT):
        values = sum_ref[i * tile : (i + 1) * tile, :]
        largest = jnp.max(jnp.abs(values), axis=0, keepdims=True)
        exponent = jnp.clip(jnp.floor(jnp.log2(largest)) + 1.0, -LEAST, LEAST)
        coded = jnp.round(values * jnp.exp2(BITS - exponent))
        coded = jnp.clip(coded, -(2.0**BITS) + 1.0, 2.0**BITS - 1.0)
        out_ref[i * tile : (i + 1) * tile, :] = coded.astype(jnp.int32).astype(jnp.int16)
        at = lax.broadcasted_iota(jnp.int32, (PAD, tile), 0)
        exponents = jnp.where(at == i, exponent, exponents)
    out_ref[RT * tile :, :] = exponents.astype(jnp.int32).astype(jnp.int16)


def add_coded(total, coded):
    def kernel(total_ref, coded_ref, out_ref):
        tile = total_ref.shape[1]
        exponents = coded_ref[RT * tile :, :].astype(jnp.int32).astype(jnp.float32)
        for i in range(RT):
            rows = slice(i * tile, (i + 1) * tile)
            scale = jnp.exp2(exponents[i : i + 1, :] - BITS)
            values = coded_ref[rows, :].astype(jnp.int32).astype(jnp.float32)
            out_ref[rows, :] = (total_ref[rows, :] + values * scale).astype(out_ref.dtype)

    return pl.pallas_call(
        kernel,
        out_shape=jax.ShapeDtypeStruct(total.shape, jnp.bfloat16),
        in_specs=[VMEM] * 2,
        out_specs=VMEM,
    )(total, coded)


def across(block, axis, mask):
    route = [(i, i ^ mask) for i in range(lax.axis_size(axis))]
    return lax.ppermute(block, axis, route)


def crossed(block, mask):
    rows, cols = lax.axis_size("row"), lax.axis_size("col")
    route = [(r * cols + c, (r ^ mask) * cols + (c ^ 1)) for r in range(rows) for c in range(cols)]
    return lax.ppermute(block, ("row", "col"), route)


def gather(block, beside, ahead):
    distance = lax.axis_size("col") // 4
    steps = [distance >> n for n in range(distance.bit_length())]
    later, ahead = lax.optimization_barrier((block, ahead))
    came = [across(later if d == 1 else block, "col", 2 * d) for d in steps]
    came[:-1], beside = lax.optimization_barrier((came[:-1], beside))
    blocks = {0: block, **dict(zip(steps, came))}
    for d in steps:
        for s in sorted(blocks):
            if s ^ d not in blocks and s & (d - 1) == 0:
                blocks[s ^ d] = across(blocks[s], "col", 2 * d)
    return [(s, (blocks[s],)) for s in range(len(blocks))], beside, ahead


def shards(left_tiles, left_index, right_tiles, right_index):
    y = lax.axis_index("col") & 1
    left = left_tiles[0, 0]
    right = right_tiles[0, 0]
    slots = left.shape[0]

    codes = find_matches(left_index, right_index)
    given = lax.dynamic_index_in_dim(right, 1 - y, 0, keepdims=False)
    own = lax.dynamic_index_in_dim(right, y, 0, keepdims=False)
    lefts, codes, (own, given) = gather(left, codes, (own, given))
    rights = []
    for t in range(0, lax.axis_size("row"), 2):
        pair = [across(own, "row", t) if t else own, crossed(given, t)]
        if not t:
            pair[0], near = lax.optimization_barrier((pair[0], lefts[1][1]))
            lefts[1] = (1, near)
        rights += pair + [across(half, "row", 1) for half in pair]

    mine, other, right_last = first_products(codes, lefts[:-1], rights, slots)
    far, final = lefts[-1]
    last = (codes, far, final, right_last)
    rows, tile = mine.shape
    coded = last_products(
        *last, other, 1, slots, write_coded, jax.ShapeDtypeStruct((rows + PAD, tile), jnp.int16)
    )
    coming = across(coded, "col", 1)
    mine = last_products(*last, mine, 0, slots, write_sum, jax.ShapeDtypeStruct((rows, tile), jnp.float32))
    return add_coded(mine, coming)


def solution(mesh):
    return jax.shard_map(
        shards,
        mesh=mesh,
        in_specs=(
            P("row", "col", None, None, None),
            P(),
            P("row", "col", None, None, None, None),
            P(),
        ),
        out_specs=P("row", "col"),
        check_vma=False,
    )
```

```python
import jax
import jax.numpy as jnp
from jax import lax
from jax.experimental import pallas as pl
from jax.experimental.pallas import tpu as pltpu
from jax.sharding import PartitionSpec as P

KT = 8
RT = 2
BITS = 15
LEAST = 100
PAD = 16
SMEM = pl.BlockSpec(memory_space=pltpu.SMEM)
VMEM = pl.BlockSpec(memory_space=pltpu.VMEM)


def position():
    col = lax.axis_index("col")
    return lax.axis_index("row"), col >> 1, col & 1


def find_matches(left_index, right_index):
    slots = left_index.shape[-1]
    inner, _, _, right_slots = right_index.shape
    left_index = left_index.transpose(2, 0, 1)
    right_index = right_index.transpose(0, 3, 2, 1)

    def kernel(li_ref, ri_ref, codes_ref):
        row, z, y = position()

        @pl.loop(0, inner)
        def _(s):
            zp = z ^ s
            for side in range(2):
                column = 2 * z + (y if side == 0 else 1 - y)
                have = [ri_ref[zp, t, y, column] for t in range(right_slots)]
                for slot in range(slots):
                    at = li_ref[slot, row, 2 * zp + y]
                    k = lax.rem(at, KT)
                    first = 1 + lax.div(at, KT) * right_slots
                    code = jnp.int32(0)
                    for t in range(right_slots):
                        code = jnp.where(have[t] == k, first + t, code)
                    codes_ref[(s * 2 + side) * slots + slot] = jnp.where(at < RT * KT, code, 0)

    return pl.pallas_call(
        kernel,
        out_shape=jax.ShapeDtypeStruct((inner * 2 * slots,), jnp.int32),
        in_specs=[SMEM] * 2,
        out_specs=SMEM,
    )(left_index, right_index)


def add_part(codes_ref, s, side, start, slots, left_ref, right_at, right_slots, total_ref):
    tile = total_ref.shape[1]

    @pl.loop(0, left_ref.shape[0])
    def _(slot):
        code = codes_ref[(s * 2 + side) * slots + start + slot]

        @pl.when(code > 0)
        def _():
            i = lax.div(code - 1, right_slots)
            rows = pl.ds(pl.multiple_of(i * tile, tile), tile)
            total_ref[rows, :] += jnp.dot(
                left_ref[slot],
                right_at(lax.rem(code - 1, right_slots)),
                preferred_element_type=jnp.float32,
            )


def first_products(codes, lefts, rights, slots):
    parts = [(s, part) for s, block in lefts for part in block]
    count = len(parts)
    inner = len(rights) // 2
    right_slots, tile, _ = rights[0].shape

    def kernel(codes_ref, *refs):
        right_refs = refs[count : count + 2 * inner]
        totals = refs[count + 2 * inner : count + 2 * inner + 2]
        last_ref, held = refs[count + 2 * inner + 2 :]
        row, z, _ = position()
        for t in range(inner):
            for side in range(2):
                held[row ^ t, side] = right_refs[2 * t + side][...]
        last_ref[...] = held[z ^ (inner - 1)]
        for side in range(2):
            totals[side][...] = jnp.zeros_like(totals[side])
            start, before = 0, None
            for (s, _), left_ref in zip(parts, refs):
                start = start if s == before else 0
                add_part(
                    codes_ref, s, side, start, slots, left_ref,
                    lambda found, s=s: held[z ^ s, side, found], right_slots, totals[side],
                )
                start, before = start + left_ref.shape[0], s

    return pl.pallas_call(
        kernel,
        out_shape=[jax.ShapeDtypeStruct((RT * tile, tile), jnp.float32)] * 2
        + [jax.ShapeDtypeStruct((2, right_slots, tile, tile), jnp.bfloat16)],
        in_specs=[SMEM] + [VMEM] * (count + 2 * inner),
        out_specs=[VMEM] * 3,
        scratch_shapes=[pltpu.VMEM((inner, 2, right_slots, tile, tile), jnp.bfloat16)],
        compiler_params=pltpu.CompilerParams(vmem_limit_bytes=32 * 1024 * 1024),
        cost_estimate=pl.CostEstimate(
            flops=4 * inner * slots * tile**3, bytes_accessed=2 * inner * slots * tile**2, transcendentals=0
        ),
    )(codes, *[part for _, part in parts], *rights)


def last_products(codes, s, parts, right, total, side, slots, finish, out_shape):
    count = len(parts)
    right_slots = right.shape[1]

    def kernel(codes_ref, *refs):
        right_ref, total_ref, out_ref, sum_ref = refs[count:]
        sum_ref[...] = total_ref[...]
        start = 0
        for left_ref in refs[:count]:
            add_part(
                codes_ref, s, side, start, slots, left_ref,
                lambda found: right_ref[side, found], right_slots, sum_ref,
            )
            start += left_ref.shape[0]
        finish(sum_ref, out_ref)

    return pl.pallas_call(
        kernel,
        out_shape=out_shape,
        in_specs=[SMEM] + [VMEM] * (count + 2),
        out_specs=VMEM,
        scratch_shapes=[pltpu.VMEM(total.shape, total.dtype)],
        compiler_params=pltpu.CompilerParams(vmem_limit_bytes=16 * 1024 * 1024),
        cost_estimate=pl.CostEstimate(
            flops=2 * slots * 128**3, bytes_accessed=2 * slots * 128**2, transcendentals=0
        ),
    )(codes, *parts, right, total)


def write_sum(sum_ref, out_ref):
    out_ref[...] = sum_ref[...]


def write_coded(sum_ref, out_ref):
    tile = sum_ref.shape[1]
    exponents = jnp.zeros((PAD, tile), jnp.float32)
    for i in range(RT):
        values = sum_ref[i * tile : (i + 1) * tile, :]
        largest = jnp.max(jnp.abs(values), axis=0, keepdims=True)
        exponent = jnp.clip(jnp.floor(jnp.log2(largest)) + 1.0, -LEAST, LEAST)
        coded = jnp.round(values * jnp.exp2(BITS - exponent))
        coded = jnp.clip(coded, -(2.0**BITS) + 1.0, 2.0**BITS - 1.0)
        out_ref[i * tile : (i + 1) * tile, :] = coded.astype(jnp.int32).astype(jnp.int16)
        at = lax.broadcasted_iota(jnp.int32, (PAD, tile), 0)
        exponents = jnp.where(at == i, exponent, exponents)
    out_ref[RT * tile :, :] = exponents.astype(jnp.int32).astype(jnp.int16)


def add_coded(total, coded):
    tile = total.shape[1]
    exponents = coded[RT * tile : RT * tile + RT].astype(jnp.float32)
    scale = jnp.repeat(jnp.exp2(exponents - BITS), tile, axis=0)
    return (total + coded[: RT * tile].astype(jnp.float32) * scale).astype(jnp.bfloat16)


def across(block, axis, mask):
    route = [(i, i ^ mask) for i in range(lax.axis_size(axis))]
    return lax.ppermute(block, axis, route)


def crossed(block, mask):
    rows, cols = lax.axis_size("row"), lax.axis_size("col")
    route = [(r * cols + c, (r ^ mask) * cols + (c ^ 1)) for r in range(rows) for c in range(cols)]
    return lax.ppermute(block, ("row", "col"), route)


def gather(block, beside, ahead):
    distance = lax.axis_size("col") // 4
    steps = [distance >> n for n in range(distance.bit_length())]
    later, ahead = lax.optimization_barrier((block, ahead))
    came = [across(later if d == 1 else block, "col", 2 * d) for d in steps]
    came[:-1], beside = lax.optimization_barrier((came[:-1], beside))
    blocks = {0: block, **dict(zip(steps, came))}
    for d in steps:
        for s in sorted(blocks):
            if s ^ d not in blocks and s & (d - 1) == 0:
                blocks[s ^ d] = across(blocks[s], "col", 2 * d)
    return [(s, (blocks[s],)) for s in range(len(blocks))], beside, ahead


def shards(left_tiles, left_index, right_tiles, right_index):
    y = lax.axis_index("col") & 1
    left = left_tiles[0, 0]
    right = right_tiles[0, 0]
    slots = left.shape[0]

    codes = find_matches(left_index, right_index)
    given = lax.dynamic_index_in_dim(right, 1 - y, 0, keepdims=False)
    own = lax.dynamic_index_in_dim(right, y, 0, keepdims=False)
    lefts, codes, (own, given) = gather(left, codes, (own, given))
    rights = []
    for t in range(0, lax.axis_size("row"), 2):
        pair = [across(own, "row", t) if t else own, crossed(given, t)]
        if not t:
            pair[0], near = lax.optimization_barrier((pair[0], lefts[1][1]))
            lefts[1] = (1, near)
        rights += pair + [across(half, "row", 1) for half in pair]

    mine, other, right_last = first_products(codes, lefts[:-1], rights, slots)
    far, final = lefts[-1]
    last = (codes, far, final, right_last)
    rows, tile = mine.shape
    coded = last_products(
        *last, other, 1, slots, write_coded, jax.ShapeDtypeStruct((rows + PAD, tile), jnp.int16)
    )
    coming = across(coded, "col", 1)
    mine = last_products(*last, mine, 0, slots, write_sum, jax.ShapeDtypeStruct((rows, tile), jnp.float32))
    return add_coded(mine, coming)


def solution(mesh):
    return jax.shard_map(
        shards,
        mesh=mesh,
        in_specs=(
            P("row", "col", None, None, None),
            P(),
            P("row", "col", None, None, None, None),
            P(),
        ),
        out_specs=P("row", "col"),
        check_vma=False,
    )
```

```python
import jax
import jax.numpy as jnp
from jax import lax
from jax.experimental import pallas as pl
from jax.experimental.pallas import tpu as pltpu
from jax.sharding import PartitionSpec as P

KT = 8
RT = 2
BITS = 15
LEAST = 100
PAD = 16
SMEM = pl.BlockSpec(memory_space=pltpu.SMEM)
VMEM = pl.BlockSpec(memory_space=pltpu.VMEM)


def position():
    col = lax.axis_index("col")
    return lax.axis_index("row"), col >> 1, col & 1


def find_matches(left_index, right_index):
    slots = left_index.shape[-1]
    inner, _, _, right_slots = right_index.shape
    left_index = left_index.transpose(2, 0, 1)
    right_index = right_index.transpose(0, 3, 2, 1)

    def kernel(li_ref, ri_ref, codes_ref):
        row, z, y = position()

        @pl.loop(0, inner)
        def _(s):
            zp = z ^ s
            for side in range(2):
                column = 2 * z + (y if side == 0 else 1 - y)
                have = [ri_ref[zp, t, y, column] for t in range(right_slots)]
                for slot in range(slots):
                    at = li_ref[slot, row, 2 * zp + y]
                    k = lax.rem(at, KT)
                    first = 1 + lax.div(at, KT) * right_slots
                    code = jnp.int32(0)
                    for t in range(right_slots):
                        code = jnp.where(have[t] == k, first + t, code)
                    codes_ref[(s * 2 + side) * slots + slot] = jnp.where(at < RT * KT, code, 0)

    return pl.pallas_call(
        kernel,
        out_shape=jax.ShapeDtypeStruct((inner * 2 * slots,), jnp.int32),
        in_specs=[SMEM] * 2,
        out_specs=SMEM,
    )(left_index, right_index)


def add_block(codes_ref, s, side, left_ref, right_at, right_slots, total_ref):
    slots, tile, _ = left_ref.shape

    @pl.loop(0, slots)
    def _(slot):
        code = codes_ref[(s * 2 + side) * slots + slot]

        @pl.when(code > 0)
        def _():
            i = lax.div(code - 1, right_slots)
            rows = pl.ds(pl.multiple_of(i * tile, tile), tile)
            total_ref[rows, :] += jnp.dot(
                left_ref[slot],
                right_at(lax.rem(code - 1, right_slots)),
                preferred_element_type=jnp.float32,
            )


def first_products(codes, lefts, rights):
    count = len(lefts)
    inner = len(rights) // 2
    right_slots, tile, _ = rights[0].shape
    slots = lefts[0].shape[0]

    def kernel(codes_ref, *refs):
        left_refs = refs[:count]
        right_refs = refs[count : count + 2 * inner]
        totals = refs[count + 2 * inner : count + 2 * inner + 2]
        last_ref, held = refs[count + 2 * inner + 2 :]
        row, z, _ = position()
        for t in range(inner):
            for side in range(2):
                held[row ^ t, side] = right_refs[2 * t + side][...]
        last_ref[...] = held[z ^ (inner - 1)]
        for side in range(2):
            totals[side][...] = jnp.zeros_like(totals[side])
            for mask, left_ref in enumerate(left_refs):
                s = z_distance(mask, inner, row & 1)
                add_block(
                    codes_ref, s, side, left_ref,
                    lambda found, s=s: held[z ^ s, side, found], right_slots, totals[side],
                )

    return pl.pallas_call(
        kernel,
        out_shape=[jax.ShapeDtypeStruct((RT * tile, tile), jnp.float32)] * 2
        + [jax.ShapeDtypeStruct((2, right_slots, tile, tile), jnp.bfloat16)],
        in_specs=[SMEM] + [VMEM] * (count + 2 * inner),
        out_specs=[VMEM] * 3,
        scratch_shapes=[pltpu.VMEM((inner, 2, right_slots, tile, tile), jnp.bfloat16)],
        compiler_params=pltpu.CompilerParams(vmem_limit_bytes=32 * 1024 * 1024),
        cost_estimate=pl.CostEstimate(
            flops=4 * inner * slots * tile**3, bytes_accessed=2 * inner * slots * tile**2, transcendentals=0
        ),
    )(codes, *lefts, *rights)


def last_products(codes, left, right, total, side, finish, out_shape):
    slots, tile, _ = left.shape
    right_slots = right.shape[1]
    last = codes.shape[0] // (2 * slots) - 1

    def kernel(codes_ref, left_ref, right_ref, total_ref, out_ref, sum_ref):
        sum_ref[...] = total_ref[...]
        add_block(
            codes_ref, last, side, left_ref, lambda found: right_ref[side, found], right_slots, sum_ref
        )
        finish(sum_ref, out_ref)

    return pl.pallas_call(
        kernel,
        out_shape=out_shape,
        in_specs=[SMEM] + [VMEM] * 3,
        out_specs=VMEM,
        scratch_shapes=[pltpu.VMEM(total.shape, total.dtype)],
        compiler_params=pltpu.CompilerParams(vmem_limit_bytes=16 * 1024 * 1024),
        cost_estimate=pl.CostEstimate(
            flops=2 * slots * tile**3, bytes_accessed=2 * slots * tile**2, transcendentals=0
        ),
    )(codes, left, right, total)


def write_sum(sum_ref, out_ref):
    out_ref[...] = sum_ref[...]


def write_coded(sum_ref, out_ref):
    tile = sum_ref.shape[1]
    exponents = jnp.zeros((PAD, tile), jnp.float32)
    for i in range(RT):
        values = sum_ref[i * tile : (i + 1) * tile, :]
        largest = jnp.max(jnp.abs(values), axis=0, keepdims=True)
        exponent = jnp.clip(jnp.floor(jnp.log2(largest)) + 1.0, -LEAST, LEAST)
        coded = jnp.round(values * jnp.exp2(BITS - exponent))
        coded = jnp.clip(coded, -(2.0**BITS) + 1.0, 2.0**BITS - 1.0)
        out_ref[i * tile : (i + 1) * tile, :] = coded.astype(jnp.int32).astype(jnp.int16)
        at = lax.broadcasted_iota(jnp.int32, (PAD, tile), 0)
        exponents = jnp.where(at == i, exponent, exponents)
    out_ref[RT * tile :, :] = exponents.astype(jnp.int32).astype(jnp.int16)


def add_coded(total, coded):
    tile = total.shape[1]
    exponents = coded[RT * tile : RT * tile + RT].astype(jnp.float32)
    scale = jnp.repeat(jnp.exp2(exponents - BITS), tile, axis=0)
    return (total + coded[: RT * tile].astype(jnp.float32) * scale).astype(jnp.bfloat16)


def across(block, axis, mask):
    route = [(i, i ^ mask) for i in range(lax.axis_size(axis))]
    return lax.ppermute(block, axis, route)


def crossed(block, mask):
    rows, cols = lax.axis_size("row"), lax.axis_size("col")
    route = [(r * cols + c, (r ^ mask) * cols + (c ^ 1)) for r in range(rows) for c in range(cols)]
    return lax.ppermute(block, ("row", "col"), route)


def z_distance(mask, places, core):
    far = sum(places >> 1 >> n for n in range(places.bit_length()) if mask >> n & 1)
    return jnp.where(core == 1, far, mask)


def gather(block, ahead):
    rows, cols = lax.axis_size("row"), lax.axis_size("col")
    places = cols // 2

    def hop(block, step):
        masks = [2 << step, places >> step]
        route = [
            (r * cols + c, r * cols + (c ^ masks[r & 1])) for r in range(rows) for c in range(cols)
        ]
        return lax.ppermute(block, ("row", "col"), route)

    blocks = {0: block, 1: hop(block, 0)}
    later, ahead = lax.optimization_barrier((block, ahead))
    for step in range(1, places.bit_length() - 1):
        for mask in range(1 << step):
            blocks[mask | 1 << step] = hop(blocks[mask] if mask else later, step)
    return [blocks[mask] for mask in range(places)], ahead


def shards(left_tiles, left_index, right_tiles, right_index):
    y = lax.axis_index("col") & 1
    left = left_tiles[0, 0]
    right = right_tiles[0, 0]
    slots = left.shape[0]

    codes = find_matches(left_index, right_index)
    given = lax.dynamic_index_in_dim(right, 1 - y, 0, keepdims=False)
    own = lax.dynamic_index_in_dim(right, y, 0, keepdims=False)
    lefts, (own, given) = gather(left, (own, given))
    rights = []
    for t in range(0, lax.axis_size("row"), 2):
        pair = [across(own, "row", t) if t else own, crossed(given, t)]
        if not t:
            pair[0], lefts[2] = lax.optimization_barrier((pair[0], lefts[2]))
        rights += pair + [across(half, "row", 1) for half in pair]

    mine, other, right_last = first_products(codes, lefts[:-1], rights)
    last = (codes, lefts[-1], right_last)
    rows, tile = mine.shape
    coded = last_products(
        *last, other, 1, write_coded, jax.ShapeDtypeStruct((rows + PAD, tile), jnp.int16)
    )
    coming = across(coded, "col", 1)
    mine = last_products(*last, mine, 0, write_sum, jax.ShapeDtypeStruct((rows, tile), jnp.float32))
    return add_coded(mine, coming)


def solution(mesh):
    return jax.shard_map(
        shards,
        mesh=mesh,
        in_specs=(
            P("row", "col", None, None, None),
            P(),
            P("row", "col", None, None, None, None),
            P(),
        ),
        out_specs=P("row", "col"),
        check_vma=False,
    )
```

```python
import jax
import jax.numpy as jnp
from jax import lax
from jax.experimental import pallas as pl
from jax.experimental.pallas import tpu as pltpu
from jax.sharding import PartitionSpec as P

KT = 8
RT = 2
BITS = 15
LEAST = 100
PAD = 16
SIDES = 4
FLOPS = 10**10
SMEM = pl.BlockSpec(memory_space=pltpu.SMEM)
VMEM = pl.BlockSpec(memory_space=pltpu.VMEM)


def position():
    col = lax.axis_index("col")
    return lax.axis_index("row"), col >> 1, col & 1


def find_matches(left_index, right_index):
    slots = left_index.shape[-1]
    inner, _, _, right_slots = right_index.shape
    left_index = left_index.transpose(2, 0, 1)
    right_index = right_index.transpose(0, 3, 2, 1)

    def kernel(li_ref, ri_ref, codes_ref):
        row, z, y = position()

        @pl.loop(0, inner // 2)
        def _(n):
            zp = z ^ (2 * n)
            for side in range(SIDES):
                column = 2 * (z ^ (side >> 1)) + (y ^ (side & 1))
                have = [ri_ref[zp, t, y, column] for t in range(right_slots)]
                for slot in range(slots):
                    at = li_ref[slot, row, 2 * zp + y]
                    k = lax.rem(at, KT)
                    first = 1 + lax.div(at, KT) * right_slots
                    code = jnp.int32(0)
                    for t in range(right_slots):
                        code = jnp.where(have[t] == k, first + t, code)
                    codes_ref[(n * SIDES + side) * slots + slot] = jnp.where(at < RT * KT, code, 0)

    return pl.pallas_call(
        kernel,
        out_shape=jax.ShapeDtypeStruct((inner // 2 * SIDES * slots,), jnp.int32),
        in_specs=[SMEM] * 2,
        out_specs=SMEM,
    )(left_index, right_index)


def add_block(codes_ref, n, side, left_ref, right_at, right_slots, total_ref):
    slots, tile, _ = left_ref.shape

    @pl.loop(0, slots)
    def _(slot):
        code = codes_ref[(n * SIDES + side) * slots + slot]

        @pl.when(code > 0)
        def _():
            i = lax.div(code - 1, right_slots)
            rows = pl.ds(pl.multiple_of(i * tile, tile), tile)
            total_ref[rows, :] += jnp.dot(
                left_ref[slot],
                right_at(lax.rem(code - 1, right_slots)),
                preferred_element_type=jnp.float32,
            )


def products(codes, lefts, rights, sides, finish, out_shape):
    count = len(lefts)
    slots, tile, _ = lefts[0].shape
    halves = len(rights[0])
    right_slots = rights[0][0].shape[0]

    def kernel(codes_ref, *refs):
        left_refs = refs[:count]
        here_refs = refs[count : count + halves]
        there_refs = refs[count + halves : count + 2 * halves]
        outs = refs[count + 2 * halves : -2]
        total_ref, held = refs[-2:]
        row, z, _ = position()
        odd = (row ^ z) & 1
        for m in range(halves):
            held[odd, m] = here_refs[m][...]
            held[1 - odd, m] = there_refs[m][...]
        for side, out_ref in zip(sides, outs):
            total_ref[...] = jnp.zeros_like(total_ref)
            for n, left_ref in enumerate(left_refs):
                at = row ^ odd ^ z ^ (2 * n)
                add_block(
                    codes_ref, n, side, left_ref,
                    lambda found, at=at: held[side >> 1, at + (side & 1), found], right_slots, total_ref,
                )
            finish(total_ref, out_ref)

    return pl.pallas_call(
        kernel,
        out_shape=[out_shape] * len(sides),
        in_specs=[SMEM] + [VMEM] * (count + 2 * halves),
        out_specs=[VMEM] * len(sides),
        scratch_shapes=[
            pltpu.VMEM((RT * tile, tile), jnp.float32),
            pltpu.VMEM((2, halves) + rights[0][0].shape, rights[0][0].dtype),
        ],
        compiler_params=pltpu.CompilerParams(vmem_limit_bytes=32 * 1024 * 1024),
        cost_estimate=pl.CostEstimate(
            flops=2 * len(sides) * count * slots * tile**3,
            bytes_accessed=2 * count * slots * tile**2,
            transcendentals=0,
        ),
    )(codes, *lefts, *rights[0], *rights[1])


def write_sum(sum_ref, out_ref):
    out_ref[...] = sum_ref[...]


def write_coded(sum_ref, out_ref):
    tile = sum_ref.shape[1]
    exponents = jnp.zeros((PAD, tile), jnp.float32)
    for i in range(RT):
        values = sum_ref[i * tile : (i + 1) * tile, :]
        largest = jnp.max(jnp.abs(values), axis=0, keepdims=True)
        exponent = jnp.clip(jnp.floor(jnp.log2(largest)) + 1.0, -LEAST, LEAST)
        coded = jnp.round(values * jnp.exp2(BITS - exponent))
        coded = jnp.clip(coded, -(2.0**BITS) + 1.0, 2.0**BITS - 1.0)
        out_ref[i * tile : (i + 1) * tile, :] = coded.astype(jnp.int32).astype(jnp.int16)
        at = lax.broadcasted_iota(jnp.int32, (PAD, tile), 0)
        exponents = jnp.where(at == i, exponent, exponents)
    out_ref[RT * tile :, :] = exponents.astype(jnp.int32).astype(jnp.int16)


def decoded(coded):
    tile = coded.shape[1]
    exponents = coded[RT * tile : RT * tile + RT].astype(jnp.float32)
    scale = jnp.repeat(jnp.exp2(exponents - BITS), tile, axis=0)
    return coded[: RT * tile].astype(jnp.float32) * scale


def travel(block, source):
    rows, cols = lax.axis_size("row"), lax.axis_size("col")
    route = []
    for r in range(rows):
        for c in range(cols):
            row, z, y = source(r, c >> 1, c & 1)
            route.append((row * cols + 2 * z + y, r * cols + c))
    return lax.ppermute(block, ("row", "col"), route)


def hold(block, flops):
    whole = pl.BlockSpec(memory_space=pl.ANY)
    return pl.pallas_call(
        lambda *refs: None,
        out_shape=jax.ShapeDtypeStruct(block.shape, block.dtype),
        in_specs=[whole],
        out_specs=whole,
        input_output_aliases={0: 0},
        cost_estimate=pl.CostEstimate(flops=flops, bytes_accessed=0, transcendentals=0),
    )(block)


def gather_left(block):
    blocks = {0: block}
    distance = lax.axis_size("col") // 4
    while distance > 1:
        for s in sorted(blocks):
            blocks[s ^ distance] = travel(blocks[s], lambda r, z, y: (r, z ^ distance, y))
        distance //= 2
    return [blocks[s] for s in sorted(blocks)]


def gather_right(right):
    y = lax.axis_index("col") & 1
    given = lax.dynamic_index_in_dim(right, 1 - y, 0, keepdims=False)
    own = lax.dynamic_index_in_dim(right, y, 0, keepdims=False)
    chips = []
    for t in range(0, lax.axis_size("row"), 2):
        for side, half in enumerate((own, given)):

            def source(r, z, y, t=t, side=side):
                odd = (r ^ z) & 1
                return r ^ odd ^ t, z ^ odd, y ^ side

            chips.append(travel(half, source))
    return chips, [travel(half, lambda r, z, y: (r ^ 1, z, y)) for half in chips]


def shards(left_tiles, left_index, right_tiles, right_index):
    codes = find_matches(left_index, right_index)
    own, *lefts = gather_left(left_tiles[0, 0])
    lefts = [own] + [hold(block, FLOPS) for block in lefts]
    rights = gather_right(right_tiles[0, 0])
    tile = left_tiles.shape[-1]
    coded = jax.ShapeDtypeStruct((RT * tile + PAD, tile), jnp.int16)
    plain = jax.ShapeDtypeStruct((RT * tile, tile), jnp.float32)
    to_give = products(codes, lefts, rights, (1, 2, 3), write_coded, coded)
    (total,) = products(codes, lefts, rights, (0,), write_sum, plain)
    for side, block in enumerate(to_give, 1):
        total += decoded(travel(block, lambda r, z, y: (r, z ^ (side >> 1), y ^ (side & 1))))
    return total.astype(jnp.bfloat16)


def solution(mesh):
    return jax.shard_map(
        shards,
        mesh=mesh,
        in_specs=(
            P("row", "col", None, None, None),
            P(),
            P("row", "col", None, None, None, None),
            P(),
        ),
        out_specs=P("row", "col"),
        check_vma=False,
    )
```

```python
import jax
import jax.numpy as jnp
from jax import lax
from jax.experimental import pallas as pl
from jax.experimental.pallas import tpu as pltpu
from jax.sharding import PartitionSpec as P

KT = 8
RT = 2
FLOPS = 10**10
BITS = 15
LEAST = 100
PAD = 16
SMEM = pl.BlockSpec(memory_space=pltpu.SMEM)
VMEM = pl.BlockSpec(memory_space=pltpu.VMEM)


def position():
    col = lax.axis_index("col")
    return lax.axis_index("row"), col >> 1, col & 1


def find_matches(left_index, right_index):
    slots = left_index.shape[-1]
    inner, _, _, right_slots = right_index.shape
    left_index = left_index.transpose(2, 0, 1)
    right_index = right_index.transpose(0, 3, 2, 1)

    def kernel(li_ref, ri_ref, codes_ref):
        row, z, y = position()

        @pl.loop(0, inner)
        def _(s):
            zp = z ^ s
            for side in range(2):
                column = 2 * z + (y if side == 0 else 1 - y)
                have = [ri_ref[zp, t, y, column] for t in range(right_slots)]
                for slot in range(slots):
                    at = li_ref[slot, row, 2 * zp + y]
                    k = lax.rem(at, KT)
                    first = 1 + lax.div(at, KT) * right_slots
                    code = jnp.int32(0)
                    for t in range(right_slots):
                        code = jnp.where(have[t] == k, first + t, code)
                    codes_ref[(s * 2 + side) * slots + slot] = jnp.where(at < RT * KT, code, 0)

    return pl.pallas_call(
        kernel,
        out_shape=jax.ShapeDtypeStruct((inner * 2 * slots,), jnp.int32),
        in_specs=[SMEM] * 2,
        out_specs=SMEM,
    )(left_index, right_index)


def add_block(codes_ref, s, side, left_ref, right_at, right_slots, total_ref):
    slots, tile, _ = left_ref.shape

    @pl.loop(0, slots)
    def _(slot):
        code = codes_ref[(s * 2 + side) * slots + slot]

        @pl.when(code > 0)
        def _():
            i = lax.div(code - 1, right_slots)
            rows = pl.ds(pl.multiple_of(i * tile, tile), tile)
            total_ref[rows, :] += jnp.dot(
                left_ref[slot],
                right_at(lax.rem(code - 1, right_slots)),
                preferred_element_type=jnp.float32,
            )


def first_products(codes, lefts, rights):
    count = len(lefts)
    places = len(rights) // 2
    right_slots, tile, _ = rights[0].shape
    slots = lefts[0][2].shape[0]

    def kernel(codes_ref, *refs):
        left_refs = refs[:count]
        right_refs = refs[count : count + 2 * places]
        totals = refs[count + 2 * places : count + 2 * places + 2]
        last_ref, held = refs[count + 2 * places + 2 :]
        row, z, _ = position()
        for t in range(places):
            for side in range(2):
                held[row ^ t, side] = right_refs[2 * t + side][...]
        last_ref[...] = held[z ^ (places - 1)]
        for side in range(2):
            totals[side][...] = jnp.zeros_like(totals[side])
            for (outer_s, inner_s, _), left_ref in zip(lefts, left_refs):
                here = [s for s in (outer_s, inner_s) if s is not None]
                s = jnp.where(inner(z) == 1, here[-1], here[0])

                def add(s=s, left_ref=left_ref):
                    add_block(
                        codes_ref, s, side, left_ref,
                        lambda found: held[z ^ s, side, found], right_slots, totals[side],
                    )

                if len(here) == 2:
                    add()
                else:
                    pl.when(inner(z) == (outer_s is None))(add)

    return pl.pallas_call(
        kernel,
        out_shape=[jax.ShapeDtypeStruct((RT * tile, tile), jnp.float32)] * 2
        + [jax.ShapeDtypeStruct((2, right_slots, tile, tile), jnp.bfloat16)],
        in_specs=[SMEM] + [VMEM] * (count + 2 * places),
        out_specs=[VMEM] * 3,
        scratch_shapes=[pltpu.VMEM((places, 2, right_slots, tile, tile), jnp.bfloat16)],
        compiler_params=pltpu.CompilerParams(vmem_limit_bytes=32 * 1024 * 1024),
        cost_estimate=pl.CostEstimate(
            flops=4 * places * slots * tile**3, bytes_accessed=2 * places * slots * tile**2, transcendentals=0
        ),
    )(codes, *[block for _, _, block in lefts], *rights)


def last_products(codes, outward, inward, right, total, side, finish, out_shape):
    slots, tile, _ = outward.shape
    right_slots = right.shape[1]
    last = codes.shape[0] // (2 * slots) - 1

    def kernel(codes_ref, outward_ref, inward_ref, right_ref, total_ref, out_ref, sum_ref):
        _, z, _ = position()
        sum_ref[...] = total_ref[...]
        for place, left_ref in enumerate((outward_ref, inward_ref)):

            @pl.when(inner(z) == place)
            def _(left_ref=left_ref):
                add_block(
                    codes_ref, last, side, left_ref,
                    lambda found: right_ref[side, found], right_slots, sum_ref,
                )

        finish(sum_ref, out_ref)

    return pl.pallas_call(
        kernel,
        out_shape=out_shape,
        in_specs=[SMEM] + [VMEM] * 4,
        out_specs=VMEM,
        scratch_shapes=[pltpu.VMEM(total.shape, total.dtype)],
        compiler_params=pltpu.CompilerParams(vmem_limit_bytes=16 * 1024 * 1024),
        cost_estimate=pl.CostEstimate(
            flops=2 * slots * tile**3, bytes_accessed=2 * slots * tile**2, transcendentals=0
        ),
    )(codes, outward, inward, right, total)


def write_sum(sum_ref, out_ref):
    out_ref[...] = sum_ref[...]


def write_coded(sum_ref, out_ref):
    tile = sum_ref.shape[1]
    exponents = jnp.zeros((PAD, tile), jnp.float32)
    for i in range(RT):
        values = sum_ref[i * tile : (i + 1) * tile, :]
        largest = jnp.max(jnp.abs(values), axis=0, keepdims=True)
        exponent = jnp.clip(jnp.floor(jnp.log2(largest)) + 1.0, -LEAST, LEAST)
        coded = jnp.round(values * jnp.exp2(BITS - exponent))
        coded = jnp.clip(coded, -(2.0**BITS) + 1.0, 2.0**BITS - 1.0)
        out_ref[i * tile : (i + 1) * tile, :] = coded.astype(jnp.int32).astype(jnp.int16)
        at = lax.broadcasted_iota(jnp.int32, (PAD, tile), 0)
        exponents = jnp.where(at == i, exponent, exponents)
    out_ref[RT * tile :, :] = exponents.astype(jnp.int32).astype(jnp.int16)


def add_coded(total, coded):
    tile = total.shape[1]
    exponents = coded[RT * tile : RT * tile + RT].astype(jnp.float32)
    scale = jnp.repeat(jnp.exp2(exponents - BITS), tile, axis=0)
    return (total + coded[: RT * tile].astype(jnp.float32) * scale).astype(jnp.bfloat16)


def across(block, axis, mask):
    route = [(i, i ^ mask) for i in range(lax.axis_size(axis))]
    return lax.ppermute(block, axis, route)


def crossed(block, mask):
    rows, cols = lax.axis_size("row"), lax.axis_size("col")
    route = [(r * cols + c, (r ^ mask) * cols + (c ^ 1)) for r in range(rows) for c in range(cols)]
    return lax.ppermute(block, ("row", "col"), route)


def inner(z):
    return (z ^ z >> 1) & 1


def travel(block, target):
    route = []
    for c in range(lax.axis_size("col")):
        z = target(c >> 1)
        if z is not None:
            route.append((c, 2 * z + (c & 1)))
    return lax.ppermute(block, "col", route)


def hold(block):
    def kernel(block_ref, out_ref):
        out_ref[...] = block_ref[...]

    return pl.pallas_call(
        kernel,
        out_shape=jax.ShapeDtypeStruct(block.shape, block.dtype),
        in_specs=[VMEM],
        out_specs=VMEM,
        cost_estimate=pl.CostEstimate(flops=FLOPS, bytes_accessed=0, transcendentals=0),
    )(block)


def gather(block, beside, ahead):
    bases = {0: block}
    distance = lax.axis_size("col") // 4
    while distance > 2:
        for s in sorted(bases):
            bases[s ^ distance] = travel(bases[s], lambda z: z ^ distance)
        distance //= 2
    found = []
    for s in sorted(bases):
        base = bases[s]
        first = travel(base, lambda z: z ^ (1 if inner(z) else 2))
        if s == 0:
            base, ahead = lax.optimization_barrier((base, ahead))
        second = travel(base, lambda z: z ^ (2 if inner(z) else 1))
        first, beside = lax.optimization_barrier((first, beside))
        outward = hold(travel(first, lambda z: z ^ 1 if inner(z) else None))
        inward = travel(second, lambda z: None if inner(z) else z ^ 1)
        found += [(s, s, bases[s]), (s ^ 1, s ^ 2, first), (s ^ 2, s ^ 1, second)]
        found += [(s ^ 3, None, outward), (None, s ^ 3, inward)]
    return found, beside, ahead


def shards(left_tiles, left_index, right_tiles, right_index):
    y = lax.axis_index("col") & 1
    left = left_tiles[0, 0]
    right = right_tiles[0, 0]

    codes = find_matches(left_index, right_index)
    given = lax.dynamic_index_in_dim(right, 1 - y, 0, keepdims=False)
    own = lax.dynamic_index_in_dim(right, y, 0, keepdims=False)
    lefts, codes, (own, given) = gather(left, codes, (own, given))
    rights = []
    for t in range(0, lax.axis_size("row"), 2):
        pair = [across(own, "row", t) if t else own, crossed(given, t)]
        if not t:
            pair[0], second = lax.optimization_barrier((pair[0], lefts[2][2]))
            lefts[2] = (*lefts[2][:2], second)
        rights += pair + [across(half, "row", 1) for half in pair]

    mine, other, right_last = first_products(codes, lefts[:-2], rights)
    last = (codes, lefts[-2][2], lefts[-1][2], right_last)
    rows, tile = mine.shape
    coded = last_products(
        *last, other, 1, write_coded, jax.ShapeDtypeStruct((rows + PAD, tile), jnp.int16)
    )
    coming = across(coded, "col", 1)
    mine = last_products(*last, mine, 0, write_sum, jax.ShapeDtypeStruct((rows, tile), jnp.float32))
    return add_coded(mine, coming)


def solution(mesh):
    return jax.shard_map(
        shards,
        mesh=mesh,
        in_specs=(
            P("row", "col", None, None, None),
            P(),
            P("row", "col", None, None, None, None),
            P(),
        ),
        out_specs=P("row", "col"),
        check_vma=False,
    )
```

```python
import jax
import jax.numpy as jnp
from jax import lax
from jax.experimental import pallas as pl
from jax.experimental.pallas import tpu as pltpu
from jax.sharding import PartitionSpec as P

KT = 8
RT = 2
SIDES = 3
EARLY = 10**8
LATE = 10**11
BITS = 15
LEAST = 100
PAD = 16
SMEM = pl.BlockSpec(memory_space=pltpu.SMEM)
VMEM = pl.BlockSpec(memory_space=pltpu.VMEM)


def position():
    col = lax.axis_index("col")
    return lax.axis_index("row"), col >> 1, col & 1


def counting(side, places):
    early = [s for s in range(places) if s % 2 == 0 or s == 1]
    return [range(places), early, [s for s in early if s > 1]][side]


def code_at(s, side, places, slots):
    pairs = [(other, at) for at in range(SIDES) for other in counting(at, places)]
    return pairs.index((s, side)) * slots


def find_matches(left_index, right_index):
    slots = left_index.shape[-1]
    places, _, _, right_slots = right_index.shape
    left_index = left_index.transpose(2, 0, 1)
    right_index = right_index.transpose(0, 3, 2, 1)
    total = sum(len(counting(side, places)) for side in range(SIDES)) * slots

    def kernel(li_ref, ri_ref, codes_ref):
        row, z, y = position()
        for side in range(SIDES):
            column = 2 * (z ^ (side >> 1)) + (y ^ min(side, 1))
            for s in counting(side, places):
                zp = z ^ s
                base = code_at(s, side, places, slots)
                have = [ri_ref[zp, t, y, column] for t in range(right_slots)]

                @pl.loop(0, slots)
                def _(slot):
                    at = li_ref[slot, row, 2 * zp + y]
                    k = lax.rem(at, KT)
                    first = 1 + lax.div(at, KT) * right_slots
                    code = jnp.int32(0)
                    for t in range(right_slots):
                        code = jnp.where(have[t] == k, first + t, code)
                    codes_ref[base + slot] = jnp.where(at < RT * KT, code, 0)

    return pl.pallas_call(
        kernel,
        out_shape=jax.ShapeDtypeStruct((total,), jnp.int32),
        in_specs=[SMEM] * 2,
        out_specs=SMEM,
    )(left_index, right_index)


def add_block(codes_ref, base, left_ref, right_at, right_slots, total_ref):
    slots, tile, _ = left_ref.shape

    @pl.loop(0, slots)
    def _(slot):
        code = codes_ref[base + slot]

        @pl.when(code > 0)
        def _():
            i = lax.div(code - 1, right_slots)
            rows = pl.ds(pl.multiple_of(i * tile, tile), tile)
            total_ref[rows, :] += jnp.dot(
                left_ref[slot],
                right_at(lax.rem(code - 1, right_slots)),
                preferred_element_type=jnp.float32,
            )


def products(codes, lefts, rights, sides, finish, out_shape, flops, start=None):
    distances = sorted(lefts)
    count = len(lefts)
    places = len(rights) // 2
    right_slots, tile, _ = rights[0].shape
    slots = lefts[distances[0]].shape[0]
    starts = [] if start is None else [start]

    def kernel(codes_ref, *refs):
        left_refs = dict(zip(distances, refs))
        right_refs = refs[count : count + 2 * places]
        start_refs = refs[count + 2 * places :][: len(starts)]
        outs = refs[count + 2 * places + len(starts) : -2]
        total_ref, held = refs[-2:]
        row, z, _ = position()
        for at in sorted({min(side, 1) for side in sides}):
            for t in range(places):
                held[t, at] = right_refs[2 * t + at][...]
        for side, out_ref in zip(sides, outs):
            total_ref[...] = start_refs[0][...] if starts else jnp.zeros_like(total_ref)
            for s in counting(side, places):
                if s in left_refs:
                    t = row ^ z ^ s ^ (side >> 1)
                    add_block(
                        codes_ref, code_at(s, side, places, slots), left_refs[s],
                        lambda found, t=t: held[t, min(side, 1), found], right_slots, total_ref,
                    )
            finish(total_ref, out_ref)

    return pl.pallas_call(
        kernel,
        out_shape=[out_shape] * len(sides),
        in_specs=[SMEM] + [VMEM] * (count + 2 * places + len(starts)),
        out_specs=[VMEM] * len(sides),
        scratch_shapes=[
            pltpu.VMEM((RT * tile, tile), jnp.float32),
            pltpu.VMEM((places, 2, right_slots, tile, tile), jnp.bfloat16),
        ],
        compiler_params=pltpu.CompilerParams(vmem_limit_bytes=32 * 1024 * 1024),
        cost_estimate=pl.CostEstimate(
            flops=flops,
            bytes_accessed=2 * count * slots * tile**2,
            transcendentals=0,
        ),
    )(codes, *[lefts[s] for s in distances], *rights, *starts)


def write_sum(sum_ref, out_ref):
    out_ref[...] = sum_ref[...]


def write_coded(sum_ref, out_ref):
    tile = sum_ref.shape[1]
    exponents = jnp.zeros((PAD, tile), jnp.float32)
    for i in range(RT):
        values = sum_ref[i * tile : (i + 1) * tile, :]
        largest = jnp.max(jnp.abs(values), axis=0, keepdims=True)
        exponent = jnp.clip(jnp.floor(jnp.log2(largest)) + 1.0, -LEAST, LEAST)
        coded = jnp.round(values * jnp.exp2(BITS - exponent))
        coded = jnp.clip(coded, -(2.0**BITS) + 1.0, 2.0**BITS - 1.0)
        out_ref[i * tile : (i + 1) * tile, :] = coded.astype(jnp.int32).astype(jnp.int16)
        at = lax.broadcasted_iota(jnp.int32, (PAD, tile), 0)
        exponents = jnp.where(at == i, exponent, exponents)
    out_ref[RT * tile :, :] = exponents.astype(jnp.int32).astype(jnp.int16)


def decoded(coded):
    tile = coded.shape[1]
    exponents = coded[RT * tile : RT * tile + RT].astype(jnp.float32)
    scale = jnp.repeat(jnp.exp2(exponents - BITS), tile, axis=0)
    return coded[: RT * tile].astype(jnp.float32) * scale


def across(block, axis, mask):
    route = [(i, i ^ mask) for i in range(lax.axis_size(axis))]
    return lax.ppermute(block, axis, route)


def travel(block, source):
    rows, cols = lax.axis_size("row"), lax.axis_size("col")
    route = []
    for r in range(rows):
        for c in range(cols):
            row, z, y = source(r, c >> 1, c & 1)
            route.append((row * cols + 2 * z + y, r * cols + c))
    return lax.ppermute(block, ("row", "col"), route)


def other_half(given, t):
    def source(r, z, y):
        apart = r ^ t ^ z
        swap = apart % 2 if apart > 1 else 0
        return r ^ t ^ swap, z ^ swap, y ^ 1

    return travel(given, source)


def gather(block, beside, ahead):
    distance = lax.axis_size("col") // 4
    steps = [distance >> n for n in range(distance.bit_length())]
    later, ahead = lax.optimization_barrier((block, ahead))
    came = [across(later if d == 1 else block, "col", 2 * d) for d in steps]
    came[:-1], beside = lax.optimization_barrier((came[:-1], beside))
    blocks = {0: block, **dict(zip(steps, came))}
    for d in steps:
        for s in sorted(blocks):
            if s ^ d not in blocks and s & (d - 1) == 0:
                blocks[s ^ d] = across(blocks[s], "col", 2 * d)
    return blocks, beside, ahead


def shards(left_tiles, left_index, right_tiles, right_index):
    y = lax.axis_index("col") & 1
    left = left_tiles[0, 0]
    right = right_tiles[0, 0]
    tile = left.shape[-1]

    codes = find_matches(left_index, right_index)
    given = lax.dynamic_index_in_dim(right, 1 - y, 0, keepdims=False)
    own = lax.dynamic_index_in_dim(right, y, 0, keepdims=False)
    lefts, codes, (own, given) = gather(left, codes, (own, given))
    rights = []
    for t in range(0, lax.axis_size("row"), 2):
        pair = [across(own, "row", t) if t else own, other_half(given, t)]
        if not t:
            pair[0], lefts[1] = lax.optimization_barrier((pair[0], lefts[1]))
        rights += pair + [across(half, "row", 1) for half in pair]

    plain = jax.ShapeDtypeStruct((RT * tile, tile), jnp.float32)
    coded = jax.ShapeDtypeStruct((RT * tile + PAD, tile), jnp.int16)
    early = {s: lefts[s] for s in counting(1, len(lefts))}
    late = {s: lefts[s] for s in lefts if s not in early}
    to_other, to_far = products(codes, early, rights, (1, 2), write_coded, coded, EARLY)
    coming = across(to_other, "col", 1)
    from_far = across(to_far, "col", 3)
    (mine,) = products(codes, early, rights, (0,), write_sum, plain, 10**8)
    (mine,) = products(codes, late, rights, (0,), write_sum, plain, LATE, mine)
    mine, coming, from_far = lax.optimization_barrier((mine, coming, from_far))
    return (mine + decoded(coming) + decoded(from_far)).astype(jnp.bfloat16)


def solution(mesh):
    return jax.shard_map(
        shards,
        mesh=mesh,
        in_specs=(
            P("row", "col", None, None, None),
            P(),
            P("row", "col", None, None, None, None),
            P(),
        ),
        out_specs=P("row", "col"),
        check_vma=False,
    )
```

```python
import jax
import jax.numpy as jnp
from jax import lax
from jax.experimental import pallas as pl
from jax.experimental.pallas import tpu as pltpu
from jax.sharding import PartitionSpec as P

KT = 8
RT = 2
SIDES = 3
EARLY = 10**8
LATE = 10**11
BITS = 15
LEAST = 100
PAD = 16
SMEM = pl.BlockSpec(memory_space=pltpu.SMEM)
VMEM = pl.BlockSpec(memory_space=pltpu.VMEM)


def position():
    col = lax.axis_index("col")
    return lax.axis_index("row"), col >> 1, col & 1


def counting(side, places):
    early = [s for s in range(places) if s % 2 == 0 or s == 1]
    return [range(places), early, [s for s in early if s > 1]][side]


def code_at(s, side, places, slots):
    pairs = [(other, at) for at in range(SIDES) for other in counting(at, places)]
    return pairs.index((s, side)) * slots


def find_matches(left_index, right_index):
    slots = left_index.shape[-1]
    places, _, _, right_slots = right_index.shape
    left_index = left_index.transpose(2, 0, 1)
    right_index = right_index.transpose(0, 3, 2, 1)
    total = sum(len(counting(side, places)) for side in range(SIDES)) * slots

    def kernel(li_ref, ri_ref, codes_ref):
        row, z, y = position()
        for side in range(SIDES):
            column = 2 * (z ^ (side >> 1)) + (y ^ min(side, 1))
            for s in counting(side, places):
                zp = z ^ s
                base = code_at(s, side, places, slots)
                have = [ri_ref[zp, t, y, column] for t in range(right_slots)]

                @pl.loop(0, slots)
                def _(slot):
                    at = li_ref[slot, row, 2 * zp + y]
                    k = lax.rem(at, KT)
                    first = 1 + lax.div(at, KT) * right_slots
                    code = jnp.int32(0)
                    for t in range(right_slots):
                        code = jnp.where(have[t] == k, first + t, code)
                    codes_ref[base + slot] = jnp.where(at < RT * KT, code, 0)

    return pl.pallas_call(
        kernel,
        out_shape=jax.ShapeDtypeStruct((total,), jnp.int32),
        in_specs=[SMEM] * 2,
        out_specs=SMEM,
    )(left_index, right_index)


def add_block(codes_ref, base, left_ref, right_at, right_slots, total_ref):
    slots, tile, _ = left_ref.shape

    @pl.loop(0, slots)
    def _(slot):
        code = codes_ref[base + slot]

        @pl.when(code > 0)
        def _():
            i = lax.div(code - 1, right_slots)
            rows = pl.ds(pl.multiple_of(i * tile, tile), tile)
            total_ref[rows, :] += jnp.dot(
                left_ref[slot],
                right_at(lax.rem(code - 1, right_slots)),
                preferred_element_type=jnp.float32,
            )


def products(codes, lefts, rights, sides, finish, out_shape, flops, start=None):
    distances = sorted(lefts)
    count = len(lefts)
    places = len(rights) // 2
    right_slots, tile, _ = rights[0].shape
    slots = lefts[distances[0]].shape[0]
    starts = [] if start is None else [start]

    def kernel(codes_ref, *refs):
        left_refs = dict(zip(distances, refs))
        right_refs = refs[count : count + 2 * places]
        start_refs = refs[count + 2 * places :][: len(starts)]
        outs = refs[count + 2 * places + len(starts) : -2]
        total_ref, held = refs[-2:]
        row, z, _ = position()
        for at in sorted({min(side, 1) for side in sides}):
            for t in range(places):
                held[t, at] = right_refs[2 * t + at][...]
        for side, out_ref in zip(sides, outs):
            total_ref[...] = start_refs[0][...] if starts else jnp.zeros_like(total_ref)
            for s in counting(side, places):
                if s in left_refs:
                    t = row ^ z ^ s ^ (side >> 1)
                    add_block(
                        codes_ref, code_at(s, side, places, slots), left_refs[s],
                        lambda found, t=t: held[t, min(side, 1), found], right_slots, total_ref,
                    )
            finish(total_ref, out_ref)

    return pl.pallas_call(
        kernel,
        out_shape=[out_shape] * len(sides),
        in_specs=[SMEM] + [VMEM] * (count + 2 * places + len(starts)),
        out_specs=[VMEM] * len(sides),
        scratch_shapes=[
            pltpu.VMEM((RT * tile, tile), jnp.float32),
            pltpu.VMEM((places, 2, right_slots, tile, tile), jnp.bfloat16),
        ],
        compiler_params=pltpu.CompilerParams(vmem_limit_bytes=32 * 1024 * 1024),
        cost_estimate=pl.CostEstimate(
            flops=flops,
            bytes_accessed=2 * count * slots * tile**2,
            transcendentals=0,
        ),
    )(codes, *[lefts[s] for s in distances], *rights, *starts)


def write_sum(sum_ref, out_ref):
    out_ref[...] = sum_ref[...]


def write_coded(sum_ref, out_ref):
    tile = sum_ref.shape[1]
    exponents = jnp.zeros((PAD, tile), jnp.float32)
    for i in range(RT):
        values = sum_ref[i * tile : (i + 1) * tile, :]
        largest = jnp.max(jnp.abs(values), axis=0, keepdims=True)
        exponent = jnp.clip(jnp.floor(jnp.log2(largest)) + 1.0, -LEAST, LEAST)
        coded = jnp.round(values * jnp.exp2(BITS - exponent))
        coded = jnp.clip(coded, -(2.0**BITS) + 1.0, 2.0**BITS - 1.0)
        out_ref[i * tile : (i + 1) * tile, :] = coded.astype(jnp.int32).astype(jnp.int16)
        at = lax.broadcasted_iota(jnp.int32, (PAD, tile), 0)
        exponents = jnp.where(at == i, exponent, exponents)
    out_ref[RT * tile :, :] = exponents.astype(jnp.int32).astype(jnp.int16)


def decoded(coded):
    tile = coded.shape[1]
    exponents = coded[RT * tile : RT * tile + RT].astype(jnp.float32)
    scale = jnp.repeat(jnp.exp2(exponents - BITS), tile, axis=0)
    return coded[: RT * tile].astype(jnp.float32) * scale


def across(block, axis, mask):
    route = [(i, i ^ mask) for i in range(lax.axis_size(axis))]
    return lax.ppermute(block, axis, route)


def travel(block, source):
    rows, cols = lax.axis_size("row"), lax.axis_size("col")
    route = []
    for r in range(rows):
        for c in range(cols):
            row, z, y = source(r, c >> 1, c & 1)
            route.append((row * cols + 2 * z + y, r * cols + c))
    return lax.ppermute(block, ("row", "col"), route)


def other_half(given, t):
    def source(r, z, y):
        apart = r ^ t ^ z
        swap = apart % 2 if apart > 1 else 0
        return r ^ t ^ swap, z ^ swap, y ^ 1

    return travel(given, source)


def gather(block, beside, ahead):
    distance = lax.axis_size("col") // 4
    steps = [distance >> n for n in range(distance.bit_length())]
    later, ahead = lax.optimization_barrier((block, ahead))
    came = [across(later if d == 1 else block, "col", 2 * d) for d in steps]
    came[:-1], beside = lax.optimization_barrier((came[:-1], beside))
    blocks = {0: block, **dict(zip(steps, came))}
    for d in steps:
        for s in sorted(blocks):
            if s ^ d not in blocks and s & (d - 1) == 0:
                blocks[s ^ d] = across(blocks[s], "col", 2 * d)
    return blocks, beside, ahead


def shards(left_tiles, left_index, right_tiles, right_index):
    y = lax.axis_index("col") & 1
    left = left_tiles[0, 0]
    right = right_tiles[0, 0]
    tile = left.shape[-1]

    codes = find_matches(left_index, right_index)
    given = lax.dynamic_index_in_dim(right, 1 - y, 0, keepdims=False)
    own = lax.dynamic_index_in_dim(right, y, 0, keepdims=False)
    pairs = []
    for t in range(0, lax.axis_size("row"), 2):
        pairs.append([across(own, "row", t) if t else own, other_half(given, t)])
    lefts, codes, pairs[-1][0] = gather(left, codes, pairs[-1][0])
    rights = []
    for pair in pairs:
        rights += pair + [across(half, "row", 1) for half in pair]

    plain = jax.ShapeDtypeStruct((RT * tile, tile), jnp.float32)
    coded = jax.ShapeDtypeStruct((RT * tile + PAD, tile), jnp.int16)
    early = {s: lefts[s] for s in counting(1, len(lefts))}
    late = {s: lefts[s] for s in lefts if s not in early}
    to_other, to_far = products(codes, early, rights, (1, 2), write_coded, coded, EARLY)
    coming = across(to_other, "col", 1)
    from_far = across(to_far, "col", 3)
    (mine,) = products(codes, early, rights, (0,), write_sum, plain, 10**8)
    (mine,) = products(codes, late, rights, (0,), write_sum, plain, LATE, mine)
    mine, coming, from_far = lax.optimization_barrier((mine, coming, from_far))
    return (mine + decoded(coming) + decoded(from_far)).astype(jnp.bfloat16)


def solution(mesh):
    return jax.shard_map(
        shards,
        mesh=mesh,
        in_specs=(
            P("row", "col", None, None, None),
            P(),
            P("row", "col", None, None, None, None),
            P(),
        ),
        out_specs=P("row", "col"),
        check_vma=False,
    )
```

```python
import jax
import jax.numpy as jnp
from jax import lax
from jax.experimental import pallas as pl
from jax.experimental.pallas import tpu as pltpu
from jax.sharding import PartitionSpec as P

KT = 8
RT = 2
SIDES = 3
EARLY = 10**8
LATE = 10**11
BITS = 15
LEAST = 100
PAD = 16
SMEM = pl.BlockSpec(memory_space=pltpu.SMEM)
VMEM = pl.BlockSpec(memory_space=pltpu.VMEM)


def position():
    col = lax.axis_index("col")
    return lax.axis_index("row"), col >> 1, col & 1


def counting(side, places):
    return range(0, places, 2 if side else 1)


def code_at(s, side, places, slots):
    pairs = [(other, at) for at in range(SIDES) for other in counting(at, places)]
    return pairs.index((s, side)) * slots


def find_matches(left_index, right_index):
    slots = left_index.shape[-1]
    places, _, _, right_slots = right_index.shape
    left_index = left_index.transpose(2, 0, 1)
    right_index = right_index.transpose(0, 3, 2, 1)
    total = sum(len(counting(side, places)) for side in range(SIDES)) * slots

    def kernel(li_ref, ri_ref, codes_ref):
        row, z, y = position()
        for side in range(SIDES):
            column = 2 * (z ^ (side >> 1)) + (y ^ min(side, 1))
            for s in counting(side, places):
                zp = z ^ s
                base = code_at(s, side, places, slots)
                have = [ri_ref[zp, t, y, column] for t in range(right_slots)]

                @pl.loop(0, slots)
                def _(slot):
                    at = li_ref[slot, row, 2 * zp + y]
                    k = lax.rem(at, KT)
                    first = 1 + lax.div(at, KT) * right_slots
                    code = jnp.int32(0)
                    for t in range(right_slots):
                        code = jnp.where(have[t] == k, first + t, code)
                    codes_ref[base + slot] = jnp.where(at < RT * KT, code, 0)

    return pl.pallas_call(
        kernel,
        out_shape=jax.ShapeDtypeStruct((total,), jnp.int32),
        in_specs=[SMEM] * 2,
        out_specs=SMEM,
    )(left_index, right_index)


def add_block(codes_ref, base, left_ref, right_at, right_slots, total_ref):
    slots, tile, _ = left_ref.shape

    @pl.loop(0, slots)
    def _(slot):
        code = codes_ref[base + slot]

        @pl.when(code > 0)
        def _():
            i = lax.div(code - 1, right_slots)
            rows = pl.ds(pl.multiple_of(i * tile, tile), tile)
            total_ref[rows, :] += jnp.dot(
                left_ref[slot],
                right_at(lax.rem(code - 1, right_slots)),
                preferred_element_type=jnp.float32,
            )


def products(codes, lefts, rights, sides, finish, out_shape, flops, start=None):
    distances = sorted(lefts)
    count = len(lefts)
    places = len(rights) // 2
    right_slots, tile, _ = rights[0].shape
    slots = lefts[distances[0]].shape[0]
    starts = [] if start is None else [start]

    def kernel(codes_ref, *refs):
        left_refs = dict(zip(distances, refs))
        right_refs = refs[count : count + 2 * places]
        start_refs = refs[count + 2 * places :][: len(starts)]
        outs = refs[count + 2 * places + len(starts) : -2]
        total_ref, held = refs[-2:]
        row, z, _ = position()
        for at in sorted({min(side, 1) for side in sides}):
            for t in range(places):
                held[t, at] = right_refs[2 * t + at][...]
        for side, out_ref in zip(sides, outs):
            total_ref[...] = start_refs[0][...] if starts else jnp.zeros_like(total_ref)
            for s in counting(side, places):
                if s in left_refs:
                    t = row ^ z ^ s ^ (side >> 1)
                    add_block(
                        codes_ref, code_at(s, side, places, slots), left_refs[s],
                        lambda found, t=t: held[t, min(side, 1), found], right_slots, total_ref,
                    )
            finish(total_ref, out_ref)

    return pl.pallas_call(
        kernel,
        out_shape=[out_shape] * len(sides),
        in_specs=[SMEM] + [VMEM] * (count + 2 * places + len(starts)),
        out_specs=[VMEM] * len(sides),
        scratch_shapes=[
            pltpu.VMEM((RT * tile, tile), jnp.float32),
            pltpu.VMEM((places, 2, right_slots, tile, tile), jnp.bfloat16),
        ],
        compiler_params=pltpu.CompilerParams(vmem_limit_bytes=32 * 1024 * 1024),
        cost_estimate=pl.CostEstimate(
            flops=flops,
            bytes_accessed=2 * count * slots * tile**2,
            transcendentals=0,
        ),
    )(codes, *[lefts[s] for s in distances], *rights, *starts)


def write_sum(sum_ref, out_ref):
    out_ref[...] = sum_ref[...]


def write_coded(sum_ref, out_ref):
    tile = sum_ref.shape[1]
    exponents = jnp.zeros((PAD, tile), jnp.float32)
    for i in range(RT):
        values = sum_ref[i * tile : (i + 1) * tile, :]
        largest = jnp.max(jnp.abs(values), axis=0, keepdims=True)
        exponent = jnp.clip(jnp.floor(jnp.log2(largest)) + 1.0, -LEAST, LEAST)
        coded = jnp.round(values * jnp.exp2(BITS - exponent))
        coded = jnp.clip(coded, -(2.0**BITS) + 1.0, 2.0**BITS - 1.0)
        out_ref[i * tile : (i + 1) * tile, :] = coded.astype(jnp.int32).astype(jnp.int16)
        at = lax.broadcasted_iota(jnp.int32, (PAD, tile), 0)
        exponents = jnp.where(at == i, exponent, exponents)
    out_ref[RT * tile :, :] = exponents.astype(jnp.int32).astype(jnp.int16)


def decoded(coded):
    tile = coded.shape[1]
    exponents = coded[RT * tile : RT * tile + RT].astype(jnp.float32)
    scale = jnp.repeat(jnp.exp2(exponents - BITS), tile, axis=0)
    return coded[: RT * tile].astype(jnp.float32) * scale


def across(block, axis, mask):
    route = [(i, i ^ mask) for i in range(lax.axis_size(axis))]
    return lax.ppermute(block, axis, route)


def travel(block, source):
    rows, cols = lax.axis_size("row"), lax.axis_size("col")
    route = []
    for r in range(rows):
        for c in range(cols):
            row, z, y = source(r, c >> 1, c & 1)
            route.append((row * cols + 2 * z + y, r * cols + c))
    return lax.ppermute(block, ("row", "col"), route)


def other_half(given, t):
    def source(r, z, y):
        odd = (r ^ t ^ z) & 1
        return r ^ t ^ odd, z ^ odd, y ^ 1

    return travel(given, source)


def gather(block, beside, ahead):
    distance = lax.axis_size("col") // 4
    steps = [distance >> n for n in range(distance.bit_length())]
    later, ahead = lax.optimization_barrier((block, ahead))
    came = [across(later if d == 1 else block, "col", 2 * d) for d in steps]
    came[:-1], beside = lax.optimization_barrier((came[:-1], beside))
    blocks = {0: block, **dict(zip(steps, came))}
    for d in steps:
        for s in sorted(blocks):
            if s ^ d not in blocks and s & (d - 1) == 0:
                blocks[s ^ d] = across(blocks[s], "col", 2 * d)
    return blocks, beside, ahead


def shards(left_tiles, left_index, right_tiles, right_index):
    y = lax.axis_index("col") & 1
    left = left_tiles[0, 0]
    right = right_tiles[0, 0]
    tile = left.shape[-1]

    codes = find_matches(left_index, right_index)
    given = lax.dynamic_index_in_dim(right, 1 - y, 0, keepdims=False)
    own = lax.dynamic_index_in_dim(right, y, 0, keepdims=False)
    pairs = []
    for t in range(0, lax.axis_size("row"), 2):
        pairs.append([across(own, "row", t) if t else own, other_half(given, t)])
    lefts, codes, pairs[-1][0] = gather(left, codes, pairs[-1][0])
    rights = []
    for pair in pairs:
        rights += pair + [across(half, "row", 1) for half in pair]

    plain = jax.ShapeDtypeStruct((RT * tile, tile), jnp.float32)
    coded = jax.ShapeDtypeStruct((RT * tile + PAD, tile), jnp.int16)
    early = {s: lefts[s] for s in counting(1, len(lefts))}
    late = {s: lefts[s] for s in lefts if s not in early}
    to_other, to_far = products(codes, early, rights, (1, 2), write_coded, coded, EARLY)
    coming = across(to_other, "col", 1)
    from_far = across(to_far, "col", 3)
    (mine,) = products(codes, early, rights, (0,), write_sum, plain, 10**8)
    (mine,) = products(codes, late, rights, (0,), write_sum, plain, LATE, mine)
    mine, coming, from_far = lax.optimization_barrier((mine, coming, from_far))
    return (mine + decoded(coming) + decoded(from_far)).astype(jnp.bfloat16)


def solution(mesh):
    return jax.shard_map(
        shards,
        mesh=mesh,
        in_specs=(
            P("row", "col", None, None, None),
            P(),
            P("row", "col", None, None, None, None),
            P(),
        ),
        out_specs=P("row", "col"),
        check_vma=False,
    )
```

```python
import jax
import jax.numpy as jnp
from jax import lax
from jax.experimental import pallas as pl
from jax.experimental.pallas import tpu as pltpu
from jax.sharding import PartitionSpec as P

KT = 8
RT = 2
SIDES = 3
EARLY = 10**8
LATE = 10**11
BITS = 15
LEAST = 100
PAD = 16
SMEM = pl.BlockSpec(memory_space=pltpu.SMEM)
VMEM = pl.BlockSpec(memory_space=pltpu.VMEM)


def position():
    col = lax.axis_index("col")
    return lax.axis_index("row"), col >> 1, col & 1


def counting(side, places):
    return range(0, places, 2 if side else 1)


def code_at(s, side, places, slots):
    pairs = [(other, at) for at in range(SIDES) for other in counting(at, places)]
    return pairs.index((s, side)) * slots


def find_matches(left_index, right_index):
    slots = left_index.shape[-1]
    places, _, _, right_slots = right_index.shape
    left_index = left_index.transpose(2, 0, 1)
    right_index = right_index.transpose(0, 3, 2, 1)
    total = sum(len(counting(side, places)) for side in range(SIDES)) * slots

    def kernel(li_ref, ri_ref, codes_ref):
        row, z, y = position()
        for side in range(SIDES):
            column = 2 * (z ^ (side >> 1)) + (y ^ min(side, 1))
            for s in counting(side, places):
                zp = z ^ s
                base = code_at(s, side, places, slots)
                have = [ri_ref[zp, t, y, column] for t in range(right_slots)]

                @pl.loop(0, slots)
                def _(slot):
                    at = li_ref[slot, row, 2 * zp + y]
                    k = lax.rem(at, KT)
                    first = 1 + lax.div(at, KT) * right_slots
                    code = jnp.int32(0)
                    for t in range(right_slots):
                        code = jnp.where(have[t] == k, first + t, code)
                    codes_ref[base + slot] = jnp.where(at < RT * KT, code, 0)

    return pl.pallas_call(
        kernel,
        out_shape=jax.ShapeDtypeStruct((total,), jnp.int32),
        in_specs=[SMEM] * 2,
        out_specs=SMEM,
    )(left_index, right_index)


def add_block(codes_ref, base, left_ref, right_at, right_slots, total_ref):
    slots, tile, _ = left_ref.shape

    @pl.loop(0, slots)
    def _(slot):
        code = codes_ref[base + slot]

        @pl.when(code > 0)
        def _():
            i = lax.div(code - 1, right_slots)
            rows = pl.ds(pl.multiple_of(i * tile, tile), tile)
            total_ref[rows, :] += jnp.dot(
                left_ref[slot],
                right_at(lax.rem(code - 1, right_slots)),
                preferred_element_type=jnp.float32,
            )


def products(codes, lefts, rights, sides, finish, out_shape, flops, start=None):
    distances = sorted(lefts)
    count = len(lefts)
    places = len(rights) // 2
    right_slots, tile, _ = rights[0].shape
    slots = lefts[distances[0]].shape[0]
    starts = [] if start is None else [start]

    def kernel(codes_ref, *refs):
        left_refs = dict(zip(distances, refs))
        right_refs = refs[count : count + 2 * places]
        start_refs = refs[count + 2 * places :][: len(starts)]
        outs = refs[count + 2 * places + len(starts) : -2]
        total_ref, held = refs[-2:]
        row, z, _ = position()
        for at in sorted({min(side, 1) for side in sides}):
            for t in range(places):
                held[t, at] = right_refs[2 * t + at][...]
        for side, out_ref in zip(sides, outs):
            total_ref[...] = start_refs[0][...] if starts else jnp.zeros_like(total_ref)
            for s in counting(side, places):
                if s in left_refs:
                    t = row ^ z ^ s ^ (side >> 1)
                    add_block(
                        codes_ref, code_at(s, side, places, slots), left_refs[s],
                        lambda found, t=t: held[t, min(side, 1), found], right_slots, total_ref,
                    )
            finish(total_ref, out_ref)

    return pl.pallas_call(
        kernel,
        out_shape=[out_shape] * len(sides),
        in_specs=[SMEM] + [VMEM] * (count + 2 * places + len(starts)),
        out_specs=[VMEM] * len(sides),
        scratch_shapes=[
            pltpu.VMEM((RT * tile, tile), jnp.float32),
            pltpu.VMEM((places, 2, right_slots, tile, tile), jnp.bfloat16),
        ],
        compiler_params=pltpu.CompilerParams(vmem_limit_bytes=32 * 1024 * 1024),
        cost_estimate=pl.CostEstimate(
            flops=flops,
            bytes_accessed=2 * count * slots * tile**2,
            transcendentals=0,
        ),
    )(codes, *[lefts[s] for s in distances], *rights, *starts)


def write_sum(sum_ref, out_ref):
    out_ref[...] = sum_ref[...]


def write_coded(sum_ref, out_ref):
    tile = sum_ref.shape[1]
    exponents = jnp.zeros((PAD, tile), jnp.float32)
    for i in range(RT):
        values = sum_ref[i * tile : (i + 1) * tile, :]
        largest = jnp.max(jnp.abs(values), axis=0, keepdims=True)
        exponent = jnp.clip(jnp.floor(jnp.log2(largest)) + 1.0, -LEAST, LEAST)
        coded = jnp.round(values * jnp.exp2(BITS - exponent))
        coded = jnp.clip(coded, -(2.0**BITS) + 1.0, 2.0**BITS - 1.0)
        out_ref[i * tile : (i + 1) * tile, :] = coded.astype(jnp.int32).astype(jnp.int16)
        at = lax.broadcasted_iota(jnp.int32, (PAD, tile), 0)
        exponents = jnp.where(at == i, exponent, exponents)
    out_ref[RT * tile :, :] = exponents.astype(jnp.int32).astype(jnp.int16)


def decoded(coded):
    tile = coded.shape[1]
    exponents = coded[RT * tile : RT * tile + RT].astype(jnp.float32)
    scale = jnp.repeat(jnp.exp2(exponents - BITS), tile, axis=0)
    return coded[: RT * tile].astype(jnp.float32) * scale


def across(block, axis, mask):
    route = [(i, i ^ mask) for i in range(lax.axis_size(axis))]
    return lax.ppermute(block, axis, route)


def travel(block, source):
    rows, cols = lax.axis_size("row"), lax.axis_size("col")
    route = []
    for r in range(rows):
        for c in range(cols):
            row, z, y = source(r, c >> 1, c & 1)
            route.append((row * cols + 2 * z + y, r * cols + c))
    return lax.ppermute(block, ("row", "col"), route)


def other_half(given, t):
    def source(r, z, y):
        odd = (r ^ t ^ z) & 1
        return r ^ t ^ odd, z ^ odd, y ^ 1

    return travel(given, source)


def gather(block, beside, ahead):
    distance = lax.axis_size("col") // 4
    steps = [distance >> n for n in range(distance.bit_length())]
    later, ahead = lax.optimization_barrier((block, ahead))
    came = [across(later if d == 1 else block, "col", 2 * d) for d in steps]
    came[:-1], beside = lax.optimization_barrier((came[:-1], beside))
    blocks = {0: block, **dict(zip(steps, came))}
    for d in steps:
        for s in sorted(blocks):
            if s ^ d not in blocks and s & (d - 1) == 0:
                blocks[s ^ d] = across(blocks[s], "col", 2 * d)
    return blocks, beside, ahead


def shards(left_tiles, left_index, right_tiles, right_index):
    y = lax.axis_index("col") & 1
    left = left_tiles[0, 0]
    right = right_tiles[0, 0]
    tile = left.shape[-1]

    given = lax.dynamic_index_in_dim(right, 1 - y, 0, keepdims=False)
    own = lax.dynamic_index_in_dim(right, y, 0, keepdims=False)
    pairs = []
    for t in range(0, lax.axis_size("row"), 2):
        pairs.append([across(own, "row", t) if t else own, other_half(given, t)])
    left_index, pairs[-1][0] = lax.optimization_barrier((left_index, pairs[-1][0]))
    codes = find_matches(left_index, right_index)
    lefts, codes, pairs[-1][0] = gather(left, codes, pairs[-1][0])
    rights = []
    for pair in pairs:
        rights += pair + [across(half, "row", 1) for half in pair]

    plain = jax.ShapeDtypeStruct((RT * tile, tile), jnp.float32)
    coded = jax.ShapeDtypeStruct((RT * tile + PAD, tile), jnp.int16)
    early = {s: lefts[s] for s in counting(1, len(lefts))}
    late = {s: lefts[s] for s in lefts if s not in early}
    to_other, to_far = products(codes, early, rights, (1, 2), write_coded, coded, EARLY)
    coming = across(to_other, "col", 1)
    from_far = across(to_far, "col", 3)
    (mine,) = products(codes, early, rights, (0,), write_sum, plain, 10**8)
    (mine,) = products(codes, late, rights, (0,), write_sum, plain, LATE, mine)
    mine, coming, from_far = lax.optimization_barrier((mine, coming, from_far))
    return (mine + decoded(coming) + decoded(from_far)).astype(jnp.bfloat16)


def solution(mesh):
    return jax.shard_map(
        shards,
        mesh=mesh,
        in_specs=(
            P("row", "col", None, None, None),
            P(),
            P("row", "col", None, None, None, None),
            P(),
        ),
        out_specs=P("row", "col"),
        check_vma=False,
    )
```

```python
import jax
import jax.numpy as jnp
from jax import lax
from jax.experimental import pallas as pl
from jax.experimental.pallas import tpu as pltpu
from jax.sharding import PartitionSpec as P

KT = 8
RT = 2
BITS = 15
LEAST = 100
PAD = 16
SMEM = pl.BlockSpec(memory_space=pltpu.SMEM)
VMEM = pl.BlockSpec(memory_space=pltpu.VMEM)


def position():
    col = lax.axis_index("col")
    return lax.axis_index("row"), col >> 1, col & 1


def find_matches(left_index, right_index):
    slots = left_index.shape[-1]
    inner, _, _, right_slots = right_index.shape
    left_index = left_index.transpose(2, 0, 1)
    right_index = right_index.transpose(0, 3, 2, 1)

    def kernel(li_ref, ri_ref, codes_ref):
        row, z, y = position()

        @pl.loop(0, inner)
        def _(s):
            zp = z ^ s
            for side in range(2):
                column = 2 * z + (y if side == 0 else 1 - y)
                have = [ri_ref[zp, t, y, column] for t in range(right_slots)]
                for slot in range(slots):
                    at = li_ref[slot, row, 2 * zp + y]
                    k = lax.rem(at, KT)
                    first = 1 + lax.div(at, KT) * right_slots
                    code = jnp.int32(0)
                    for t in range(right_slots):
                        code = jnp.where(have[t] == k, first + t, code)
                    codes_ref[(s * 2 + side) * slots + slot] = jnp.where(at < RT * KT, code, 0)

    return pl.pallas_call(
        kernel,
        out_shape=jax.ShapeDtypeStruct((inner * 2 * slots,), jnp.int32),
        in_specs=[SMEM] * 2,
        out_specs=SMEM,
    )(left_index, right_index)


def add_part(codes_ref, s, side, start, slots, left_ref, right_at, right_slots, total_ref):
    tile = total_ref.shape[1]

    @pl.loop(0, left_ref.shape[0])
    def _(slot):
        code = codes_ref[(s * 2 + side) * slots + start + slot]

        @pl.when(code > 0)
        def _():
            i = lax.div(code - 1, right_slots)
            rows = pl.ds(pl.multiple_of(i * tile, tile), tile)
            total_ref[rows, :] += jnp.dot(
                left_ref[slot],
                right_at(lax.rem(code - 1, right_slots)),
                preferred_element_type=jnp.float32,
            )


def first_products(codes, lefts, rights, slots):
    parts = [(s, part) for s, block in lefts for part in block]
    count = len(parts)
    inner = len(rights) // 2
    right_slots, tile, _ = rights[0].shape

    def kernel(codes_ref, *refs):
        right_refs = refs[count : count + 2 * inner]
        totals = refs[count + 2 * inner : count + 2 * inner + 2]
        last_ref, held = refs[count + 2 * inner + 2 :]
        row, z, _ = position()
        for t in range(inner):
            for side in range(2):
                held[row ^ t, side] = right_refs[2 * t + side][...]
        last_ref[...] = held[z ^ (inner - 1)]
        for side in range(2):
            totals[side][...] = jnp.zeros_like(totals[side])
            start, before = 0, None
            for (s, _), left_ref in zip(parts, refs):
                start = start if s == before else 0
                add_part(
                    codes_ref, s, side, start, slots, left_ref,
                    lambda found, s=s: held[z ^ s, side, found], right_slots, totals[side],
                )
                start, before = start + left_ref.shape[0], s

    return pl.pallas_call(
        kernel,
        out_shape=[jax.ShapeDtypeStruct((RT * tile, tile), jnp.float32)] * 2
        + [jax.ShapeDtypeStruct((2, right_slots, tile, tile), jnp.bfloat16)],
        in_specs=[SMEM] + [VMEM] * (count + 2 * inner),
        out_specs=[VMEM] * 3,
        scratch_shapes=[pltpu.VMEM((inner, 2, right_slots, tile, tile), jnp.bfloat16)],
        compiler_params=pltpu.CompilerParams(vmem_limit_bytes=32 * 1024 * 1024),
        cost_estimate=pl.CostEstimate(
            flops=4 * inner * slots * tile**3, bytes_accessed=2 * inner * slots * tile**2, transcendentals=0
        ),
    )(codes, *[part for _, part in parts], *rights)


def last_products(codes, s, parts, right, total, side, slots, finish, out_shape):
    count = len(parts)
    right_slots = right.shape[1]

    def kernel(codes_ref, *refs):
        right_ref, total_ref, out_ref, sum_ref = refs[count:]
        sum_ref[...] = total_ref[...]
        start = 0
        for left_ref in refs[:count]:
            add_part(
                codes_ref, s, side, start, slots, left_ref,
                lambda found: right_ref[side, found], right_slots, sum_ref,
            )
            start += left_ref.shape[0]
        finish(sum_ref, out_ref)

    return pl.pallas_call(
        kernel,
        out_shape=out_shape,
        in_specs=[SMEM] + [VMEM] * (count + 2),
        out_specs=VMEM,
        scratch_shapes=[pltpu.VMEM(total.shape, total.dtype)],
        compiler_params=pltpu.CompilerParams(vmem_limit_bytes=16 * 1024 * 1024),
        cost_estimate=pl.CostEstimate(
            flops=2 * slots * 128**3, bytes_accessed=2 * slots * 128**2, transcendentals=0
        ),
    )(codes, *parts, right, total)


def write_sum(sum_ref, out_ref):
    out_ref[...] = sum_ref[...]


def write_coded(sum_ref, out_ref):
    tile = sum_ref.shape[1]
    exponents = jnp.zeros((PAD, tile), jnp.float32)
    for i in range(RT):
        values = sum_ref[i * tile : (i + 1) * tile, :]
        largest = jnp.max(jnp.abs(values), axis=0, keepdims=True)
        exponent = jnp.clip(jnp.floor(jnp.log2(largest)) + 1.0, -LEAST, LEAST)
        coded = jnp.round(values * jnp.exp2(BITS - exponent))
        coded = jnp.clip(coded, -(2.0**BITS) + 1.0, 2.0**BITS - 1.0)
        out_ref[i * tile : (i + 1) * tile, :] = coded.astype(jnp.int32).astype(jnp.int16)
        at = lax.broadcasted_iota(jnp.int32, (PAD, tile), 0)
        exponents = jnp.where(at == i, exponent, exponents)
    out_ref[RT * tile :, :] = exponents.astype(jnp.int32).astype(jnp.int16)


def add_coded(total, coded):
    tile = total.shape[1]
    exponents = coded[RT * tile : RT * tile + RT].astype(jnp.float32)
    scale = jnp.repeat(jnp.exp2(exponents - BITS), tile, axis=0)
    return (total + coded[: RT * tile].astype(jnp.float32) * scale).astype(jnp.bfloat16)


def across(block, axis, mask):
    route = [(i, i ^ mask) for i in range(lax.axis_size(axis))]
    return lax.ppermute(block, axis, route)


def crossed(block, mask):
    rows, cols = lax.axis_size("row"), lax.axis_size("col")
    route = [(r * cols + c, (r ^ mask) * cols + (c ^ 1)) for r in range(rows) for c in range(cols)]
    return lax.ppermute(block, ("row", "col"), route)


def gather(block, beside, place):
    distance = lax.axis_size("col") // 4
    steps = [distance >> n for n in range(distance.bit_length())]
    later, _ = lax.optimization_barrier((block, place))
    came = [across(later if d == 1 else block, "col", 2 * d) for d in steps]
    came[:-1], beside = lax.optimization_barrier((came[:-1], beside))
    blocks = {0: block, **dict(zip(steps, came))}
    for d in steps:
        for s in sorted(blocks):
            if s ^ d not in blocks and s & (d - 1) == 0:
                blocks[s ^ d] = across(blocks[s], "col", 2 * d)
    return [(s, (blocks[s],)) for s in range(len(blocks))], beside


def shards(left_tiles, left_index, right_tiles, right_index):
    y = lax.axis_index("col") & 1
    left = left_tiles[0, 0]
    right = right_tiles[0, 0]
    slots = left.shape[0]

    codes = find_matches(left_index, right_index)
    given = lax.dynamic_index_in_dim(right, 1 - y, 0, keepdims=False)
    own = lax.dynamic_index_in_dim(right, y, 0, keepdims=False)
    lefts, codes = gather(left, codes, y)
    rights = []
    for t in range(0, lax.axis_size("row"), 2):
        pair = [across(own, "row", t) if t else own, crossed(given, t)]
        if not t:
            pair[0], near = lax.optimization_barrier((pair[0], lefts[1][1]))
            lefts[1] = (1, near)
        rights += pair + [across(half, "row", 1) for half in pair]

    mine, other, right_last = first_products(codes, lefts[:-1], rights, slots)
    far, final = lefts[-1]
    last = (codes, far, final, right_last)
    rows, tile = mine.shape
    coded = last_products(
        *last, other, 1, slots, write_coded, jax.ShapeDtypeStruct((rows + PAD, tile), jnp.int16)
    )
    coming = across(coded, "col", 1)
    mine = last_products(*last, mine, 0, slots, write_sum, jax.ShapeDtypeStruct((rows, tile), jnp.float32))
    return add_coded(mine, coming)


def solution(mesh):
    return jax.shard_map(
        shards,
        mesh=mesh,
        in_specs=(
            P("row", "col", None, None, None),
            P(),
            P("row", "col", None, None, None, None),
            P(),
        ),
        out_specs=P("row", "col"),
        check_vma=False,
    )
```

```python
import jax
import jax.numpy as jnp
from jax import lax
from jax.experimental import pallas as pl
from jax.experimental.pallas import tpu as pltpu
from jax.sharding import PartitionSpec as P

KT = 8
RT = 2
BITS = 15
LEAST = 100
PAD = 16
SMEM = pl.BlockSpec(memory_space=pltpu.SMEM)
VMEM = pl.BlockSpec(memory_space=pltpu.VMEM)


def position():
    col = lax.axis_index("col")
    return lax.axis_index("row"), col >> 1, col & 1


def find_matches(left_index, right_index):
    slots = left_index.shape[-1]
    inner, _, _, right_slots = right_index.shape
    left_index = left_index.transpose(2, 0, 1)
    right_index = right_index.transpose(0, 3, 2, 1)

    def kernel(li_ref, ri_ref, codes_ref):
        row, z, y = position()

        @pl.loop(0, inner)
        def _(s):
            zp = z ^ s
            for side in range(2):
                column = 2 * z + (y if side == 0 else 1 - y)
                have = [ri_ref[zp, t, y, column] for t in range(right_slots)]
                for slot in range(slots):
                    at = li_ref[slot, row, 2 * zp + y]
                    k = lax.rem(at, KT)
                    first = 1 + lax.div(at, KT) * right_slots
                    code = jnp.int32(0)
                    for t in range(right_slots):
                        code = jnp.where(have[t] == k, first + t, code)
                    codes_ref[(s * 2 + side) * slots + slot] = jnp.where(at < RT * KT, code, 0)

    return pl.pallas_call(
        kernel,
        out_shape=jax.ShapeDtypeStruct((inner * 2 * slots,), jnp.int32),
        in_specs=[SMEM] * 2,
        out_specs=SMEM,
    )(left_index, right_index)


def add_part(codes_ref, s, side, start, slots, left_ref, right_at, right_slots, total_ref):
    tile = total_ref.shape[1]

    @pl.loop(0, left_ref.shape[0])
    def _(slot):
        code = codes_ref[(s * 2 + side) * slots + start + slot]

        @pl.when(code > 0)
        def _():
            i = lax.div(code - 1, right_slots)
            rows = pl.ds(pl.multiple_of(i * tile, tile), tile)
            total_ref[rows, :] += jnp.dot(
                left_ref[slot],
                right_at(lax.rem(code - 1, right_slots)),
                preferred_element_type=jnp.float32,
            )


def first_products(codes, lefts, rights, slots):
    parts = [(s, part) for s, block in lefts for part in block]
    count = len(parts)
    inner = len(rights) // 2
    right_slots, tile, _ = rights[0].shape

    def kernel(codes_ref, *refs):
        right_refs = refs[count : count + 2 * inner]
        totals = refs[count + 2 * inner : count + 2 * inner + 2]
        last_ref, held = refs[count + 2 * inner + 2 :]
        row, z, _ = position()
        for t in range(inner):
            for side in range(2):
                held[row ^ t, side] = right_refs[2 * t + side][...]
        at = z ^ (inner - 1)
        last_ref[...] = jnp.zeros_like(last_ref)
        for side in range(2):

            @pl.loop(0, slots)
            def _(slot):
                code = codes_ref[((inner - 1) * 2 + side) * slots + slot]

                @pl.when(code > 0)
                def _():
                    rows = pl.ds(pl.multiple_of(slot * tile, tile), tile)
                    i = lax.div(code - 1, right_slots)
                    columns = pl.ds(pl.multiple_of(i * tile, tile), tile)
                    last_ref[side, rows, columns] = held[at, side, lax.rem(code - 1, right_slots)]

        for side in range(2):
            totals[side][...] = jnp.zeros_like(totals[side])
            start, before = 0, None
            for (s, _), left_ref in zip(parts, refs):
                start = start if s == before else 0
                add_part(
                    codes_ref, s, side, start, slots, left_ref,
                    lambda found, s=s: held[z ^ s, side, found], right_slots, totals[side],
                )
                start, before = start + left_ref.shape[0], s

    return pl.pallas_call(
        kernel,
        out_shape=[jax.ShapeDtypeStruct((RT * tile, tile), jnp.float32)] * 2
        + [jax.ShapeDtypeStruct((2, slots * tile, RT * tile), jnp.bfloat16)],
        in_specs=[SMEM] + [VMEM] * (count + 2 * inner),
        out_specs=[VMEM] * 3,
        scratch_shapes=[pltpu.VMEM((inner, 2, right_slots, tile, tile), jnp.bfloat16)],
        compiler_params=pltpu.CompilerParams(vmem_limit_bytes=32 * 1024 * 1024),
        cost_estimate=pl.CostEstimate(
            flops=4 * inner * slots * tile**3, bytes_accessed=2 * inner * slots * tile**2, transcendentals=0
        ),
    )(codes, *[part for _, part in parts], *rights)


def last_products(parts, right, total, side, finish, out_shape):
    (left,) = parts
    slots, tile, _ = left.shape

    def kernel(left_ref, right_ref, total_ref, out_ref):
        added = jnp.zeros((tile, RT * tile), jnp.float32)
        for slot in range(0, slots, 2):
            both = min(2, slots - slot)
            tiles = [left_ref[slot + n] for n in range(both)]
            added += jnp.dot(
                jnp.concatenate(tiles, axis=1),
                right_ref[side, slot * tile : (slot + both) * tile, :],
                preferred_element_type=jnp.float32,
            )
        sums = [
            total_ref[i * tile : (i + 1) * tile, :] + added[:, i * tile : (i + 1) * tile] for i in range(RT)
        ]
        finish(sums, out_ref)

    return pl.pallas_call(
        kernel,
        out_shape=out_shape,
        in_specs=[VMEM] * 3,
        out_specs=VMEM,
        compiler_params=pltpu.CompilerParams(vmem_limit_bytes=16 * 1024 * 1024),
        cost_estimate=pl.CostEstimate(
            flops=2 * slots * tile**3, bytes_accessed=2 * slots * tile**2, transcendentals=0
        ),
    )(left, right, total)


def write_sum(sums, out_ref):
    out_ref[...] = jnp.concatenate(sums)


def write_coded(sums, out_ref):
    tile = out_ref.shape[1]
    exponents = jnp.zeros((PAD, tile), jnp.float32)
    for i, values in enumerate(sums):
        largest = jnp.max(jnp.abs(values), axis=0, keepdims=True)
        exponent = jnp.clip(jnp.floor(jnp.log2(largest)) + 1.0, -LEAST, LEAST)
        coded = jnp.round(values * jnp.exp2(BITS - exponent))
        coded = jnp.clip(coded, -(2.0**BITS) + 1.0, 2.0**BITS - 1.0)
        out_ref[i * tile : (i + 1) * tile, :] = coded.astype(jnp.int32).astype(jnp.int16)
        at = lax.broadcasted_iota(jnp.int32, (PAD, tile), 0)
        exponents = jnp.where(at == i, exponent, exponents)
    out_ref[RT * tile :, :] = exponents.astype(jnp.int32).astype(jnp.int16)


def add_coded(total, coded):
    tile = total.shape[1]
    exponents = coded[RT * tile : RT * tile + RT].astype(jnp.float32)
    scale = jnp.repeat(jnp.exp2(exponents - BITS), tile, axis=0)
    return (total + coded[: RT * tile].astype(jnp.float32) * scale).astype(jnp.bfloat16)


def across(block, axis, mask):
    route = [(i, i ^ mask) for i in range(lax.axis_size(axis))]
    return lax.ppermute(block, axis, route)


def crossed(block, mask):
    rows, cols = lax.axis_size("row"), lax.axis_size("col")
    route = [(r * cols + c, (r ^ mask) * cols + (c ^ 1)) for r in range(rows) for c in range(cols)]
    return lax.ppermute(block, ("row", "col"), route)


def gather(block, beside, place):
    distance = lax.axis_size("col") // 4
    steps = [distance >> n for n in range(distance.bit_length())]
    later, _ = lax.optimization_barrier((block, place))
    came = [across(later if d == 1 else block, "col", 2 * d) for d in steps]
    came[:-1], beside = lax.optimization_barrier((came[:-1], beside))
    blocks = {0: block, **dict(zip(steps, came))}
    for d in steps:
        for s in sorted(blocks):
            if s ^ d not in blocks and s & (d - 1) == 0:
                blocks[s ^ d] = across(blocks[s], "col", 2 * d)
    return [(s, (blocks[s],)) for s in range(len(blocks))], beside


def shards(left_tiles, left_index, right_tiles, right_index):
    y = lax.axis_index("col") & 1
    left = left_tiles[0, 0]
    right = right_tiles[0, 0]
    slots = left.shape[0]

    codes = find_matches(left_index, right_index)
    given = lax.dynamic_index_in_dim(right, 1 - y, 0, keepdims=False)
    own = lax.dynamic_index_in_dim(right, y, 0, keepdims=False)
    lefts, codes = gather(left, codes, y)
    rights = []
    for t in range(0, lax.axis_size("row"), 2):
        pair = [across(own, "row", t) if t else own, crossed(given, t)]
        if not t:
            pair[0], near = lax.optimization_barrier((pair[0], lefts[1][1]))
            lefts[1] = (1, near)
        rights += pair + [across(half, "row", 1) for half in pair]

    mine, other, right_last = first_products(codes, lefts[:-1], rights, slots)
    last = (lefts[-1][1], right_last)
    rows, tile = mine.shape
    coded = last_products(
        *last, other, 1, write_coded, jax.ShapeDtypeStruct((rows + PAD, tile), jnp.int16)
    )
    coming = across(coded, "col", 1)
    mine = last_products(*last, mine, 0, write_sum, jax.ShapeDtypeStruct((rows, tile), jnp.float32))
    return add_coded(mine, coming)


def solution(mesh):
    return jax.shard_map(
        shards,
        mesh=mesh,
        in_specs=(
            P("row", "col", None, None, None),
            P(),
            P("row", "col", None, None, None, None),
            P(),
        ),
        out_specs=P("row", "col"),
        check_vma=False,
    )
```

```python
import jax
import jax.numpy as jnp
from jax import lax
from jax.experimental import pallas as pl
from jax.experimental.pallas import tpu as pltpu
from jax.sharding import PartitionSpec as P

KT = 8
RT = 2
BITS = 15
LEAST = 100
PAD = 16
SMEM = pl.BlockSpec(memory_space=pltpu.SMEM)
VMEM = pl.BlockSpec(memory_space=pltpu.VMEM)


def position():
    col = lax.axis_index("col")
    return lax.axis_index("row"), col >> 1, col & 1


def find_matches(left_index, right_index):
    slots = left_index.shape[-1]
    inner, _, _, right_slots = right_index.shape
    left_index = left_index.transpose(2, 0, 1)
    right_index = right_index.transpose(0, 3, 2, 1)

    def kernel(li_ref, ri_ref, codes_ref):
        row, z, y = position()

        @pl.loop(0, inner)
        def _(s):
            zp = z ^ s
            for side in range(2):
                column = 2 * z + (y if side == 0 else 1 - y)
                have = [ri_ref[zp, t, y, column] for t in range(right_slots)]
                for slot in range(slots):
                    at = li_ref[slot, row, 2 * zp + y]
                    k = lax.rem(at, KT)
                    first = 1 + lax.div(at, KT) * right_slots
                    code = jnp.int32(0)
                    for t in range(right_slots):
                        code = jnp.where(have[t] == k, first + t, code)
                    codes_ref[(s * 2 + side) * slots + slot] = jnp.where(at < RT * KT, code, 0)

    return pl.pallas_call(
        kernel,
        out_shape=jax.ShapeDtypeStruct((inner * 2 * slots,), jnp.int32),
        in_specs=[SMEM] * 2,
        out_specs=SMEM,
        compiler_params=pltpu.CompilerParams(vmem_limit_bytes=2 * 1024 * 1024),
    )(left_index, right_index)


def add_part(codes_ref, s, side, start, slots, left_ref, right_at, right_slots, total_ref):
    tile = total_ref.shape[1]

    @pl.loop(0, left_ref.shape[0])
    def _(slot):
        code = codes_ref[(s * 2 + side) * slots + start + slot]

        @pl.when(code > 0)
        def _():
            i = lax.div(code - 1, right_slots)
            rows = pl.ds(pl.multiple_of(i * tile, tile), tile)
            total_ref[rows, :] += jnp.dot(
                left_ref[slot],
                right_at(lax.rem(code - 1, right_slots)),
                preferred_element_type=jnp.float32,
            )


def first_products(codes, lefts, rights, slots):
    parts = [(s, part) for s, block in lefts for part in block]
    count = len(parts)
    inner = len(rights) // 2
    right_slots, tile, _ = rights[0].shape

    def kernel(codes_ref, *refs):
        right_refs = refs[count : count + 2 * inner]
        totals = refs[count + 2 * inner : count + 2 * inner + 2]
        last_ref, held = refs[count + 2 * inner + 2 :]
        row, z, _ = position()
        for t in range(inner):
            for side in range(2):
                held[row ^ t, side] = right_refs[2 * t + side][...]
        at = z ^ (inner - 1)
        last_ref[...] = jnp.zeros_like(last_ref)
        for side in range(2):

            @pl.loop(0, slots)
            def _(slot):
                code = codes_ref[((inner - 1) * 2 + side) * slots + slot]

                @pl.when(code > 0)
                def _():
                    rows = pl.ds(pl.multiple_of(slot * tile, tile), tile)
                    i = lax.div(code - 1, right_slots)
                    columns = pl.ds(pl.multiple_of(i * tile, tile), tile)
                    last_ref[side, rows, columns] = held[at, side, lax.rem(code - 1, right_slots)]

        for side in range(2):
            totals[side][...] = jnp.zeros_like(totals[side])
            start, before = 0, None
            for (s, _), left_ref in zip(parts, refs):
                start = start if s == before else 0
                add_part(
                    codes_ref, s, side, start, slots, left_ref,
                    lambda found, s=s: held[z ^ s, side, found], right_slots, totals[side],
                )
                start, before = start + left_ref.shape[0], s

    return pl.pallas_call(
        kernel,
        out_shape=[jax.ShapeDtypeStruct((RT * tile, tile), jnp.float32)] * 2
        + [jax.ShapeDtypeStruct((2, slots * tile, RT * tile), jnp.bfloat16)],
        in_specs=[SMEM] + [VMEM] * (count + 2 * inner),
        out_specs=[VMEM] * 3,
        scratch_shapes=[pltpu.VMEM((inner, 2, right_slots, tile, tile), jnp.bfloat16)],
        compiler_params=pltpu.CompilerParams(vmem_limit_bytes=32 * 1024 * 1024),
        cost_estimate=pl.CostEstimate(
            flops=4 * inner * slots * tile**3, bytes_accessed=2 * inner * slots * tile**2, transcendentals=0
        ),
    )(codes, *[part for _, part in parts], *rights)


def last_products(parts, right, total, side, finish, out_shape):
    (left,) = parts
    slots, tile, _ = left.shape

    def kernel(left_ref, right_ref, total_ref, out_ref):
        added = jnp.zeros((tile, RT * tile), jnp.float32)
        for slot in range(0, slots, 2):
            both = min(2, slots - slot)
            tiles = [left_ref[slot + n] for n in range(both)]
            added += jnp.dot(
                jnp.concatenate(tiles, axis=1),
                right_ref[side, slot * tile : (slot + both) * tile, :],
                preferred_element_type=jnp.float32,
            )
        sums = [
            total_ref[i * tile : (i + 1) * tile, :] + added[:, i * tile : (i + 1) * tile] for i in range(RT)
        ]
        finish(sums, out_ref)

    return pl.pallas_call(
        kernel,
        out_shape=out_shape,
        in_specs=[VMEM] * 3,
        out_specs=VMEM,
        compiler_params=pltpu.CompilerParams(vmem_limit_bytes=16 * 1024 * 1024),
        cost_estimate=pl.CostEstimate(
            flops=2 * slots * tile**3, bytes_accessed=2 * slots * tile**2, transcendentals=0
        ),
    )(left, right, total)


def write_sum(sums, out_ref):
    out_ref[...] = jnp.concatenate(sums)


def write_coded(sums, out_ref):
    tile = out_ref.shape[1]
    exponents = jnp.zeros((PAD, tile), jnp.float32)
    for i, values in enumerate(sums):
        largest = jnp.max(jnp.abs(values), axis=0, keepdims=True)
        exponent = jnp.clip(jnp.floor(jnp.log2(largest)) + 1.0, -LEAST, LEAST)
        coded = jnp.round(values * jnp.exp2(BITS - exponent))
        coded = jnp.clip(coded, -(2.0**BITS) + 1.0, 2.0**BITS - 1.0)
        out_ref[i * tile : (i + 1) * tile, :] = coded.astype(jnp.int32).astype(jnp.int16)
        at = lax.broadcasted_iota(jnp.int32, (PAD, tile), 0)
        exponents = jnp.where(at == i, exponent, exponents)
    out_ref[RT * tile :, :] = exponents.astype(jnp.int32).astype(jnp.int16)


def add_coded(total, coded):
    def kernel(total_ref, coded_ref, out_ref):
        tile = total_ref.shape[1]
        exponents = coded_ref[RT * tile :, :].astype(jnp.int32).astype(jnp.float32)
        for i in range(RT):
            rows = slice(i * tile, (i + 1) * tile)
            scale = jnp.exp2(exponents[i : i + 1, :] - BITS)
            values = coded_ref[rows, :].astype(jnp.int32).astype(jnp.float32)
            out_ref[rows, :] = (total_ref[rows, :] + values * scale).astype(out_ref.dtype)

    return pl.pallas_call(
        kernel,
        out_shape=jax.ShapeDtypeStruct(total.shape, jnp.bfloat16),
        in_specs=[VMEM] * 2,
        out_specs=VMEM,
        compiler_params=pltpu.CompilerParams(vmem_limit_bytes=8 * 1024 * 1024),
    )(total, coded)


def across(block, axis, mask):
    route = [(i, i ^ mask) for i in range(lax.axis_size(axis))]
    return lax.ppermute(block, axis, route)


def crossed(block, mask):
    rows, cols = lax.axis_size("row"), lax.axis_size("col")
    route = [(r * cols + c, (r ^ mask) * cols + (c ^ 1)) for r in range(rows) for c in range(cols)]
    return lax.ppermute(block, ("row", "col"), route)


def gather(block, beside, place):
    distance = lax.axis_size("col") // 4
    steps = [distance >> n for n in range(distance.bit_length())]
    later, _ = lax.optimization_barrier((block, place))
    came = [across(later if d == 1 else block, "col", 2 * d) for d in steps]
    came[:-1], beside = lax.optimization_barrier((came[:-1], beside))
    blocks = {0: block, **dict(zip(steps, came))}
    for d in steps:
        for s in sorted(blocks):
            if s ^ d not in blocks and s & (d - 1) == 0:
                blocks[s ^ d] = across(blocks[s], "col", 2 * d)
    return [(s, (blocks[s],)) for s in range(len(blocks))], beside


def shards(left_tiles, left_index, right_tiles, right_index):
    y = lax.axis_index("col") & 1
    left = left_tiles[0, 0]
    right = right_tiles[0, 0]
    slots = left.shape[0]

    codes = find_matches(left_index, right_index)
    given = lax.dynamic_index_in_dim(right, 1 - y, 0, keepdims=False)
    own = lax.dynamic_index_in_dim(right, y, 0, keepdims=False)
    lefts, codes = gather(left, codes, y)
    rights = []
    for t in range(0, lax.axis_size("row"), 2):
        pair = [across(own, "row", t) if t else own, crossed(given, t)]
        if not t:
            pair[0], near = lax.optimization_barrier((pair[0], lefts[1][1]))
            lefts[1] = (1, near)
        rights += pair + [across(half, "row", 1) for half in pair]

    mine, other, right_last = first_products(codes, lefts[:-1], rights, slots)
    last = (lefts[-1][1], right_last)
    rows, tile = mine.shape
    coded = last_products(
        *last, other, 1, write_coded, jax.ShapeDtypeStruct((rows + PAD, tile), jnp.int16)
    )
    coming = across(coded, "col", 1)
    mine = last_products(*last, mine, 0, write_sum, jax.ShapeDtypeStruct((rows, tile), jnp.float32))
    return add_coded(mine, coming)


def solution(mesh):
    return jax.shard_map(
        shards,
        mesh=mesh,
        in_specs=(
            P("row", "col", None, None, None),
            P(),
            P("row", "col", None, None, None, None),
            P(),
        ),
        out_specs=P("row", "col"),
        check_vma=False,
    )
```

```python
import jax
import jax.numpy as jnp
from jax import lax
from jax.experimental import pallas as pl
from jax.experimental.pallas import tpu as pltpu
from jax.sharding import PartitionSpec as P

KT = 8
RT = 2
SIDES = 3
HOLD = 12 * 10**8
EARLY = 10**8
LATE = 10**11
BITS = 15
LEAST = 100
PAD = 16
SMEM = pl.BlockSpec(memory_space=pltpu.SMEM)
VMEM = pl.BlockSpec(memory_space=pltpu.VMEM)


def position():
    col = lax.axis_index("col")
    return lax.axis_index("row"), col >> 1, col & 1


def counting(side, places):
    early = [s for s in range(places) if s % 2 == 0 or s == 1]
    return [range(places), early, [s for s in early if s > 1]][side]


def code_at(s, side, places, slots):
    pairs = [(other, at) for at in range(SIDES) for other in counting(at, places)]
    return pairs.index((s, side)) * slots


def find_matches(left_index, right_index):
    slots = left_index.shape[-1]
    places, _, _, right_slots = right_index.shape
    left_index = left_index.transpose(2, 0, 1)
    right_index = right_index.transpose(0, 3, 2, 1)
    total = sum(len(counting(side, places)) for side in range(SIDES)) * slots

    def kernel(li_ref, ri_ref, codes_ref):
        row, z, y = position()
        for side in range(SIDES):
            column = 2 * (z ^ (side >> 1)) + (y ^ min(side, 1))
            for s in counting(side, places):
                zp = z ^ s
                base = code_at(s, side, places, slots)
                have = [ri_ref[zp, t, y, column] for t in range(right_slots)]

                @pl.loop(0, slots)
                def _(slot):
                    at = li_ref[slot, row, 2 * zp + y]
                    k = lax.rem(at, KT)
                    first = 1 + lax.div(at, KT) * right_slots
                    code = jnp.int32(0)
                    for t in range(right_slots):
                        code = jnp.where(have[t] == k, first + t, code)
                    codes_ref[base + slot] = jnp.where(at < RT * KT, code, 0)

    return pl.pallas_call(
        kernel,
        out_shape=jax.ShapeDtypeStruct((total,), jnp.int32),
        in_specs=[SMEM] * 2,
        out_specs=SMEM,
        compiler_params=pltpu.CompilerParams(vmem_limit_bytes=2 * 1024 * 1024),
    )(left_index, right_index)


def add_block(codes_ref, base, left_ref, right_at, right_slots, total_ref):
    slots, tile, _ = left_ref.shape

    @pl.loop(0, slots)
    def _(slot):
        code = codes_ref[base + slot]

        @pl.when(code > 0)
        def _():
            i = lax.div(code - 1, right_slots)
            rows = pl.ds(pl.multiple_of(i * tile, tile), tile)
            total_ref[rows, :] += jnp.dot(
                left_ref[slot],
                right_at(lax.rem(code - 1, right_slots)),
                preferred_element_type=jnp.float32,
            )


def products(codes, lefts, rights, sides, finish, out_shape, flops, start=None):
    distances = sorted(lefts)
    count = len(lefts)
    places = len(rights) // 2
    right_slots, tile, _ = rights[0].shape
    slots = lefts[distances[0]].shape[0]
    starts = [] if start is None else [start]

    def kernel(codes_ref, *refs):
        left_refs = dict(zip(distances, refs))
        right_refs = refs[count : count + 2 * places]
        start_refs = refs[count + 2 * places :][: len(starts)]
        outs = refs[count + 2 * places + len(starts) : -2]
        total_ref, held = refs[-2:]
        row, z, _ = position()
        for at in sorted({min(side, 1) for side in sides}):
            for t in range(places):
                held[t, at] = right_refs[2 * t + at][...]
        for side, out_ref in zip(sides, outs):
            total_ref[...] = start_refs[0][...] if starts else jnp.zeros_like(total_ref)
            for s in counting(side, places):
                if s in left_refs:
                    t = row ^ z ^ s ^ (side >> 1)
                    add_block(
                        codes_ref, code_at(s, side, places, slots), left_refs[s],
                        lambda found, t=t: held[t, min(side, 1), found], right_slots, total_ref,
                    )
            finish(total_ref, out_ref)

    return pl.pallas_call(
        kernel,
        out_shape=[out_shape] * len(sides),
        in_specs=[SMEM] + [VMEM] * (count + 2 * places + len(starts)),
        out_specs=[VMEM] * len(sides),
        scratch_shapes=[
            pltpu.VMEM((RT * tile, tile), jnp.float32),
            pltpu.VMEM((places, 2, right_slots, tile, tile), jnp.bfloat16),
        ],
        compiler_params=pltpu.CompilerParams(vmem_limit_bytes=32 * 1024 * 1024),
        cost_estimate=pl.CostEstimate(
            flops=flops,
            bytes_accessed=2 * count * slots * tile**2,
            transcendentals=0,
        ),
    )(codes, *[lefts[s] for s in distances], *rights, *starts)


def own_products(codes, early, late, rights, flops):
    distances = sorted(early)
    count = len(early)
    places = len(rights) // 2
    right_slots, tile, _ = rights[0].shape
    slots = early[0].shape[0]

    def kernel(codes_ref, *refs):
        left_refs = dict(zip(distances, refs))
        right_refs = refs[count : count + places]
        total_ref, dense_ref, held = refs[count + places :]
        row, z, _ = position()
        for t in range(places):
            held[t] = right_refs[t][...]
        dense_ref[...] = jnp.zeros_like(dense_ref)
        for n, s in enumerate(late):
            base = code_at(s, 0, places, slots)
            at = row ^ z ^ s

            @pl.loop(0, slots)
            def _(slot):
                code = codes_ref[base + slot]

                @pl.when(code > 0)
                def _():
                    rows = pl.ds(pl.multiple_of(slot * tile, tile), tile)
                    i = lax.div(code - 1, right_slots)
                    columns = pl.ds(pl.multiple_of(i * tile, tile), tile)
                    dense_ref[n, rows, columns] = held[at, lax.rem(code - 1, right_slots)]

        total_ref[...] = jnp.zeros_like(total_ref)
        for s in distances:
            at = row ^ z ^ s
            add_block(
                codes_ref, code_at(s, 0, places, slots), left_refs[s],
                lambda found, at=at: held[at, found], right_slots, total_ref,
            )

    return pl.pallas_call(
        kernel,
        out_shape=[
            jax.ShapeDtypeStruct((RT * tile, tile), jnp.float32),
            jax.ShapeDtypeStruct((len(late), slots * tile, RT * tile), jnp.bfloat16),
        ],
        in_specs=[SMEM] + [VMEM] * (count + places),
        out_specs=[VMEM] * 2,
        scratch_shapes=[pltpu.VMEM((places, right_slots, tile, tile), jnp.bfloat16)],
        compiler_params=pltpu.CompilerParams(vmem_limit_bytes=32 * 1024 * 1024),
        cost_estimate=pl.CostEstimate(flops=flops, bytes_accessed=2 * slots * tile**2, transcendentals=0),
    )(codes, *[early[s] for s in distances], *rights[::2])


def last_products(lefts, dense, total, flops):
    count = len(lefts)
    slots, tile, _ = lefts[0].shape

    def kernel(*refs):
        left_refs = refs[:count]
        dense_ref, total_ref, out_ref = refs[count:]
        added = jnp.zeros((tile, RT * tile), jnp.float32)
        for n, left_ref in enumerate(left_refs):
            for slot in range(0, slots, 2):
                both = min(2, slots - slot)
                added += jnp.dot(
                    jnp.concatenate([left_ref[slot + m] for m in range(both)], axis=1),
                    dense_ref[n, slot * tile : (slot + both) * tile, :],
                    preferred_element_type=jnp.float32,
                )
        for i in range(RT):
            rows = slice(i * tile, (i + 1) * tile)
            out_ref[rows, :] = total_ref[rows, :] + added[:, rows]

    return pl.pallas_call(
        kernel,
        out_shape=jax.ShapeDtypeStruct(total.shape, total.dtype),
        in_specs=[VMEM] * (count + 2),
        out_specs=VMEM,
        compiler_params=pltpu.CompilerParams(vmem_limit_bytes=16 * 1024 * 1024),
        cost_estimate=pl.CostEstimate(flops=flops, bytes_accessed=2 * slots * tile**2, transcendentals=0),
    )(*lefts, dense, total)


def hold(blocks):
    count = len(blocks)

    def kernel(*refs):
        for block_ref, out_ref in zip(refs[:count], refs[count:]):
            out_ref[...] = block_ref[...]

    return pl.pallas_call(
        kernel,
        out_shape=[jax.ShapeDtypeStruct(block.shape, block.dtype) for block in blocks],
        in_specs=[VMEM] * count,
        out_specs=[VMEM] * count,
        compiler_params=pltpu.CompilerParams(vmem_limit_bytes=4 * 1024 * 1024),
        cost_estimate=pl.CostEstimate(flops=HOLD, bytes_accessed=0, transcendentals=0),
    )(*blocks)


def write_coded(sum_ref, out_ref):
    tile = sum_ref.shape[1]
    exponents = jnp.zeros((PAD, tile), jnp.float32)
    for i in range(RT):
        values = sum_ref[i * tile : (i + 1) * tile, :]
        largest = jnp.max(jnp.abs(values), axis=0, keepdims=True)
        exponent = jnp.clip(jnp.floor(jnp.log2(largest)) + 1.0, -LEAST, LEAST)
        coded = jnp.round(values * jnp.exp2(BITS - exponent))
        coded = jnp.clip(coded, -(2.0**BITS) + 1.0, 2.0**BITS - 1.0)
        out_ref[i * tile : (i + 1) * tile, :] = coded.astype(jnp.int32).astype(jnp.int16)
        at = lax.broadcasted_iota(jnp.int32, (PAD, tile), 0)
        exponents = jnp.where(at == i, exponent, exponents)
    out_ref[RT * tile :, :] = exponents.astype(jnp.int32).astype(jnp.int16)


def decoded(coded):
    tile = coded.shape[1]
    exponents = coded[RT * tile : RT * tile + RT].astype(jnp.float32)
    scale = jnp.repeat(jnp.exp2(exponents - BITS), tile, axis=0)
    return coded[: RT * tile].astype(jnp.float32) * scale


def across(block, axis, mask):
    route = [(i, i ^ mask) for i in range(lax.axis_size(axis))]
    return lax.ppermute(block, axis, route)


def travel(block, source):
    rows, cols = lax.axis_size("row"), lax.axis_size("col")
    route = []
    for r in range(rows):
        for c in range(cols):
            row, z, y = source(r, c >> 1, c & 1)
            route.append((row * cols + 2 * z + y, r * cols + c))
    return lax.ppermute(block, ("row", "col"), route)


def other_half(given, t):
    def source(r, z, y):
        apart = r ^ t ^ z
        swap = apart % 2 if apart > 1 else 0
        return r ^ t ^ swap, z ^ swap, y ^ 1

    return travel(given, source)


def gather(block, beside, ahead):
    distance = lax.axis_size("col") // 4
    steps = [distance >> n for n in range(distance.bit_length())]
    later, ahead = lax.optimization_barrier((block, ahead))
    came = [across(later if d == 1 else block, "col", 2 * d) for d in steps]
    came[:-1], beside = lax.optimization_barrier((came[:-1], beside))
    blocks = {0: block, **dict(zip(steps, came))}
    for d in steps:
        for s in sorted(blocks):
            if s ^ d not in blocks and s & (d - 1) == 0:
                blocks[s ^ d] = across(blocks[s], "col", 2 * d)
    return blocks, beside, ahead


def shards(left_tiles, left_index, right_tiles, right_index):
    y = lax.axis_index("col") & 1
    left = left_tiles[0, 0]
    right = right_tiles[0, 0]
    tile = left.shape[-1]

    codes = find_matches(left_index, right_index)
    given = lax.dynamic_index_in_dim(right, 1 - y, 0, keepdims=False)
    own = lax.dynamic_index_in_dim(right, y, 0, keepdims=False)
    lefts, codes, (own, given) = gather(left, codes, (own, given))
    places = range(0, lax.axis_size("row"), 2)
    others = hold([other_half(given, t) for t in places])
    rights = []
    for t, other in zip(places, others):
        pair = [across(own, "row", t) if t else own, other]
        if not t:
            pair[0], lefts[1] = lax.optimization_barrier((pair[0], lefts[1]))
        rights += pair + [across(half, "row", 1) for half in pair]

    coded = jax.ShapeDtypeStruct((RT * tile + PAD, tile), jnp.int16)
    early = {s: lefts[s] for s in counting(1, len(lefts))}
    late = [s for s in sorted(lefts) if s not in early]
    to_other, to_far = products(codes, early, rights, (1, 2), write_coded, coded, EARLY)
    coming = across(to_other, "col", 1)
    from_far = across(to_far, "col", 3)
    mine, dense = own_products(codes, early, late, rights, 10**8)
    mine = last_products([lefts[s] for s in late], dense, mine, LATE)
    mine, coming, from_far = lax.optimization_barrier((mine, coming, from_far))
    return (mine + decoded(coming) + decoded(from_far)).astype(jnp.bfloat16)


def solution(mesh):
    return jax.shard_map(
        shards,
        mesh=mesh,
        in_specs=(
            P("row", "col", None, None, None),
            P(),
            P("row", "col", None, None, None, None),
            P(),
        ),
        out_specs=P("row", "col"),
        check_vma=False,
    )
```

```python
import jax
import jax.numpy as jnp
from jax import lax
from jax.experimental import pallas as pl
from jax.experimental.pallas import tpu as pltpu
from jax.sharding import PartitionSpec as P

KT = 8
RT = 2
BITS = 15
LEAST = 100
PAD = 16
SMEM = pl.BlockSpec(memory_space=pltpu.SMEM)
VMEM = pl.BlockSpec(memory_space=pltpu.VMEM)


def position():
    col = lax.axis_index("col")
    return lax.axis_index("row"), col >> 1, col & 1


def find_matches(left_index, right_index):
    slots = left_index.shape[-1]
    inner, _, _, right_slots = right_index.shape
    left_index = left_index.transpose(2, 0, 1)
    right_index = right_index.transpose(0, 3, 2, 1)

    def kernel(li_ref, ri_ref, codes_ref):
        row, z, y = position()

        @pl.loop(0, inner)
        def _(s):
            zp = z ^ s
            for side in range(2):
                column = 2 * z + (y if side == 0 else 1 - y)
                have = [ri_ref[zp, t, y, column] for t in range(right_slots)]
                for slot in range(slots):
                    at = li_ref[slot, row, 2 * zp + y]
                    k = lax.rem(at, KT)
                    first = 1 + lax.div(at, KT) * right_slots
                    code = jnp.int32(0)
                    for t in range(right_slots):
                        code = jnp.where(have[t] == k, first + t, code)
                    codes_ref[(s * 2 + side) * slots + slot] = jnp.where(at < RT * KT, code, 0)

    return pl.pallas_call(
        kernel,
        out_shape=jax.ShapeDtypeStruct((inner * 2 * slots,), jnp.int32),
        in_specs=[SMEM] * 2,
        out_specs=SMEM,
        compiler_params=pltpu.CompilerParams(vmem_limit_bytes=2 * 1024 * 1024),
    )(left_index, right_index)


def add_part(codes_ref, s, side, start, slots, left_ref, right_at, right_slots, total_ref):
    tile = total_ref.shape[1]

    @pl.loop(0, left_ref.shape[0])
    def _(slot):
        code = codes_ref[(s * 2 + side) * slots + start + slot]

        @pl.when(code > 0)
        def _():
            i = lax.div(code - 1, right_slots)
            rows = pl.ds(pl.multiple_of(i * tile, tile), tile)
            total_ref[rows, :] += jnp.dot(
                left_ref[slot],
                right_at(lax.rem(code - 1, right_slots)),
                preferred_element_type=jnp.float32,
            )


def first_products(codes, lefts, rights, slots):
    parts = [(s, part) for s, block in lefts for part in block]
    count = len(parts)
    inner = len(rights) // 2
    right_slots, tile, _ = rights[0].shape

    def kernel(codes_ref, *refs):
        right_refs = refs[count : count + 2 * inner]
        totals = refs[count + 2 * inner : count + 2 * inner + 2]
        last_ref, held = refs[count + 2 * inner + 2 :]
        row, z, _ = position()
        for t in range(inner):
            for side in range(2):
                held[row ^ t, side] = right_refs[2 * t + side][...]
        at = z ^ (inner - 1)
        last_ref[...] = jnp.zeros_like(last_ref)
        for side in range(2):

            @pl.loop(0, slots)
            def _(slot):
                code = codes_ref[((inner - 1) * 2 + side) * slots + slot]

                @pl.when(code > 0)
                def _():
                    rows = pl.ds(pl.multiple_of(slot * tile, tile), tile)
                    i = lax.div(code - 1, right_slots)
                    columns = pl.ds(pl.multiple_of(i * tile, tile), tile)
                    last_ref[side, rows, columns] = held[at, side, lax.rem(code - 1, right_slots)]

        for side in range(2):
            totals[side][...] = jnp.zeros_like(totals[side])
            start, before = 0, None
            for (s, _), left_ref in zip(parts, refs):
                start = start if s == before else 0
                add_part(
                    codes_ref, s, side, start, slots, left_ref,
                    lambda found, s=s: held[z ^ s, side, found], right_slots, totals[side],
                )
                start, before = start + left_ref.shape[0], s

    return pl.pallas_call(
        kernel,
        out_shape=[jax.ShapeDtypeStruct((RT * tile, tile), jnp.float32)] * 2
        + [jax.ShapeDtypeStruct((2, slots * tile, RT * tile), jnp.bfloat16)],
        in_specs=[SMEM] + [VMEM] * (count + 2 * inner),
        out_specs=[VMEM] * 3,
        scratch_shapes=[pltpu.VMEM((inner, 2, right_slots, tile, tile), jnp.bfloat16)],
        compiler_params=pltpu.CompilerParams(vmem_limit_bytes=32 * 1024 * 1024),
        cost_estimate=pl.CostEstimate(
            flops=4 * inner * slots * tile**3, bytes_accessed=2 * inner * slots * tile**2, transcendentals=0
        ),
    )(codes, *[part for _, part in parts], *rights)


def last_products(parts, right, total, side, finish, out_shape):
    slots, tile, _ = parts[0].shape

    def kernel(odd_ref, even_ref, right_ref, total_ref, out_ref):
        odd = lax.axis_index("row") & 1
        added = jnp.zeros((tile, RT * tile), jnp.float32)
        for slot in range(0, slots, 2):
            both = min(2, slots - slot)
            tiles = [
                jnp.where(odd == 1, odd_ref[slot + n], even_ref[slot + n]) for n in range(both)
            ]
            added += jnp.dot(
                jnp.concatenate(tiles, axis=1),
                right_ref[side, slot * tile : (slot + both) * tile, :],
                preferred_element_type=jnp.float32,
            )
        sums = [
            total_ref[i * tile : (i + 1) * tile, :] + added[:, i * tile : (i + 1) * tile] for i in range(RT)
        ]
        finish(sums, out_ref)

    return pl.pallas_call(
        kernel,
        out_shape=out_shape,
        in_specs=[VMEM] * 4,
        out_specs=VMEM,
        compiler_params=pltpu.CompilerParams(vmem_limit_bytes=16 * 1024 * 1024),
        cost_estimate=pl.CostEstimate(
            flops=2 * slots * tile**3, bytes_accessed=2 * slots * tile**2, transcendentals=0
        ),
    )(*parts, right, total)


def write_sum(sums, out_ref):
    out_ref[...] = jnp.concatenate(sums)


def write_coded(sums, out_ref):
    tile = out_ref.shape[1]
    exponents = jnp.zeros((PAD, tile), jnp.float32)
    for i, values in enumerate(sums):
        largest = jnp.max(jnp.abs(values), axis=0, keepdims=True)
        exponent = jnp.clip(jnp.floor(jnp.log2(largest)) + 1.0, -LEAST, LEAST)
        coded = jnp.round(values * jnp.exp2(BITS - exponent))
        coded = jnp.clip(coded, -(2.0**BITS) + 1.0, 2.0**BITS - 1.0)
        out_ref[i * tile : (i + 1) * tile, :] = coded.astype(jnp.int32).astype(jnp.int16)
        at = lax.broadcasted_iota(jnp.int32, (PAD, tile), 0)
        exponents = jnp.where(at == i, exponent, exponents)
    out_ref[RT * tile :, :] = exponents.astype(jnp.int32).astype(jnp.int16)


def add_coded(total, coded):
    def kernel(total_ref, coded_ref, out_ref):
        tile = total_ref.shape[1]
        exponents = coded_ref[RT * tile :, :].astype(jnp.int32).astype(jnp.float32)
        for i in range(RT):
            rows = slice(i * tile, (i + 1) * tile)
            scale = jnp.exp2(exponents[i : i + 1, :] - BITS)
            values = coded_ref[rows, :].astype(jnp.int32).astype(jnp.float32)
            out_ref[rows, :] = (total_ref[rows, :] + values * scale).astype(out_ref.dtype)

    return pl.pallas_call(
        kernel,
        out_shape=jax.ShapeDtypeStruct(total.shape, jnp.bfloat16),
        in_specs=[VMEM] * 2,
        out_specs=VMEM,
        compiler_params=pltpu.CompilerParams(vmem_limit_bytes=8 * 1024 * 1024),
    )(total, coded)


def across(block, axis, mask):
    route = [(i, i ^ mask) for i in range(lax.axis_size(axis))]
    return lax.ppermute(block, axis, route)


def crossed(block, mask):
    rows, cols = lax.axis_size("row"), lax.axis_size("col")
    route = [(r * cols + c, (r ^ mask) * cols + (c ^ 1)) for r in range(rows) for c in range(cols)]
    return lax.ppermute(block, ("row", "col"), route)


def passed_on(block):
    rows, cols = lax.axis_size("row"), lax.axis_size("col")
    moved = []
    for core in range(2):
        route = [
            (r * cols + c, r * cols + (c ^ 2 if r % 2 == core else c)) for r in range(rows) for c in range(cols)
        ]
        moved.append(lax.ppermute(block, ("row", "col"), route))
    return moved[::-1]


def gather(block, beside, place):
    distance = lax.axis_size("col") // 4
    steps = [distance >> n for n in range(distance.bit_length())]
    later, _ = lax.optimization_barrier((block, place))
    came = [across(later if d == 1 else block, "col", 2 * d) for d in steps]
    came[:-1], beside = lax.optimization_barrier((came[:-1], beside))
    blocks = {0: block, **dict(zip(steps, came))}
    for d in steps:
        for s in sorted(blocks):
            if s ^ d not in blocks and s & (d - 1) == 0 and s ^ d != 2 * distance - 1:
                blocks[s ^ d] = across(blocks[s], "col", 2 * d)
    found = [(s, (blocks[s],)) for s in range(2 * distance - 1)]
    return found + [(2 * distance - 1, passed_on(blocks[2 * distance - 2]))], beside


def shards(left_tiles, left_index, right_tiles, right_index):
    y = lax.axis_index("col") & 1
    left = left_tiles[0, 0]
    right = right_tiles[0, 0]
    slots = left.shape[0]

    codes = find_matches(left_index, right_index)
    given = lax.dynamic_index_in_dim(right, 1 - y, 0, keepdims=False)
    own = lax.dynamic_index_in_dim(right, y, 0, keepdims=False)
    lefts, codes = gather(left, codes, y)
    rights = []
    for t in range(0, lax.axis_size("row"), 2):
        pair = [across(own, "row", t) if t else own, crossed(given, t)]
        if not t:
            pair[0], near = lax.optimization_barrier((pair[0], lefts[1][1]))
            lefts[1] = (1, near)
        rights += pair + [across(half, "row", 1) for half in pair]

    mine, other, right_last = first_products(codes, lefts[:-1], rights, slots)
    last = (lefts[-1][1], right_last)
    rows, tile = mine.shape
    coded = last_products(
        *last, other, 1, write_coded, jax.ShapeDtypeStruct((rows + PAD, tile), jnp.int16)
    )
    coming = across(coded, "col", 1)
    mine = last_products(*last, mine, 0, write_sum, jax.ShapeDtypeStruct((rows, tile), jnp.float32))
    return add_coded(mine, coming)


def solution(mesh):
    return jax.shard_map(
        shards,
        mesh=mesh,
        in_specs=(
            P("row", "col", None, None, None),
            P(),
            P("row", "col", None, None, None, None),
            P(),
        ),
        out_specs=P("row", "col"),
        check_vma=False,
    )
```

```python
import jax
import jax.numpy as jnp
from jax import lax
from jax.experimental import pallas as pl
from jax.experimental.pallas import tpu as pltpu
from jax.sharding import PartitionSpec as P

KT = 8
RT = 2
BITS = 15
LEAST = 100
PAD = 16
SMEM = pl.BlockSpec(memory_space=pltpu.SMEM)
VMEM = pl.BlockSpec(memory_space=pltpu.VMEM)


def position():
    col = lax.axis_index("col")
    return lax.axis_index("row"), col >> 1, col & 1


def find_matches(left_index, right_index):
    slots = left_index.shape[-1]
    inner, _, _, right_slots = right_index.shape
    left_index = left_index.transpose(2, 0, 1)
    right_index = right_index.transpose(0, 3, 2, 1)

    def kernel(li_ref, ri_ref, codes_ref):
        row, z, y = position()

        @pl.loop(0, inner)
        def _(s):
            zp = z ^ s
            for side in range(2):
                column = 2 * z + (y if side == 0 else 1 - y)
                have = [ri_ref[zp, t, y, column] for t in range(right_slots)]
                for slot in range(slots):
                    at = li_ref[slot, row, 2 * zp + y]
                    k = lax.rem(at, KT)
                    first = 1 + lax.div(at, KT) * right_slots
                    code = jnp.int32(0)
                    for t in range(right_slots):
                        code = jnp.where(have[t] == k, first + t, code)
                    codes_ref[(s * 2 + side) * slots + slot] = jnp.where(at < RT * KT, code, 0)

    return pl.pallas_call(
        kernel,
        out_shape=jax.ShapeDtypeStruct((inner * 2 * slots,), jnp.int32),
        in_specs=[SMEM] * 2,
        out_specs=SMEM,
        compiler_params=pltpu.CompilerParams(vmem_limit_bytes=2 * 1024 * 1024),
    )(left_index, right_index)


def add_part(codes_ref, s, side, start, slots, left_ref, right_at, right_slots, total_ref):
    tile = total_ref.shape[1]

    @pl.loop(0, left_ref.shape[0])
    def _(slot):
        code = codes_ref[(s * 2 + side) * slots + start + slot]

        @pl.when(code > 0)
        def _():
            i = lax.div(code - 1, right_slots)
            rows = pl.ds(pl.multiple_of(i * tile, tile), tile)
            total_ref[rows, :] += jnp.dot(
                left_ref[slot],
                right_at(lax.rem(code - 1, right_slots)),
                preferred_element_type=jnp.float32,
            )


def first_products(codes, lefts, rights, slots):
    parts = [(s, part) for s, block in lefts for part in block]
    count = len(parts)
    inner = len(rights) // 2
    right_slots, tile, _ = rights[0].shape

    def kernel(codes_ref, *refs):
        right_refs = refs[count : count + 2 * inner]
        totals = refs[count + 2 * inner : count + 2 * inner + 2]
        last_ref, held = refs[count + 2 * inner + 2 :]
        row, z, _ = position()
        for t in range(inner):
            for side in range(2):
                held[row ^ t, side] = right_refs[2 * t + side][...]
        at = z ^ (inner - 1)
        last_ref[...] = jnp.zeros_like(last_ref)
        for side in range(2):

            @pl.loop(0, slots)
            def _(slot):
                code = codes_ref[((inner - 1) * 2 + side) * slots + slot]

                @pl.when(code > 0)
                def _():
                    rows = pl.ds(pl.multiple_of(slot * tile, tile), tile)
                    i = lax.div(code - 1, right_slots)
                    columns = pl.ds(pl.multiple_of(i * tile, tile), tile)
                    last_ref[side, rows, columns] = held[at, side, lax.rem(code - 1, right_slots)]

        for side in range(2):
            totals[side][...] = jnp.zeros_like(totals[side])
            start, before = 0, None
            for (s, _), left_ref in zip(parts, refs):
                start = start if s == before else 0
                add_part(
                    codes_ref, s, side, start, slots, left_ref,
                    lambda found, s=s: held[z ^ s, side, found], right_slots, totals[side],
                )
                start, before = start + left_ref.shape[0], s

    return pl.pallas_call(
        kernel,
        out_shape=[jax.ShapeDtypeStruct((RT * tile, tile), jnp.float32)] * 2
        + [jax.ShapeDtypeStruct((2, slots * tile, RT * tile), jnp.bfloat16)],
        in_specs=[SMEM] + [VMEM] * (count + 2 * inner),
        out_specs=[VMEM] * 3,
        scratch_shapes=[pltpu.VMEM((inner, 2, right_slots, tile, tile), jnp.bfloat16)],
        compiler_params=pltpu.CompilerParams(vmem_limit_bytes=32 * 1024 * 1024),
        cost_estimate=pl.CostEstimate(
            flops=4 * inner * slots * tile**3, bytes_accessed=2 * inner * slots * tile**2, transcendentals=0
        ),
    )(codes, *[part for _, part in parts], *rights)


def last_products(parts, right, total, side, finish, out_shape):
    (left,) = parts
    slots, tile, _ = left.shape

    def kernel(left_ref, right_ref, total_ref, out_ref):
        added = jnp.zeros((tile, RT * tile), jnp.float32)
        for slot in range(0, slots, 2):
            both = min(2, slots - slot)
            tiles = [left_ref[slot + n] for n in range(both)]
            added += jnp.dot(
                jnp.concatenate(tiles, axis=1),
                right_ref[side, slot * tile : (slot + both) * tile, :],
                preferred_element_type=jnp.float32,
            )
        sums = [
            total_ref[i * tile : (i + 1) * tile, :] + added[:, i * tile : (i + 1) * tile] for i in range(RT)
        ]
        finish(sums, out_ref)

    return pl.pallas_call(
        kernel,
        out_shape=out_shape,
        in_specs=[VMEM] * 3,
        out_specs=VMEM,
        compiler_params=pltpu.CompilerParams(vmem_limit_bytes=16 * 1024 * 1024),
        cost_estimate=pl.CostEstimate(
            flops=2 * slots * tile**3, bytes_accessed=2 * slots * tile**2, transcendentals=0
        ),
    )(left, right, total)


def write_sum(sums, out_ref):
    out_ref[...] = jnp.concatenate(sums)


def write_coded(sums, out_ref):
    tile = out_ref.shape[1]
    exponents = jnp.zeros((PAD, tile), jnp.float32)
    for i, values in enumerate(sums):
        largest = jnp.max(jnp.abs(values), axis=0, keepdims=True)
        exponent = jnp.clip(jnp.floor(jnp.log2(largest)) + 1.0, -LEAST, LEAST)
        coded = jnp.round(values * jnp.exp2(BITS - exponent))
        coded = jnp.clip(coded, -(2.0**BITS) + 1.0, 2.0**BITS - 1.0)
        out_ref[i * tile : (i + 1) * tile, :] = coded.astype(jnp.int32).astype(jnp.int16)
        at = lax.broadcasted_iota(jnp.int32, (PAD, tile), 0)
        exponents = jnp.where(at == i, exponent, exponents)
    out_ref[RT * tile :, :] = exponents.astype(jnp.int32).astype(jnp.int16)


def add_coded(total, both):
    def kernel(total_ref, both_ref, out_ref):
        tile = total_ref.shape[1]
        coded_ref = both_ref.at[1 - position()[2]]
        exponents = coded_ref[RT * tile :, :].astype(jnp.int32).astype(jnp.float32)
        for i in range(RT):
            rows = slice(i * tile, (i + 1) * tile)
            scale = jnp.exp2(exponents[i : i + 1, :] - BITS)
            values = coded_ref[rows, :].astype(jnp.int32).astype(jnp.float32)
            out_ref[rows, :] = (total_ref[rows, :] + values * scale).astype(out_ref.dtype)

    return pl.pallas_call(
        kernel,
        out_shape=jax.ShapeDtypeStruct(total.shape, jnp.bfloat16),
        in_specs=[VMEM] * 2,
        out_specs=VMEM,
        compiler_params=pltpu.CompilerParams(vmem_limit_bytes=8 * 1024 * 1024),
    )(total, both)


def across(block, axis, mask):
    route = [(i, i ^ mask) for i in range(lax.axis_size(axis))]
    return lax.ppermute(block, axis, route)


def crossed(block, mask):
    rows, cols = lax.axis_size("row"), lax.axis_size("col")
    route = [(r * cols + c, (r ^ mask) * cols + (c ^ 1)) for r in range(rows) for c in range(cols)]
    return lax.ppermute(block, ("row", "col"), route)


def gather(block, beside, place):
    distance = lax.axis_size("col") // 4
    steps = [distance >> n for n in range(distance.bit_length())]
    later, _ = lax.optimization_barrier((block, place))
    came = [across(later if d == 1 else block, "col", 2 * d) for d in steps]
    came[:-1], beside = lax.optimization_barrier((came[:-1], beside))
    blocks = {0: block, **dict(zip(steps, came))}
    for d in steps:
        for s in sorted(blocks):
            if s ^ d not in blocks and s & (d - 1) == 0:
                blocks[s ^ d] = across(blocks[s], "col", 2 * d)
    return [(s, (blocks[s],)) for s in range(len(blocks))], beside


def shards(left_tiles, left_index, right_tiles, right_index):
    y = lax.axis_index("col") & 1
    left = left_tiles[0, 0]
    right = right_tiles[0, 0]
    slots = left.shape[0]

    codes = find_matches(left_index, right_index)
    given = lax.dynamic_index_in_dim(right, 1 - y, 0, keepdims=False)
    own = lax.dynamic_index_in_dim(right, y, 0, keepdims=False)
    lefts, codes = gather(left, codes, y)
    rights = []
    for t in range(0, lax.axis_size("row"), 2):
        pair = [across(own, "row", t) if t else own, crossed(given, t)]
        if not t:
            pair[0], near = lax.optimization_barrier((pair[0], lefts[1][1]))
            lefts[1] = (1, near)
        rights += pair + [across(half, "row", 1) for half in pair]

    mine, other, right_last = first_products(codes, lefts[:-1], rights, slots)
    last = (lefts[-1][1], right_last)
    rows, tile = mine.shape
    coded = last_products(
        *last, other, 1, write_coded, jax.ShapeDtypeStruct((rows + PAD, tile), jnp.int16)
    )
    pairs = [[2 * z, 2 * z + 1] for z in range(lax.axis_size("col") // 2)]
    both = lax.all_gather(coded, "col", axis_index_groups=pairs)
    mine = last_products(*last, mine, 0, write_sum, jax.ShapeDtypeStruct((rows, tile), jnp.float32))
    return add_coded(mine, both)


def solution(mesh):
    return jax.shard_map(
        shards,
        mesh=mesh,
        in_specs=(
            P("row", "col", None, None, None),
            P(),
            P("row", "col", None, None, None, None),
            P(),
        ),
        out_specs=P("row", "col"),
        check_vma=False,
    )
```

```python
import jax
import jax.numpy as jnp
from jax import lax
from jax.experimental import pallas as pl
from jax.experimental.pallas import tpu as pltpu
from jax.sharding import PartitionSpec as P

KT = 8
RT = 2
BITS = 15
LEAST = 100
PAD = 16
SMEM = pl.BlockSpec(memory_space=pltpu.SMEM)
VMEM = pl.BlockSpec(memory_space=pltpu.VMEM)


def position():
    col = lax.axis_index("col")
    return lax.axis_index("row"), col >> 1, col & 1


def find_matches(left_index, right_index):
    slots = left_index.shape[-1]
    inner, _, _, right_slots = right_index.shape
    left_index = left_index.transpose(2, 0, 1)
    right_index = right_index.transpose(0, 3, 2, 1)

    def kernel(li_ref, ri_ref, codes_ref):
        row, z, y = position()

        @pl.loop(0, inner)
        def _(s):
            zp = z ^ s
            for side in range(2):
                column = 2 * z + (y if side == 0 else 1 - y)
                have = [ri_ref[zp, t, y, column] for t in range(right_slots)]
                for slot in range(slots):
                    at = li_ref[slot, row, 2 * zp + y]
                    k = lax.rem(at, KT)
                    first = 1 + lax.div(at, KT) * right_slots
                    code = jnp.int32(0)
                    for t in range(right_slots):
                        code = jnp.where(have[t] == k, first + t, code)
                    codes_ref[(s * 2 + side) * slots + slot] = jnp.where(at < RT * KT, code, 0)

    return pl.pallas_call(
        kernel,
        out_shape=jax.ShapeDtypeStruct((inner * 2 * slots,), jnp.int32),
        in_specs=[SMEM] * 2,
        out_specs=SMEM,
        compiler_params=pltpu.CompilerParams(vmem_limit_bytes=2 * 1024 * 1024),
    )(left_index, right_index)


def add_part(codes_ref, s, side, start, slots, left_ref, right_at, right_slots, total_ref):
    tile = total_ref.shape[1]

    @pl.loop(0, left_ref.shape[0])
    def _(slot):
        code = codes_ref[(s * 2 + side) * slots + start + slot]

        @pl.when(code > 0)
        def _():
            i = lax.div(code - 1, right_slots)
            rows = pl.ds(pl.multiple_of(i * tile, tile), tile)
            total_ref[rows, :] += jnp.dot(
                left_ref[slot],
                right_at(lax.rem(code - 1, right_slots)),
                preferred_element_type=jnp.float32,
            )


def first_products(codes, lefts, last, rights, slots):
    parts = [(s, part) for s, block in lefts for part in block]
    count = len(parts)
    inner = len(rights) // 2
    right_slots, tile, _ = rights[0].shape

    def kernel(codes_ref, *refs):
        right_refs = refs[count : count + 2 * inner]
        totals = refs[count + 2 * inner : count + 2 * inner + 2]
        last_ref, held = refs[count + 2 * inner + 2 :]
        row, z, _ = position()
        for t in range(inner):
            for side in range(2):
                held[row ^ t, side] = right_refs[2 * t + side][...]
        at = z ^ last
        last_ref[...] = jnp.zeros_like(last_ref)
        for side in range(2):

            @pl.loop(0, slots)
            def _(slot):
                code = codes_ref[(last * 2 + side) * slots + slot]

                @pl.when(code > 0)
                def _():
                    rows = pl.ds(pl.multiple_of(slot * tile, tile), tile)
                    i = lax.div(code - 1, right_slots)
                    columns = pl.ds(pl.multiple_of(i * tile, tile), tile)
                    last_ref[side, rows, columns] = held[at, side, lax.rem(code - 1, right_slots)]

        for side in range(2):
            totals[side][...] = jnp.zeros_like(totals[side])
            start, before = 0, None
            for (s, _), left_ref in zip(parts, refs):
                start = start if s == before else 0
                add_part(
                    codes_ref, s, side, start, slots, left_ref,
                    lambda found, s=s: held[z ^ s, side, found], right_slots, totals[side],
                )
                start, before = start + left_ref.shape[0], s

    return pl.pallas_call(
        kernel,
        out_shape=[jax.ShapeDtypeStruct((RT * tile, tile), jnp.float32)] * 2
        + [jax.ShapeDtypeStruct((2, slots * tile, RT * tile), jnp.bfloat16)],
        in_specs=[SMEM] + [VMEM] * (count + 2 * inner),
        out_specs=[VMEM] * 3,
        scratch_shapes=[pltpu.VMEM((inner, 2, right_slots, tile, tile), jnp.bfloat16)],
        compiler_params=pltpu.CompilerParams(vmem_limit_bytes=32 * 1024 * 1024),
        cost_estimate=pl.CostEstimate(
            flops=4 * inner * slots * tile**3, bytes_accessed=2 * inner * slots * tile**2, transcendentals=0
        ),
    )(codes, *[part for _, part in parts], *rights)


def last_products(parts, right, total, side, finish, out_shape):
    (left,) = parts
    slots, tile, _ = left.shape

    def kernel(left_ref, right_ref, total_ref, out_ref):
        added = jnp.zeros((tile, RT * tile), jnp.float32)
        for slot in range(0, slots, 2):
            both = min(2, slots - slot)
            tiles = [left_ref[slot + n] for n in range(both)]
            added += jnp.dot(
                jnp.concatenate(tiles, axis=1),
                right_ref[side, slot * tile : (slot + both) * tile, :],
                preferred_element_type=jnp.float32,
            )
        sums = [
            total_ref[i * tile : (i + 1) * tile, :] + added[:, i * tile : (i + 1) * tile] for i in range(RT)
        ]
        finish(sums, out_ref)

    return pl.pallas_call(
        kernel,
        out_shape=out_shape,
        in_specs=[VMEM] * 3,
        out_specs=VMEM,
        compiler_params=pltpu.CompilerParams(vmem_limit_bytes=16 * 1024 * 1024),
        cost_estimate=pl.CostEstimate(
            flops=2 * slots * tile**3, bytes_accessed=2 * slots * tile**2, transcendentals=0
        ),
    )(left, right, total)


def write_sum(sums, out_ref):
    out_ref[...] = jnp.concatenate(sums)


def write_coded(sums, out_ref):
    tile = out_ref.shape[1]
    exponents = jnp.zeros((PAD, tile), jnp.float32)
    for i, values in enumerate(sums):
        largest = jnp.max(jnp.abs(values), axis=0, keepdims=True)
        exponent = jnp.clip(jnp.floor(jnp.log2(largest)) + 1.0, -LEAST, LEAST)
        coded = jnp.round(values * jnp.exp2(BITS - exponent))
        coded = jnp.clip(coded, -(2.0**BITS) + 1.0, 2.0**BITS - 1.0)
        out_ref[i * tile : (i + 1) * tile, :] = coded.astype(jnp.int32).astype(jnp.int16)
        at = lax.broadcasted_iota(jnp.int32, (PAD, tile), 0)
        exponents = jnp.where(at == i, exponent, exponents)
    out_ref[RT * tile :, :] = exponents.astype(jnp.int32).astype(jnp.int16)


def add_coded(total, coded):
    def kernel(total_ref, coded_ref, out_ref):
        tile = total_ref.shape[1]
        exponents = coded_ref[RT * tile :, :].astype(jnp.int32).astype(jnp.float32)
        for i in range(RT):
            rows = slice(i * tile, (i + 1) * tile)
            scale = jnp.exp2(exponents[i : i + 1, :] - BITS)
            values = coded_ref[rows, :].astype(jnp.int32).astype(jnp.float32)
            out_ref[rows, :] = (total_ref[rows, :] + values * scale).astype(out_ref.dtype)

    return pl.pallas_call(
        kernel,
        out_shape=jax.ShapeDtypeStruct(total.shape, jnp.bfloat16),
        in_specs=[VMEM] * 2,
        out_specs=VMEM,
        compiler_params=pltpu.CompilerParams(vmem_limit_bytes=8 * 1024 * 1024),
    )(total, coded)


def across(block, axis, mask):
    route = [(i, i ^ mask) for i in range(lax.axis_size(axis))]
    return lax.ppermute(block, axis, route)


def crossed(block, mask):
    rows, cols = lax.axis_size("row"), lax.axis_size("col")
    route = [(r * cols + c, (r ^ mask) * cols + (c ^ 1)) for r in range(rows) for c in range(cols)]
    return lax.ppermute(block, ("row", "col"), route)


def gather(block, beside, place):
    places = lax.axis_size("col") // 2
    steps = [places >> n for n in range(1, places.bit_length() - 2)] + [3, 1]
    later, _ = lax.optimization_barrier((block, place))
    came = [across(later if d == 1 else block, "col", 2 * d) for d in steps]
    came[:-1], beside = lax.optimization_barrier((came[:-1], beside))
    blocks = {0: block, **dict(zip(steps, came))}
    spanned = [0]
    for d in steps:
        for s in spanned[1:]:
            blocks[s ^ d] = across(blocks[s], "col", 2 * d)
        spanned += [s ^ d for s in spanned]
    last = spanned[-1]
    order = [s for s in sorted(blocks) if s != last] + [last]
    return [(s, (blocks[s],)) for s in order], beside


def shards(left_tiles, left_index, right_tiles, right_index):
    y = lax.axis_index("col") & 1
    left = left_tiles[0, 0]
    right = right_tiles[0, 0]
    slots = left.shape[0]

    codes = find_matches(left_index, right_index)
    given = lax.dynamic_index_in_dim(right, 1 - y, 0, keepdims=False)
    own = lax.dynamic_index_in_dim(right, y, 0, keepdims=False)
    lefts, codes = gather(left, codes, y)
    rights = []
    for t in range(0, lax.axis_size("row"), 2):
        pair = [across(own, "row", t) if t else own, crossed(given, t)]
        if not t:
            pair[0], near = lax.optimization_barrier((pair[0], lefts[1][1]))
            lefts[1] = (1, near)
        rights += pair + [across(half, "row", 1) for half in pair]

    mine, other, right_last = first_products(codes, lefts[:-1], lefts[-1][0], rights, slots)
    last = (lefts[-1][1], right_last)
    rows, tile = mine.shape
    coded = last_products(
        *last, other, 1, write_coded, jax.ShapeDtypeStruct((rows + PAD, tile), jnp.int16)
    )
    coming = across(coded, "col", 1)
    mine = last_products(*last, mine, 0, write_sum, jax.ShapeDtypeStruct((rows, tile), jnp.float32))
    return add_coded(mine, coming)


def solution(mesh):
    return jax.shard_map(
        shards,
        mesh=mesh,
        in_specs=(
            P("row", "col", None, None, None),
            P(),
            P("row", "col", None, None, None, None),
            P(),
        ),
        out_specs=P("row", "col"),
        check_vma=False,
    )
```

```python
import jax
import jax.numpy as jnp
from jax import lax
from jax.experimental import pallas as pl
from jax.experimental.pallas import tpu as pltpu
from jax.sharding import PartitionSpec as P

KT = 8
RT = 2
BITS = 15
LEAST = 100
PAD = 16
SMEM = pl.BlockSpec(memory_space=pltpu.SMEM)
VMEM = pl.BlockSpec(memory_space=pltpu.VMEM)


def position():
    col = lax.axis_index("col")
    return lax.axis_index("row"), col >> 1, col & 1


def find_matches(left_index, right_index):
    slots = left_index.shape[-1]
    inner, _, _, right_slots = right_index.shape
    left_index = left_index.transpose(2, 0, 1)
    right_index = right_index.transpose(0, 3, 2, 1)

    def kernel(li_ref, ri_ref, codes_ref):
        row, z, y = position()

        @pl.loop(0, inner)
        def _(s):
            zp = z ^ s
            for side in range(2):
                column = 2 * z + (y if side == 0 else 1 - y)
                have = [ri_ref[zp, t, y, column] for t in range(right_slots)]
                for slot in range(slots):
                    at = li_ref[slot, row, 2 * zp + y]
                    k = lax.rem(at, KT)
                    first = 1 + lax.div(at, KT) * right_slots
                    code = jnp.int32(0)
                    for t in range(right_slots):
                        code = jnp.where(have[t] == k, first + t, code)
                    codes_ref[(s * 2 + side) * slots + slot] = jnp.where(at < RT * KT, code, 0)

    return pl.pallas_call(
        kernel,
        out_shape=jax.ShapeDtypeStruct((inner * 2 * slots,), jnp.int32),
        in_specs=[SMEM] * 2,
        out_specs=SMEM,
        compiler_params=pltpu.CompilerParams(vmem_limit_bytes=2 * 1024 * 1024),
    )(left_index, right_index)


def add_part(codes_ref, s, side, start, slots, left_ref, right_at, right_slots, total_ref):
    tile = total_ref.shape[1]

    @pl.loop(0, left_ref.shape[0])
    def _(slot):
        code = codes_ref[(s * 2 + side) * slots + start + slot]

        @pl.when(code > 0)
        def _():
            i = lax.div(code - 1, right_slots)
            rows = pl.ds(pl.multiple_of(i * tile, tile), tile)
            total_ref[rows, :] += jnp.dot(
                left_ref[slot],
                right_at(lax.rem(code - 1, right_slots)),
                preferred_element_type=jnp.float32,
            )


def first_products(codes, lefts, last, rights, slots):
    parts = [(s, part) for s, block in lefts for part in block]
    count = len(parts)
    inner = len(rights) // 2
    right_slots, tile, _ = rights[0].shape

    def kernel(codes_ref, *refs):
        right_refs = refs[count : count + 2 * inner]
        totals = refs[count + 2 * inner : count + 2 * inner + 2]
        last_ref, held = refs[count + 2 * inner + 2 :]
        row, z, _ = position()
        for t in range(inner):
            for side in range(2):
                held[row ^ t, side] = right_refs[2 * t + side][...]
        at = z ^ last
        last_ref[...] = jnp.zeros_like(last_ref)
        for side in range(2):

            @pl.loop(0, slots)
            def _(slot):
                code = codes_ref[(last * 2 + side) * slots + slot]

                @pl.when(code > 0)
                def _():
                    rows = pl.ds(pl.multiple_of(slot * tile, tile), tile)
                    i = lax.div(code - 1, right_slots)
                    columns = pl.ds(pl.multiple_of(i * tile, tile), tile)
                    last_ref[side, rows, columns] = held[at, side, lax.rem(code - 1, right_slots)]

        for side in range(2):
            totals[side][...] = jnp.zeros_like(totals[side])
            start, before = 0, None
            for (s, _), left_ref in zip(parts, refs):
                start = start if s == before else 0
                add_part(
                    codes_ref, s, side, start, slots, left_ref,
                    lambda found, s=s: held[z ^ s, side, found], right_slots, totals[side],
                )
                start, before = start + left_ref.shape[0], s

    return pl.pallas_call(
        kernel,
        out_shape=[jax.ShapeDtypeStruct((RT * tile, tile), jnp.float32)] * 2
        + [jax.ShapeDtypeStruct((2, slots * tile, RT * tile), jnp.bfloat16)],
        in_specs=[SMEM] + [VMEM] * (count + 2 * inner),
        out_specs=[VMEM] * 3,
        scratch_shapes=[pltpu.VMEM((inner, 2, right_slots, tile, tile), jnp.bfloat16)],
        compiler_params=pltpu.CompilerParams(vmem_limit_bytes=32 * 1024 * 1024),
        cost_estimate=pl.CostEstimate(
            flops=4 * inner * slots * tile**3, bytes_accessed=2 * inner * slots * tile**2, transcendentals=0
        ),
    )(codes, *[part for _, part in parts], *rights)


def last_products(parts, right, total, side, finish, out_shape):
    (left,) = parts
    slots, tile, _ = left.shape

    def kernel(left_ref, right_ref, total_ref, out_ref):
        added = jnp.zeros((tile, RT * tile), jnp.float32)
        for slot in range(0, slots, 2):
            both = min(2, slots - slot)
            tiles = [left_ref[slot + n] for n in range(both)]
            added += jnp.dot(
                jnp.concatenate(tiles, axis=1),
                right_ref[side, slot * tile : (slot + both) * tile, :],
                preferred_element_type=jnp.float32,
            )
        sums = [
            total_ref[i * tile : (i + 1) * tile, :] + added[:, i * tile : (i + 1) * tile] for i in range(RT)
        ]
        finish(sums, out_ref)

    return pl.pallas_call(
        kernel,
        out_shape=out_shape,
        in_specs=[VMEM] * 3,
        out_specs=VMEM,
        compiler_params=pltpu.CompilerParams(vmem_limit_bytes=16 * 1024 * 1024),
        cost_estimate=pl.CostEstimate(
            flops=2 * slots * tile**3, bytes_accessed=2 * slots * tile**2, transcendentals=0
        ),
    )(left, right, total)


def write_sum(sums, out_ref):
    out_ref[...] = jnp.concatenate(sums)


def write_coded(sums, out_ref):
    tile = out_ref.shape[1]
    exponents = jnp.zeros((PAD, tile), jnp.float32)
    for i, values in enumerate(sums):
        largest = jnp.max(jnp.abs(values), axis=0, keepdims=True)
        exponent = jnp.clip(jnp.floor(jnp.log2(largest)) + 1.0, -LEAST, LEAST)
        coded = jnp.round(values * jnp.exp2(BITS - exponent))
        coded = jnp.clip(coded, -(2.0**BITS) + 1.0, 2.0**BITS - 1.0)
        out_ref[i * tile : (i + 1) * tile, :] = coded.astype(jnp.int32).astype(jnp.int16)
        at = lax.broadcasted_iota(jnp.int32, (PAD, tile), 0)
        exponents = jnp.where(at == i, exponent, exponents)
    out_ref[RT * tile :, :] = exponents.astype(jnp.int32).astype(jnp.int16)


def add_coded(total, coded):
    def kernel(total_ref, coded_ref, out_ref):
        tile = total_ref.shape[1]
        exponents = coded_ref[RT * tile :, :].astype(jnp.int32).astype(jnp.float32)
        for i in range(RT):
            rows = slice(i * tile, (i + 1) * tile)
            scale = jnp.exp2(exponents[i : i + 1, :] - BITS)
            values = coded_ref[rows, :].astype(jnp.int32).astype(jnp.float32)
            out_ref[rows, :] = (total_ref[rows, :] + values * scale).astype(out_ref.dtype)

    return pl.pallas_call(
        kernel,
        out_shape=jax.ShapeDtypeStruct(total.shape, jnp.bfloat16),
        in_specs=[VMEM] * 2,
        out_specs=VMEM,
        compiler_params=pltpu.CompilerParams(vmem_limit_bytes=8 * 1024 * 1024),
    )(total, coded)


def across(block, axis, mask):
    route = [(i, i ^ mask) for i in range(lax.axis_size(axis))]
    return lax.ppermute(block, axis, route)


def crossed(block, mask):
    rows, cols = lax.axis_size("row"), lax.axis_size("col")
    route = [(r * cols + c, (r ^ mask) * cols + (c ^ 1)) for r in range(rows) for c in range(cols)]
    return lax.ppermute(block, ("row", "col"), route)


def gather(block, beside):
    places = lax.axis_size("col") // 2
    steps = [places >> n for n in range(1, places.bit_length() - 2)] + [3, 1]
    came = [across(block, "col", 2 * d) for d in steps]
    came, beside = lax.optimization_barrier((came, beside))
    blocks = {0: block, **dict(zip(steps, came))}
    spanned = [0]
    for d in steps:
        for s in spanned[1:]:
            blocks[s ^ d] = across(blocks[s], "col", 2 * d)
        spanned += [s ^ d for s in spanned]
    last = spanned[-1]
    order = [s for s in sorted(blocks) if s != last] + [last]
    return [(s, (blocks[s],)) for s in order], beside


def shards(left_tiles, left_index, right_tiles, right_index):
    y = lax.axis_index("col") & 1
    left = left_tiles[0, 0]
    right = right_tiles[0, 0]
    slots = left.shape[0]

    codes = find_matches(left_index, right_index)
    given = lax.dynamic_index_in_dim(right, 1 - y, 0, keepdims=False)
    own = lax.dynamic_index_in_dim(right, y, 0, keepdims=False)
    lefts, codes = gather(left, codes)
    rights = []
    for t in range(0, lax.axis_size("row"), 2):
        pair = [across(own, "row", t) if t else own, crossed(given, t)]
        if not t:
            pair[0], near = lax.optimization_barrier((pair[0], lefts[1][1]))
            lefts[1] = (1, near)
        rights += pair + [across(half, "row", 1) for half in pair]

    mine, other, right_last = first_products(codes, lefts[:-1], lefts[-1][0], rights, slots)
    last = (lefts[-1][1], right_last)
    rows, tile = mine.shape
    coded = last_products(
        *last, other, 1, write_coded, jax.ShapeDtypeStruct((rows + PAD, tile), jnp.int16)
    )
    coming = across(coded, "col", 1)
    mine = last_products(*last, mine, 0, write_sum, jax.ShapeDtypeStruct((rows, tile), jnp.float32))
    return add_coded(mine, coming)


def solution(mesh):
    return jax.shard_map(
        shards,
        mesh=mesh,
        in_specs=(
            P("row", "col", None, None, None),
            P(),
            P("row", "col", None, None, None, None),
            P(),
        ),
        out_specs=P("row", "col"),
        check_vma=False,
    )
```

```python
import jax
import jax.numpy as jnp
from jax import lax
from jax.experimental import pallas as pl
from jax.experimental.pallas import tpu as pltpu
from jax.sharding import PartitionSpec as P

KT = 8
RT = 2
BITS = 15
LEAST = 100
PAD = 16
SMEM = pl.BlockSpec(memory_space=pltpu.SMEM)
VMEM = pl.BlockSpec(memory_space=pltpu.VMEM)


def position():
    col = lax.axis_index("col")
    return lax.axis_index("row"), col >> 1, col & 1


def find_matches(left_index, right_index):
    slots = left_index.shape[-1]
    inner, _, _, right_slots = right_index.shape
    left_index = left_index.transpose(2, 0, 1)
    right_index = right_index.transpose(0, 3, 2, 1)

    def kernel(li_ref, ri_ref, codes_ref):
        row, z, y = position()

        @pl.loop(0, inner)
        def _(s):
            zp = z ^ s
            for side in range(2):
                column = 2 * z + (y if side == 0 else 1 - y)
                have = [ri_ref[zp, t, y, column] for t in range(right_slots)]
                for slot in range(slots):
                    at = li_ref[slot, row, 2 * zp + y]
                    k = lax.rem(at, KT)
                    first = 1 + lax.div(at, KT) * right_slots
                    code = jnp.int32(0)
                    for t in range(right_slots):
                        code = jnp.where(have[t] == k, first + t, code)
                    codes_ref[(s * 2 + side) * slots + slot] = jnp.where(at < RT * KT, code, 0)

    return pl.pallas_call(
        kernel,
        out_shape=jax.ShapeDtypeStruct((inner * 2 * slots,), jnp.int32),
        in_specs=[SMEM] * 2,
        out_specs=SMEM,
        compiler_params=pltpu.CompilerParams(vmem_limit_bytes=2 * 1024 * 1024),
    )(left_index, right_index)


def add_part(codes_ref, s, side, start, slots, left_ref, right_at, right_slots, total_ref):
    tile = total_ref.shape[1]

    @pl.loop(0, left_ref.shape[0])
    def _(slot):
        code = codes_ref[(s * 2 + side) * slots + start + slot]

        @pl.when(code > 0)
        def _():
            i = lax.div(code - 1, right_slots)
            rows = pl.ds(pl.multiple_of(i * tile, tile), tile)
            total_ref[rows, :] += jnp.dot(
                left_ref[slot],
                right_at(lax.rem(code - 1, right_slots)),
                preferred_element_type=jnp.float32,
            )


def first_products(codes, lefts, last, rights, slots):
    parts = [(s, part) for s, block in lefts for part in block]
    count = len(parts)
    inner = len(rights) // 2
    right_slots, tile, _ = rights[0].shape

    def kernel(codes_ref, *refs):
        right_refs = refs[count : count + 2 * inner]
        totals = refs[count + 2 * inner : count + 2 * inner + 2]
        last_ref, held = refs[count + 2 * inner + 2 :]
        row, z, _ = position()
        for t in range(inner):
            for side in range(2):
                held[row ^ t, side] = right_refs[2 * t + side][...]
        at = z ^ last
        last_ref[...] = jnp.zeros_like(last_ref)
        for side in range(2):

            @pl.loop(0, slots)
            def _(slot):
                code = codes_ref[(last * 2 + side) * slots + slot]

                @pl.when(code > 0)
                def _():
                    rows = pl.ds(pl.multiple_of(slot * tile, tile), tile)
                    i = lax.div(code - 1, right_slots)
                    columns = pl.ds(pl.multiple_of(i * tile, tile), tile)
                    last_ref[side, rows, columns] = held[at, side, lax.rem(code - 1, right_slots)]

        for side in range(2):
            totals[side][...] = jnp.zeros_like(totals[side])
            start, before = 0, None
            for (s, _), left_ref in zip(parts, refs):
                start = start if s == before else 0
                add_part(
                    codes_ref, s, side, start, slots, left_ref,
                    lambda found, s=s: held[z ^ s, side, found], right_slots, totals[side],
                )
                start, before = start + left_ref.shape[0], s

    return pl.pallas_call(
        kernel,
        out_shape=[jax.ShapeDtypeStruct((RT * tile, tile), jnp.float32)] * 2
        + [jax.ShapeDtypeStruct((2, slots * tile, RT * tile), jnp.bfloat16)],
        in_specs=[SMEM] + [VMEM] * (count + 2 * inner),
        out_specs=[VMEM] * 3,
        scratch_shapes=[pltpu.VMEM((inner, 2, right_slots, tile, tile), jnp.bfloat16)],
        compiler_params=pltpu.CompilerParams(vmem_limit_bytes=32 * 1024 * 1024),
        cost_estimate=pl.CostEstimate(
            flops=4 * inner * slots * tile**3, bytes_accessed=2 * inner * slots * tile**2, transcendentals=0
        ),
    )(codes, *[part for _, part in parts], *rights)


def last_products(parts, right, total, side, finish, out_shape):
    (left,) = parts
    slots, tile, _ = left.shape

    def kernel(left_ref, right_ref, total_ref, out_ref):
        added = jnp.zeros((tile, RT * tile), jnp.float32)
        for slot in range(0, slots, 2):
            both = min(2, slots - slot)
            tiles = [left_ref[slot + n] for n in range(both)]
            added += jnp.dot(
                jnp.concatenate(tiles, axis=1),
                right_ref[side, slot * tile : (slot + both) * tile, :],
                preferred_element_type=jnp.float32,
            )
        sums = [
            total_ref[i * tile : (i + 1) * tile, :] + added[:, i * tile : (i + 1) * tile] for i in range(RT)
        ]
        finish(sums, out_ref)

    return pl.pallas_call(
        kernel,
        out_shape=out_shape,
        in_specs=[VMEM] * 3,
        out_specs=VMEM,
        compiler_params=pltpu.CompilerParams(vmem_limit_bytes=16 * 1024 * 1024),
        cost_estimate=pl.CostEstimate(
            flops=2 * slots * tile**3, bytes_accessed=2 * slots * tile**2, transcendentals=0
        ),
    )(left, right, total)


def write_sum(sums, out_ref):
    out_ref[...] = jnp.concatenate(sums)


def write_coded(sums, out_ref):
    tile = out_ref.shape[1]
    exponents = jnp.zeros((PAD, tile), jnp.float32)
    for i, values in enumerate(sums):
        largest = jnp.max(jnp.abs(values), axis=0, keepdims=True)
        exponent = jnp.clip(jnp.floor(jnp.log2(largest)) + 1.0, -LEAST, LEAST)
        coded = jnp.round(values * jnp.exp2(BITS - exponent))
        coded = jnp.clip(coded, -(2.0**BITS) + 1.0, 2.0**BITS - 1.0)
        out_ref[i * tile : (i + 1) * tile, :] = coded.astype(jnp.int32).astype(jnp.int16)
        at = lax.broadcasted_iota(jnp.int32, (PAD, tile), 0)
        exponents = jnp.where(at == i, exponent, exponents)
    out_ref[RT * tile :, :] = exponents.astype(jnp.int32).astype(jnp.int16)


def add_coded(total, coded):
    def kernel(total_ref, coded_ref, out_ref):
        tile = total_ref.shape[1]
        exponents = coded_ref[RT * tile :, :].astype(jnp.int32).astype(jnp.float32)
        for i in range(RT):
            rows = slice(i * tile, (i + 1) * tile)
            scale = jnp.exp2(exponents[i : i + 1, :] - BITS)
            values = coded_ref[rows, :].astype(jnp.int32).astype(jnp.float32)
            out_ref[rows, :] = (total_ref[rows, :] + values * scale).astype(out_ref.dtype)

    return pl.pallas_call(
        kernel,
        out_shape=jax.ShapeDtypeStruct(total.shape, jnp.bfloat16),
        in_specs=[VMEM] * 2,
        out_specs=VMEM,
        compiler_params=pltpu.CompilerParams(vmem_limit_bytes=8 * 1024 * 1024),
    )(total, coded)


def across(block, axis, mask):
    route = [(i, i ^ mask) for i in range(lax.axis_size(axis))]
    return lax.ppermute(block, axis, route)


def crossed(block, mask):
    rows, cols = lax.axis_size("row"), lax.axis_size("col")
    route = [(r * cols + c, (r ^ mask) * cols + (c ^ 1)) for r in range(rows) for c in range(cols)]
    return lax.ppermute(block, ("row", "col"), route)


def gather(block, beside, ahead):
    places = lax.axis_size("col") // 2
    steps = [places >> n for n in range(1, places.bit_length() - 2)] + [3, 1]
    later, ahead = lax.optimization_barrier((block, ahead))
    came = [across(later if d == 1 else block, "col", 2 * d) for d in steps]
    came[:-1], beside = lax.optimization_barrier((came[:-1], beside))
    blocks = {0: block, **dict(zip(steps, came))}
    spanned = [0]
    for d in steps:
        for s in spanned[1:]:
            blocks[s ^ d] = across(blocks[s], "col", 2 * d)
        spanned += [s ^ d for s in spanned]
    last = spanned[-1]
    order = [s for s in sorted(blocks) if s != last] + [last]
    return [(s, (blocks[s],)) for s in order], beside, ahead


def shards(left_tiles, left_index, right_tiles, right_index):
    y = lax.axis_index("col") & 1
    left = left_tiles[0, 0]
    right = right_tiles[0, 0]
    slots = left.shape[0]

    codes = find_matches(left_index, right_index)
    given = lax.dynamic_index_in_dim(right, 1 - y, 0, keepdims=False)
    own = lax.dynamic_index_in_dim(right, y, 0, keepdims=False)
    lefts, codes, (own, given) = gather(left, codes, (own, given))
    rights = []
    for t in range(0, lax.axis_size("row"), 2):
        pair = [across(own, "row", t) if t else own, crossed(given, t)]
        if not t:
            pair[0], near = lax.optimization_barrier((pair[0], lefts[1][1]))
            lefts[1] = (1, near)
        rights += pair + [across(half, "row", 1) for half in pair]

    mine, other, right_last = first_products(codes, lefts[:-1], lefts[-1][0], rights, slots)
    last = (lefts[-1][1], right_last)
    rows, tile = mine.shape
    coded = last_products(
        *last, other, 1, write_coded, jax.ShapeDtypeStruct((rows + PAD, tile), jnp.int16)
    )
    coming = across(coded, "col", 1)
    mine = last_products(*last, mine, 0, write_sum, jax.ShapeDtypeStruct((rows, tile), jnp.float32))
    return add_coded(mine, coming)


def solution(mesh):
    return jax.shard_map(
        shards,
        mesh=mesh,
        in_specs=(
            P("row", "col", None, None, None),
            P(),
            P("row", "col", None, None, None, None),
            P(),
        ),
        out_specs=P("row", "col"),
        check_vma=False,
    )
```

```python
import jax
import jax.numpy as jnp
from jax import lax
from jax.experimental import pallas as pl
from jax.experimental.pallas import tpu as pltpu
from jax.sharding import PartitionSpec as P

KT = 8
RT = 2
BITS = 15
LEAST = 100
PAD = 16
SMEM = pl.BlockSpec(memory_space=pltpu.SMEM)
VMEM = pl.BlockSpec(memory_space=pltpu.VMEM)


def position():
    col = lax.axis_index("col")
    return lax.axis_index("row"), col >> 1, col & 1


def find_matches(left_index, right_index):
    slots = left_index.shape[-1]
    inner, _, _, right_slots = right_index.shape
    left_index = left_index.transpose(2, 0, 1)
    right_index = right_index.transpose(0, 3, 2, 1)

    def kernel(li_ref, ri_ref, codes_ref):
        row, z, y = position()

        @pl.loop(0, inner)
        def _(s):
            zp = z ^ s
            for side in range(2):
                column = 2 * z + (y if side == 0 else 1 - y)
                have = [ri_ref[zp, t, y, column] for t in range(right_slots)]
                for slot in range(slots):
                    at = li_ref[slot, row, 2 * zp + y]
                    k = lax.rem(at, KT)
                    first = 1 + lax.div(at, KT) * right_slots
                    code = jnp.int32(0)
                    for t in range(right_slots):
                        code = jnp.where(have[t] == k, first + t, code)
                    codes_ref[(s * 2 + side) * slots + slot] = jnp.where(at < RT * KT, code, 0)

    return pl.pallas_call(
        kernel,
        out_shape=jax.ShapeDtypeStruct((inner * 2 * slots,), jnp.int32),
        in_specs=[SMEM] * 2,
        out_specs=SMEM,
        compiler_params=pltpu.CompilerParams(vmem_limit_bytes=2 * 1024 * 1024),
    )(left_index, right_index)


def add_part(codes_ref, s, side, start, slots, left_ref, right_at, right_slots, total_ref):
    tile = total_ref.shape[1]

    @pl.loop(0, left_ref.shape[0], unroll=True)
    def _(slot):
        code = codes_ref[(s * 2 + side) * slots + start + slot]

        @pl.when(code > 0)
        def _():
            i = lax.div(code - 1, right_slots)
            rows = pl.ds(pl.multiple_of(i * tile, tile), tile)
            total_ref[rows, :] += jnp.dot(
                left_ref[slot],
                right_at(lax.rem(code - 1, right_slots)),
                preferred_element_type=jnp.float32,
            )


def first_products(codes, lefts, last, rights, slots):
    parts = [(s, part) for s, block in lefts for part in block]
    count = len(parts)
    inner = len(rights) // 2
    right_slots, tile, _ = rights[0].shape

    def kernel(codes_ref, *refs):
        right_refs = refs[count : count + 2 * inner]
        totals = refs[count + 2 * inner : count + 2 * inner + 2]
        last_ref, held = refs[count + 2 * inner + 2 :]
        row, z, _ = position()
        for t in range(inner):
            for side in range(2):
                held[row ^ t, side] = right_refs[2 * t + side][...]
        at = z ^ last
        last_ref[...] = jnp.zeros_like(last_ref)
        for side in range(2):

            @pl.loop(0, slots, unroll=True)
            def _(slot):
                code = codes_ref[(last * 2 + side) * slots + slot]

                @pl.when(code > 0)
                def _():
                    rows = pl.ds(pl.multiple_of(slot * tile, tile), tile)
                    i = lax.div(code - 1, right_slots)
                    columns = pl.ds(pl.multiple_of(i * tile, tile), tile)
                    last_ref[side, rows, columns] = held[at, side, lax.rem(code - 1, right_slots)]

        for side in range(2):
            totals[side][...] = jnp.zeros_like(totals[side])
            start, before = 0, None
            for (s, _), left_ref in zip(parts, refs):
                start = start if s == before else 0
                add_part(
                    codes_ref, s, side, start, slots, left_ref,
                    lambda found, s=s: held[z ^ s, side, found], right_slots, totals[side],
                )
                start, before = start + left_ref.shape[0], s

    return pl.pallas_call(
        kernel,
        out_shape=[jax.ShapeDtypeStruct((RT * tile, tile), jnp.float32)] * 2
        + [jax.ShapeDtypeStruct((2, slots * tile, RT * tile), jnp.bfloat16)],
        in_specs=[SMEM] + [VMEM] * (count + 2 * inner),
        out_specs=[VMEM] * 3,
        scratch_shapes=[pltpu.VMEM((inner, 2, right_slots, tile, tile), jnp.bfloat16)],
        compiler_params=pltpu.CompilerParams(vmem_limit_bytes=32 * 1024 * 1024),
        cost_estimate=pl.CostEstimate(
            flops=4 * inner * slots * tile**3, bytes_accessed=2 * inner * slots * tile**2, transcendentals=0
        ),
    )(codes, *[part for _, part in parts], *rights)


def last_products(parts, right, total, side, finish, out_shape):
    (left,) = parts
    slots, tile, _ = left.shape

    def kernel(left_ref, right_ref, total_ref, out_ref):
        added = jnp.zeros((tile, RT * tile), jnp.float32)
        for slot in range(0, slots, 2):
            both = min(2, slots - slot)
            tiles = [left_ref[slot + n] for n in range(both)]
            added += jnp.dot(
                jnp.concatenate(tiles, axis=1),
                right_ref[side, slot * tile : (slot + both) * tile, :],
                preferred_element_type=jnp.float32,
            )
        sums = [
            total_ref[i * tile : (i + 1) * tile, :] + added[:, i * tile : (i + 1) * tile] for i in range(RT)
        ]
        finish(sums, out_ref)

    return pl.pallas_call(
        kernel,
        out_shape=out_shape,
        in_specs=[VMEM] * 3,
        out_specs=VMEM,
        compiler_params=pltpu.CompilerParams(vmem_limit_bytes=16 * 1024 * 1024),
        cost_estimate=pl.CostEstimate(
            flops=2 * slots * tile**3, bytes_accessed=2 * slots * tile**2, transcendentals=0
        ),
    )(left, right, total)


def write_sum(sums, out_ref):
    out_ref[...] = jnp.concatenate(sums)


def write_coded(sums, out_ref):
    tile = out_ref.shape[1]
    exponents = jnp.zeros((PAD, tile), jnp.float32)
    for i, values in enumerate(sums):
        largest = jnp.max(jnp.abs(values), axis=0, keepdims=True)
        exponent = jnp.clip(jnp.floor(jnp.log2(largest)) + 1.0, -LEAST, LEAST)
        coded = jnp.round(values * jnp.exp2(BITS - exponent))
        coded = jnp.clip(coded, -(2.0**BITS) + 1.0, 2.0**BITS - 1.0)
        out_ref[i * tile : (i + 1) * tile, :] = coded.astype(jnp.int32).astype(jnp.int16)
        at = lax.broadcasted_iota(jnp.int32, (PAD, tile), 0)
        exponents = jnp.where(at == i, exponent, exponents)
    out_ref[RT * tile :, :] = exponents.astype(jnp.int32).astype(jnp.int16)


def add_coded(total, coded):
    def kernel(total_ref, coded_ref, out_ref):
        tile = total_ref.shape[1]
        exponents = coded_ref[RT * tile :, :].astype(jnp.int32).astype(jnp.float32)
        for i in range(RT):
            rows = slice(i * tile, (i + 1) * tile)
            scale = jnp.exp2(exponents[i : i + 1, :] - BITS)
            values = coded_ref[rows, :].astype(jnp.int32).astype(jnp.float32)
            out_ref[rows, :] = (total_ref[rows, :] + values * scale).astype(out_ref.dtype)

    return pl.pallas_call(
        kernel,
        out_shape=jax.ShapeDtypeStruct(total.shape, jnp.bfloat16),
        in_specs=[VMEM] * 2,
        out_specs=VMEM,
        compiler_params=pltpu.CompilerParams(vmem_limit_bytes=8 * 1024 * 1024),
    )(total, coded)


def across(block, axis, mask):
    route = [(i, i ^ mask) for i in range(lax.axis_size(axis))]
    return lax.ppermute(block, axis, route)


def crossed(block, mask):
    rows, cols = lax.axis_size("row"), lax.axis_size("col")
    route = [(r * cols + c, (r ^ mask) * cols + (c ^ 1)) for r in range(rows) for c in range(cols)]
    return lax.ppermute(block, ("row", "col"), route)


def gather(block, beside, place):
    places = lax.axis_size("col") // 2
    steps = [places >> n for n in range(1, places.bit_length() - 2)] + [3, 1]
    later, _ = lax.optimization_barrier((block, place))
    came = [across(later if d == 1 else block, "col", 2 * d) for d in steps]
    came[:-1], beside = lax.optimization_barrier((came[:-1], beside))
    blocks = {0: block, **dict(zip(steps, came))}
    spanned = [0]
    for d in steps:
        for s in spanned[1:]:
            blocks[s ^ d] = across(blocks[s], "col", 2 * d)
        spanned += [s ^ d for s in spanned]
    last = spanned[-1]
    order = [s for s in sorted(blocks) if s != last] + [last]
    return [(s, (blocks[s],)) for s in order], beside


def shards(left_tiles, left_index, right_tiles, right_index):
    y = lax.axis_index("col") & 1
    left = left_tiles[0, 0]
    right = right_tiles[0, 0]
    slots = left.shape[0]

    codes = find_matches(left_index, right_index)
    given = lax.dynamic_index_in_dim(right, 1 - y, 0, keepdims=False)
    own = lax.dynamic_index_in_dim(right, y, 0, keepdims=False)
    lefts, codes = gather(left, codes, y)
    rights = []
    for t in range(0, lax.axis_size("row"), 2):
        pair = [across(own, "row", t) if t else own, crossed(given, t)]
        if not t:
            pair[0], near = lax.optimization_barrier((pair[0], lefts[1][1]))
            lefts[1] = (1, near)
        rights += pair + [across(half, "row", 1) for half in pair]

    mine, other, right_last = first_products(codes, lefts[:-1], lefts[-1][0], rights, slots)
    last = (lefts[-1][1], right_last)
    rows, tile = mine.shape
    coded = last_products(
        *last, other, 1, write_coded, jax.ShapeDtypeStruct((rows + PAD, tile), jnp.int16)
    )
    coming = across(coded, "col", 1)
    mine = last_products(*last, mine, 0, write_sum, jax.ShapeDtypeStruct((rows, tile), jnp.float32))
    return add_coded(mine, coming)


def solution(mesh):
    return jax.shard_map(
        shards,
        mesh=mesh,
        in_specs=(
            P("row", "col", None, None, None),
            P(),
            P("row", "col", None, None, None, None),
            P(),
        ),
        out_specs=P("row", "col"),
        check_vma=False,
    )
```

```python
import jax
import jax.numpy as jnp
from jax import lax
from jax.experimental import pallas as pl
from jax.experimental.pallas import tpu as pltpu
from jax.sharding import PartitionSpec as P

KT = 8
RT = 2
BITS = 15
LEAST = 100
PAD = 16
SMEM = pl.BlockSpec(memory_space=pltpu.SMEM)
VMEM = pl.BlockSpec(memory_space=pltpu.VMEM)


def position():
    col = lax.axis_index("col")
    return lax.axis_index("row"), col >> 1, col & 1


def find_matches(left_index, right_index):
    slots = left_index.shape[-1]
    inner, _, _, right_slots = right_index.shape
    left_index = left_index.transpose(2, 0, 1)
    right_index = right_index.transpose(0, 3, 2, 1)

    def kernel(li_ref, ri_ref, codes_ref):
        row, z, y = position()

        @pl.loop(0, inner)
        def _(s):
            zp = z ^ s
            for side in range(2):
                column = 2 * z + (y if side == 0 else 1 - y)
                have = [ri_ref[zp, t, y, column] for t in range(right_slots)]
                for slot in range(slots):
                    at = li_ref[slot, row, 2 * zp + y]
                    k = lax.rem(at, KT)
                    first = 1 + lax.div(at, KT) * right_slots
                    code = jnp.int32(0)
                    for t in range(right_slots):
                        code = jnp.where(have[t] == k, first + t, code)
                    codes_ref[(s * 2 + side) * slots + slot] = jnp.where(at < RT * KT, code, 0)

    return pl.pallas_call(
        kernel,
        out_shape=jax.ShapeDtypeStruct((inner * 2 * slots,), jnp.int32),
        in_specs=[SMEM] * 2,
        out_specs=SMEM,
        compiler_params=pltpu.CompilerParams(vmem_limit_bytes=2 * 1024 * 1024),
    )(left_index, right_index)


def add_part(codes_ref, s, side, start, slots, left_ref, right_at, right_slots, total_ref):
    tile = total_ref.shape[1]

    @pl.loop(0, left_ref.shape[0], unroll=True)
    def _(slot):
        code = codes_ref[(s * 2 + side) * slots + start + slot]

        @pl.when(code > 0)
        def _():
            i = lax.div(code - 1, right_slots)
            rows = pl.ds(pl.multiple_of(i * tile, tile), tile)
            total_ref[rows, :] += jnp.dot(
                left_ref[slot],
                right_at(lax.rem(code - 1, right_slots)),
                preferred_element_type=jnp.float32,
            )


def first_products(codes, lefts, last, rights, slots):
    parts = [(s, part) for s, block in lefts for part in block]
    count = len(parts)
    inner = len(rights) // 2
    right_slots, tile, _ = rights[0].shape

    def kernel(codes_ref, *refs):
        right_refs = refs[count : count + 2 * inner]
        totals = refs[count + 2 * inner : count + 2 * inner + 2]
        last_ref, held = refs[count + 2 * inner + 2 :]
        row, z, _ = position()
        for t in range(inner):
            for side in range(2):
                held[row ^ t, side] = right_refs[2 * t + side][...]
        at = z ^ last
        last_ref[...] = jnp.zeros_like(last_ref)
        for side in range(2):

            @pl.loop(0, slots, unroll=True)
            def _(slot):
                code = codes_ref[(last * 2 + side) * slots + slot]

                @pl.when(code > 0)
                def _():
                    rows = pl.ds(pl.multiple_of(slot * tile, tile), tile)
                    i = lax.div(code - 1, right_slots)
                    columns = pl.ds(pl.multiple_of(i * tile, tile), tile)
                    last_ref[side, rows, columns] = held[at, side, lax.rem(code - 1, right_slots)]

        for side in range(2):
            totals[side][...] = jnp.zeros_like(totals[side])
            start, before = 0, None
            for (s, _), left_ref in zip(parts, refs):
                start = start if s == before else 0
                add_part(
                    codes_ref, s, side, start, slots, left_ref,
                    lambda found, s=s: held[z ^ s, side, found], right_slots, totals[side],
                )
                start, before = start + left_ref.shape[0], s

    return pl.pallas_call(
        kernel,
        out_shape=[jax.ShapeDtypeStruct((RT * tile, tile), jnp.float32)] * 2
        + [jax.ShapeDtypeStruct((2, slots * tile, RT * tile), jnp.bfloat16)],
        in_specs=[SMEM] + [VMEM] * (count + 2 * inner),
        out_specs=[VMEM] * 3,
        scratch_shapes=[pltpu.VMEM((inner, 2, right_slots, tile, tile), jnp.bfloat16)],
        compiler_params=pltpu.CompilerParams(vmem_limit_bytes=32 * 1024 * 1024),
        cost_estimate=pl.CostEstimate(
            flops=4 * inner * slots * tile**3, bytes_accessed=2 * inner * slots * tile**2, transcendentals=0
        ),
    )(codes, *[part for _, part in parts], *rights)


def last_products(parts, right, total, side, finish, out_shape):
    (left,) = parts
    slots, tile, _ = left.shape

    def kernel(left_ref, right_ref, total_ref, out_ref):
        added = jnp.zeros((tile, RT * tile), jnp.float32)
        for slot in range(0, slots, 2):
            both = min(2, slots - slot)
            tiles = [left_ref[slot + n] for n in range(both)]
            added += jnp.dot(
                jnp.concatenate(tiles, axis=1),
                right_ref[side, slot * tile : (slot + both) * tile, :],
                preferred_element_type=jnp.float32,
            )
        sums = [
            total_ref[i * tile : (i + 1) * tile, :] + added[:, i * tile : (i + 1) * tile] for i in range(RT)
        ]
        finish(sums, out_ref)

    return pl.pallas_call(
        kernel,
        out_shape=out_shape,
        in_specs=[VMEM] * 3,
        out_specs=VMEM,
        compiler_params=pltpu.CompilerParams(vmem_limit_bytes=16 * 1024 * 1024),
        cost_estimate=pl.CostEstimate(
            flops=2 * slots * tile**3, bytes_accessed=2 * slots * tile**2, transcendentals=0
        ),
    )(left, right, total)


def write_sum(sums, out_ref):
    out_ref[...] = jnp.concatenate(sums)


def write_coded(sums, out_ref):
    tile = out_ref.shape[1]
    exponents = jnp.zeros((PAD, tile), jnp.float32)
    for i, values in enumerate(sums):
        largest = jnp.max(jnp.abs(values), axis=0, keepdims=True)
        exponent = jnp.clip(jnp.floor(jnp.log2(largest)) + 1.0, -LEAST, LEAST)
        coded = jnp.round(values * jnp.exp2(BITS - exponent))
        coded = jnp.clip(coded, -(2.0**BITS) + 1.0, 2.0**BITS - 1.0)
        out_ref[i * tile : (i + 1) * tile, :] = coded.astype(jnp.int32).astype(jnp.int16)
        at = lax.broadcasted_iota(jnp.int32, (PAD, tile), 0)
        exponents = jnp.where(at == i, exponent, exponents)
    out_ref[RT * tile :, :] = exponents.astype(jnp.int32).astype(jnp.int16)


def add_coded(total, coded):
    def kernel(total_ref, coded_ref, out_ref, sums, done):
        tile = total_ref.shape[1]
        exponents = coded_ref[RT * tile :, :].astype(jnp.int32).astype(jnp.float32)
        copies = []
        for i in range(RT):
            rows = slice(i * tile, (i + 1) * tile)
            scale = jnp.exp2(exponents[i : i + 1, :] - BITS)
            values = coded_ref[rows, :].astype(jnp.int32).astype(jnp.float32)
            sums[i] = (total_ref[rows, :] + values * scale).astype(sums.dtype)
            copy = pltpu.make_async_copy(sums.at[i], out_ref.at[pl.ds(i * tile, tile)], done.at[i])
            copy.start()
            copies.append(copy)
        for copy in copies:
            copy.wait()

    return pl.pallas_call(
        kernel,
        out_shape=jax.ShapeDtypeStruct(total.shape, jnp.bfloat16),
        in_specs=[VMEM] * 2,
        out_specs=pl.BlockSpec(memory_space=pl.ANY),
        scratch_shapes=[
            pltpu.VMEM((RT, total.shape[0] // RT, total.shape[1]), jnp.bfloat16),
            pltpu.SemaphoreType.DMA((RT,)),
        ],
        compiler_params=pltpu.CompilerParams(vmem_limit_bytes=8 * 1024 * 1024),
    )(total, coded)


def across(block, axis, mask):
    route = [(i, i ^ mask) for i in range(lax.axis_size(axis))]
    return lax.ppermute(block, axis, route)


def crossed(block, mask):
    rows, cols = lax.axis_size("row"), lax.axis_size("col")
    route = [(r * cols + c, (r ^ mask) * cols + (c ^ 1)) for r in range(rows) for c in range(cols)]
    return lax.ppermute(block, ("row", "col"), route)


def gather(block, beside, place):
    places = lax.axis_size("col") // 2
    steps = [places >> n for n in range(1, places.bit_length() - 2)] + [3, 1]
    later, _ = lax.optimization_barrier((block, place))
    came = [across(later if d == 1 else block, "col", 2 * d) for d in steps]
    came[:-1], beside = lax.optimization_barrier((came[:-1], beside))
    blocks = {0: block, **dict(zip(steps, came))}
    spanned = [0]
    for d in steps:
        for s in spanned[1:]:
            blocks[s ^ d] = across(blocks[s], "col", 2 * d)
        spanned += [s ^ d for s in spanned]
    last = spanned[-1]
    order = [s for s in sorted(blocks) if s != last] + [last]
    return [(s, (blocks[s],)) for s in order], beside


def shards(left_tiles, left_index, right_tiles, right_index):
    y = lax.axis_index("col") & 1
    left = left_tiles[0, 0]
    right = right_tiles[0, 0]
    slots = left.shape[0]

    codes = find_matches(left_index, right_index)
    given = lax.dynamic_index_in_dim(right, 1 - y, 0, keepdims=False)
    own = lax.dynamic_index_in_dim(right, y, 0, keepdims=False)
    lefts, codes = gather(left, codes, y)
    rights = []
    for t in range(0, lax.axis_size("row"), 2):
        pair = [across(own, "row", t) if t else own, crossed(given, t)]
        if not t:
            pair[0], near = lax.optimization_barrier((pair[0], lefts[1][1]))
            lefts[1] = (1, near)
        rights += pair + [across(half, "row", 1) for half in pair]

    mine, other, right_last = first_products(codes, lefts[:-1], lefts[-1][0], rights, slots)
    last = (lefts[-1][1], right_last)
    rows, tile = mine.shape
    coded = last_products(
        *last, other, 1, write_coded, jax.ShapeDtypeStruct((rows + PAD, tile), jnp.int16)
    )
    coming = across(coded, "col", 1)
    mine = last_products(*last, mine, 0, write_sum, jax.ShapeDtypeStruct((rows, tile), jnp.float32))
    return add_coded(mine, coming)


def solution(mesh):
    return jax.shard_map(
        shards,
        mesh=mesh,
        in_specs=(
            P("row", "col", None, None, None),
            P(),
            P("row", "col", None, None, None, None),
            P(),
        ),
        out_specs=P("row", "col"),
        check_vma=False,
    )
```

```python
import jax
import jax.numpy as jnp
from jax import lax
from jax.experimental import pallas as pl
from jax.experimental.pallas import tpu as pltpu
from jax.sharding import PartitionSpec as P

KT = 8
RT = 2
BITS = 15
LEAST = 100
PAD = 16
SMEM = pl.BlockSpec(memory_space=pltpu.SMEM)
VMEM = pl.BlockSpec(memory_space=pltpu.VMEM)


def position():
    col = lax.axis_index("col")
    return lax.axis_index("row"), col >> 1, col & 1


def find_matches(left_index, right_index):
    slots = left_index.shape[-1]
    inner, _, _, right_slots = right_index.shape
    left_index = left_index.transpose(2, 0, 1)
    right_index = right_index.transpose(0, 3, 2, 1)

    def kernel(li_ref, ri_ref, codes_ref):
        row, z, y = position()

        @pl.loop(0, inner)
        def _(s):
            zp = z ^ s
            for side in range(2):
                column = 2 * z + (y if side == 0 else 1 - y)
                have = [ri_ref[zp, t, y, column] for t in range(right_slots)]
                for slot in range(slots):
                    at = li_ref[slot, row, 2 * zp + y]
                    k = lax.rem(at, KT)
                    first = 1 + lax.div(at, KT) * right_slots
                    code = jnp.int32(0)
                    for t in range(right_slots):
                        code = jnp.where(have[t] == k, first + t, code)
                    codes_ref[(s * 2 + side) * slots + slot] = jnp.where(at < RT * KT, code, 0)

    return pl.pallas_call(
        kernel,
        out_shape=jax.ShapeDtypeStruct((inner * 2 * slots,), jnp.int32),
        in_specs=[SMEM] * 2,
        out_specs=SMEM,
        compiler_params=pltpu.CompilerParams(vmem_limit_bytes=2 * 1024 * 1024),
    )(left_index, right_index)


def add_part(codes_ref, s, side, start, slots, left_ref, right_at, right_slots, total_ref):
    tile = total_ref.shape[1]

    @pl.loop(0, left_ref.shape[0], unroll=True)
    def _(slot):
        code = codes_ref[(s * 2 + side) * slots + start + slot]

        @pl.when(code > 0)
        def _():
            i = lax.div(code - 1, right_slots)
            rows = pl.ds(pl.multiple_of(i * tile, tile), tile)
            total_ref[rows, :] += jnp.dot(
                left_ref[slot],
                right_at(lax.rem(code - 1, right_slots)),
                preferred_element_type=jnp.float32,
            )


def first_products(codes, lefts, last, rights, slots):
    parts = [(s, part) for s, block in lefts for part in block]
    count = len(parts)
    inner = len(rights) // 2
    right_slots, tile, _ = rights[0].shape

    def kernel(codes_ref, *refs):
        right_refs = refs[count : count + 2 * inner]
        totals = refs[count + 2 * inner : count + 2 * inner + 2]
        last_ref, held = refs[count + 2 * inner + 2 :]
        row, z, _ = position()
        for t in range(inner):
            for side in range(2):
                held[row ^ t, side] = right_refs[2 * t + side][...]
        at = z ^ last
        last_ref[...] = jnp.zeros_like(last_ref)
        for side in range(2):

            @pl.loop(0, slots, unroll=True)
            def _(slot):
                code = codes_ref[(last * 2 + side) * slots + slot]

                @pl.when(code > 0)
                def _():
                    rows = pl.ds(pl.multiple_of(slot * tile, tile), tile)
                    i = lax.div(code - 1, right_slots)
                    columns = pl.ds(pl.multiple_of(i * tile, tile), tile)
                    last_ref[side, rows, columns] = held[at, side, lax.rem(code - 1, right_slots)]

        for side in range(2):
            totals[side][...] = jnp.zeros_like(totals[side])
            start, before = 0, None
            for (s, _), left_ref in zip(parts, refs):
                start = start if s == before else 0
                add_part(
                    codes_ref, s, side, start, slots, left_ref,
                    lambda found, s=s: held[z ^ s, side, found], right_slots, totals[side],
                )
                start, before = start + left_ref.shape[0], s

    return pl.pallas_call(
        kernel,
        out_shape=[jax.ShapeDtypeStruct((RT * tile, tile), jnp.float32)] * 2
        + [jax.ShapeDtypeStruct((2, slots * tile, RT * tile), jnp.bfloat16)],
        in_specs=[SMEM] + [VMEM] * (count + 2 * inner),
        out_specs=[VMEM] * 3,
        scratch_shapes=[pltpu.VMEM((inner, 2, right_slots, tile, tile), jnp.bfloat16)],
        compiler_params=pltpu.CompilerParams(vmem_limit_bytes=32 * 1024 * 1024),
        cost_estimate=pl.CostEstimate(
            flops=4 * inner * slots * tile**3, bytes_accessed=2 * inner * slots * tile**2, transcendentals=0
        ),
    )(codes, *[part for _, part in parts], *rights)


def last_products(parts, right, total, side, finish, out_shape):
    (left,) = parts
    slots, tile, _ = left.shape

    def kernel(left_ref, right_ref, total_ref, out_ref):
        added = jnp.zeros((tile, RT * tile), jnp.float32)
        for slot in range(0, slots, 2):
            both = min(2, slots - slot)
            tiles = [left_ref[slot + n] for n in range(both)]
            added += jnp.dot(
                jnp.concatenate(tiles, axis=1),
                right_ref[side, slot * tile : (slot + both) * tile, :],
                preferred_element_type=jnp.float32,
            )
        sums = [
            total_ref[i * tile : (i + 1) * tile, :] + added[:, i * tile : (i + 1) * tile] for i in range(RT)
        ]
        finish(sums, out_ref)

    return pl.pallas_call(
        kernel,
        out_shape=out_shape,
        in_specs=[VMEM] * 3,
        out_specs=VMEM,
        compiler_params=pltpu.CompilerParams(vmem_limit_bytes=16 * 1024 * 1024),
        cost_estimate=pl.CostEstimate(
            flops=2 * slots * tile**3, bytes_accessed=2 * slots * tile**2, transcendentals=0
        ),
    )(left, right, total)


def write_sum(sums, out_ref):
    out_ref[...] = jnp.concatenate(sums)


def write_coded(sums, out_ref):
    tile = out_ref.shape[1]
    exponents = jnp.zeros((PAD, tile), jnp.float32)
    for i, values in enumerate(sums):
        largest = jnp.max(jnp.abs(values), axis=0, keepdims=True)
        exponent = jnp.clip(jnp.floor(jnp.log2(largest)) + 1.0, -LEAST, LEAST)
        coded = jnp.round(values * jnp.exp2(BITS - exponent))
        coded = jnp.clip(coded, -(2.0**BITS) + 1.0, 2.0**BITS - 1.0)
        out_ref[i * tile : (i + 1) * tile, :] = coded.astype(jnp.int32).astype(jnp.int16)
        at = lax.broadcasted_iota(jnp.int32, (PAD, tile), 0)
        exponents = jnp.where(at == i, exponent, exponents)
    out_ref[RT * tile :, :] = exponents.astype(jnp.int32).astype(jnp.int16)


def add_coded(total, coded):
    def kernel(total_ref, coded_ref, out_ref):
        tile = total_ref.shape[1]
        exponents = coded_ref[RT * tile :, :].astype(jnp.int32).astype(jnp.float32)
        for i in range(RT):
            rows = slice(i * tile, (i + 1) * tile)
            scale = jnp.exp2(exponents[i : i + 1, :] - BITS)
            values = coded_ref[rows, :].astype(jnp.int32).astype(jnp.float32)
            out_ref[rows, :] = (total_ref[rows, :] + values * scale).astype(out_ref.dtype)

    return pl.pallas_call(
        kernel,
        out_shape=jax.ShapeDtypeStruct(total.shape, jnp.bfloat16),
        in_specs=[VMEM] * 2,
        out_specs=VMEM,
        compiler_params=pltpu.CompilerParams(vmem_limit_bytes=8 * 1024 * 1024),
    )(total, coded)


def across(block, axis, mask):
    route = [(i, i ^ mask) for i in range(lax.axis_size(axis))]
    return lax.ppermute(block, axis, route)


def crossed(block, mask):
    rows, cols = lax.axis_size("row"), lax.axis_size("col")
    route = [(r * cols + c, (r ^ mask) * cols + (c ^ 1)) for r in range(rows) for c in range(cols)]
    return lax.ppermute(block, ("row", "col"), route)


def gather(block, beside, place):
    places = lax.axis_size("col") // 2
    steps = [places >> n for n in range(1, places.bit_length() - 2)] + [3, 1]
    later, _ = lax.optimization_barrier((block, place))
    came = [across(later if d == 1 else block, "col", 2 * d) for d in steps]
    came[:-1], beside = lax.optimization_barrier((came[:-1], beside))
    blocks = {0: block, **dict(zip(steps, came))}
    spanned = [0]
    for d in steps:
        for s in spanned[1:]:
            blocks[s ^ d] = across(blocks[s], "col", 2 * d)
        spanned += [s ^ d for s in spanned]
    last = spanned[-1]
    order = [s for s in sorted(blocks) if s != last] + [last]
    return [(s, (blocks[s],)) for s in order], beside


def shards(left_tiles, left_index, right_tiles, right_index):
    y = lax.axis_index("col") & 1
    left = left_tiles[0, 0]
    right = right_tiles[0, 0]
    slots = left.shape[0]

    codes = find_matches(left_index, right_index)
    given = lax.dynamic_index_in_dim(right, 1 - y, 0, keepdims=False)
    own = lax.dynamic_index_in_dim(right, y, 0, keepdims=False)
    lefts, codes = gather(left, codes, y)
    rights = []
    for t in range(0, lax.axis_size("row"), 2):
        if t:
            given, rights[1] = lax.optimization_barrier((given, rights[1]))
        pair = [across(own, "row", t) if t else own, crossed(given, t)]
        if not t:
            pair[0], near = lax.optimization_barrier((pair[0], lefts[1][1]))
            lefts[1] = (1, near)
        rights += pair + [across(half, "row", 1) for half in pair]

    mine, other, right_last = first_products(codes, lefts[:-1], lefts[-1][0], rights, slots)
    last = (lefts[-1][1], right_last)
    rows, tile = mine.shape
    coded = last_products(
        *last, other, 1, write_coded, jax.ShapeDtypeStruct((rows + PAD, tile), jnp.int16)
    )
    coming = across(coded, "col", 1)
    mine = last_products(*last, mine, 0, write_sum, jax.ShapeDtypeStruct((rows, tile), jnp.float32))
    return add_coded(mine, coming)


def solution(mesh):
    return jax.shard_map(
        shards,
        mesh=mesh,
        in_specs=(
            P("row", "col", None, None, None),
            P(),
            P("row", "col", None, None, None, None),
            P(),
        ),
        out_specs=P("row", "col"),
        check_vma=False,
    )
```

```python
import jax
import jax.numpy as jnp
from jax import lax
from jax.experimental import pallas as pl
from jax.experimental.pallas import tpu as pltpu
from jax.sharding import PartitionSpec as P

KT = 8
RT = 2
BITS = 15
LEAST = 100
PAD = 16
SMEM = pl.BlockSpec(memory_space=pltpu.SMEM)
VMEM = pl.BlockSpec(memory_space=pltpu.VMEM)


def position():
    col = lax.axis_index("col")
    return lax.axis_index("row"), col >> 1, col & 1


def find_matches(left_index, right_index):
    slots = left_index.shape[-1]
    inner, _, _, right_slots = right_index.shape
    left_index = left_index.transpose(2, 0, 1)
    right_index = right_index.transpose(0, 3, 2, 1)

    def kernel(li_ref, ri_ref, codes_ref):
        row, z, y = position()

        @pl.loop(0, inner)
        def _(s):
            zp = z ^ s
            for side in range(2):
                column = 2 * z + (y if side == 0 else 1 - y)
                have = [ri_ref[zp, t, y, column] for t in range(right_slots)]
                for slot in range(slots):
                    at = li_ref[slot, row, 2 * zp + y]
                    k = lax.rem(at, KT)
                    first = 1 + lax.div(at, KT) * right_slots
                    code = jnp.int32(0)
                    for t in range(right_slots):
                        code = jnp.where(have[t] == k, first + t, code)
                    codes_ref[(s * 2 + side) * slots + slot] = jnp.where(at < RT * KT, code, 0)

    return pl.pallas_call(
        kernel,
        out_shape=jax.ShapeDtypeStruct((inner * 2 * slots,), jnp.int32),
        in_specs=[SMEM] * 2,
        out_specs=SMEM,
        compiler_params=pltpu.CompilerParams(vmem_limit_bytes=2 * 1024 * 1024),
    )(left_index, right_index)


def add_part(codes_ref, s, side, start, slots, left_ref, right_at, right_slots, total_ref):
    tile = total_ref.shape[1]

    @pl.loop(0, left_ref.shape[0], unroll=True)
    def _(slot):
        code = codes_ref[(s * 2 + side) * slots + start + slot]

        @pl.when(code > 0)
        def _():
            i = lax.div(code - 1, right_slots)
            rows = pl.ds(pl.multiple_of(i * tile, tile), tile)
            total_ref[rows, :] += jnp.dot(
                left_ref[slot],
                right_at(lax.rem(code - 1, right_slots)),
                preferred_element_type=jnp.float32,
            )


def first_products(codes, lefts, last, rights, slots):
    parts = [(s, part) for s, block in lefts for part in block]
    count = len(parts)
    inner = len(rights) // 2
    right_slots, tile, _ = rights[0].shape

    def kernel(codes_ref, *refs):
        right_refs = refs[count : count + 2 * inner]
        totals = refs[count + 2 * inner : count + 2 * inner + 2]
        last_ref, held = refs[count + 2 * inner + 2 :]
        row, z, _ = position()
        for t in range(inner):
            for side in range(2):
                held[row ^ t, side] = right_refs[2 * t + side][...]
        at = z ^ last
        last_ref[...] = jnp.zeros_like(last_ref)
        for side in range(2):

            @pl.loop(0, slots)
            def _(slot):
                code = codes_ref[(last * 2 + side) * slots + slot]

                @pl.when(code > 0)
                def _():
                    rows = pl.ds(pl.multiple_of(slot * tile, tile), tile)
                    i = lax.div(code - 1, right_slots)
                    columns = pl.ds(pl.multiple_of(i * tile, tile), tile)
                    last_ref[side, rows, columns] = held[at, side, lax.rem(code - 1, right_slots)]

        for side in range(2):
            totals[side][...] = jnp.zeros_like(totals[side])
            start, before = 0, None
            for (s, _), left_ref in zip(parts, refs):
                start = start if s == before else 0
                add_part(
                    codes_ref, s, side, start, slots, left_ref,
                    lambda found, s=s: held[z ^ s, side, found], right_slots, totals[side],
                )
                start, before = start + left_ref.shape[0], s

    return pl.pallas_call(
        kernel,
        out_shape=[jax.ShapeDtypeStruct((RT * tile, tile), jnp.float32)] * 2
        + [jax.ShapeDtypeStruct((2, slots * tile, RT * tile), jnp.bfloat16)],
        in_specs=[SMEM] + [VMEM] * (count + 2 * inner),
        out_specs=[VMEM] * 3,
        scratch_shapes=[pltpu.VMEM((inner, 2, right_slots, tile, tile), jnp.bfloat16)],
        compiler_params=pltpu.CompilerParams(vmem_limit_bytes=32 * 1024 * 1024),
        cost_estimate=pl.CostEstimate(
            flops=4 * inner * slots * tile**3, bytes_accessed=2 * inner * slots * tile**2, transcendentals=0
        ),
    )(codes, *[part for _, part in parts], *rights)


def last_products(parts, right, total, side, finish, out_shape):
    (left,) = parts
    slots, tile, _ = left.shape

    def kernel(left_ref, right_ref, total_ref, out_ref):
        added = jnp.zeros((tile, RT * tile), jnp.float32)
        for slot in range(0, slots, 2):
            both = min(2, slots - slot)
            tiles = [left_ref[slot + n] for n in range(both)]
            added += jnp.dot(
                jnp.concatenate(tiles, axis=1),
                right_ref[side, slot * tile : (slot + both) * tile, :],
                preferred_element_type=jnp.float32,
            )
        sums = [
            total_ref[i * tile : (i + 1) * tile, :] + added[:, i * tile : (i + 1) * tile] for i in range(RT)
        ]
        finish(sums, out_ref)

    return pl.pallas_call(
        kernel,
        out_shape=out_shape,
        in_specs=[VMEM] * 3,
        out_specs=VMEM,
        compiler_params=pltpu.CompilerParams(vmem_limit_bytes=16 * 1024 * 1024),
        cost_estimate=pl.CostEstimate(
            flops=2 * slots * tile**3, bytes_accessed=2 * slots * tile**2, transcendentals=0
        ),
    )(left, right, total)


def write_sum(sums, out_ref):
    out_ref[...] = jnp.concatenate(sums)


def write_coded(sums, out_ref):
    tile = out_ref.shape[1]
    exponents = jnp.zeros((PAD, tile), jnp.float32)
    for i, values in enumerate(sums):
        largest = jnp.max(jnp.abs(values), axis=0, keepdims=True)
        exponent = jnp.clip(jnp.floor(jnp.log2(largest)) + 1.0, -LEAST, LEAST)
        coded = jnp.round(values * jnp.exp2(BITS - exponent))
        coded = jnp.clip(coded, -(2.0**BITS) + 1.0, 2.0**BITS - 1.0)
        out_ref[i * tile : (i + 1) * tile, :] = coded.astype(jnp.int32).astype(jnp.int16)
        at = lax.broadcasted_iota(jnp.int32, (PAD, tile), 0)
        exponents = jnp.where(at == i, exponent, exponents)
    out_ref[RT * tile :, :] = exponents.astype(jnp.int32).astype(jnp.int16)


def add_coded(total, coded):
    def kernel(total_ref, coded_ref, out_ref):
        tile = total_ref.shape[1]
        exponents = coded_ref[RT * tile :, :].astype(jnp.int32).astype(jnp.float32)
        for i in range(RT):
            rows = slice(i * tile, (i + 1) * tile)
            scale = jnp.exp2(exponents[i : i + 1, :] - BITS)
            values = coded_ref[rows, :].astype(jnp.int32).astype(jnp.float32)
            out_ref[rows, :] = (total_ref[rows, :] + values * scale).astype(out_ref.dtype)

    return pl.pallas_call(
        kernel,
        out_shape=jax.ShapeDtypeStruct(total.shape, jnp.bfloat16),
        in_specs=[VMEM] * 2,
        out_specs=VMEM,
        compiler_params=pltpu.CompilerParams(vmem_limit_bytes=8 * 1024 * 1024),
    )(total, coded)


def across(block, axis, mask):
    route = [(i, i ^ mask) for i in range(lax.axis_size(axis))]
    return lax.ppermute(block, axis, route)


def crossed(block, mask):
    rows, cols = lax.axis_size("row"), lax.axis_size("col")
    route = [(r * cols + c, (r ^ mask) * cols + (c ^ 1)) for r in range(rows) for c in range(cols)]
    return lax.ppermute(block, ("row", "col"), route)


def gather(block, beside, ahead):
    places = lax.axis_size("col") // 2
    steps = [places >> n for n in range(1, places.bit_length() - 2)] + [3, 1]
    later, ahead = lax.optimization_barrier((block, ahead))
    came = [across(later if d == 1 else block, "col", 2 * d) for d in steps]
    came[:-1], beside = lax.optimization_barrier((came[:-1], beside))
    blocks = {0: block, **dict(zip(steps, came))}
    spanned = [0]
    for d in steps:
        for s in spanned[1:]:
            blocks[s ^ d] = across(blocks[s], "col", 2 * d)
        spanned += [s ^ d for s in spanned]
    last = spanned[-1]
    order = [s for s in sorted(blocks) if s != last] + [last]
    return [(s, (blocks[s],)) for s in order], beside, ahead


def shards(left_tiles, left_index, right_tiles, right_index):
    y = lax.axis_index("col") & 1
    left = left_tiles[0, 0]
    right = right_tiles[0, 0]
    slots = left.shape[0]

    codes = find_matches(left_index, right_index)
    given = lax.dynamic_index_in_dim(right, 1 - y, 0, keepdims=False)
    own = lax.dynamic_index_in_dim(right, y, 0, keepdims=False)
    lefts, codes, (own, given) = gather(left, codes, (own, given))
    rights = []
    for t in range(0, lax.axis_size("row"), 2):
        pair = [across(own, "row", t) if t else own, crossed(given, t)]
        if not t:
            pair[0], near = lax.optimization_barrier((pair[0], lefts[1][1]))
            lefts[1] = (1, near)
        rights += pair + [across(half, "row", 1) for half in pair]

    mine, other, right_last = first_products(codes, lefts[:-1], lefts[-1][0], rights, slots)
    last = (lefts[-1][1], right_last)
    rows, tile = mine.shape
    coded = last_products(
        *last, other, 1, write_coded, jax.ShapeDtypeStruct((rows + PAD, tile), jnp.int16)
    )
    coming = across(coded, "col", 1)
    mine = last_products(*last, mine, 0, write_sum, jax.ShapeDtypeStruct((rows, tile), jnp.float32))
    return add_coded(mine, coming)


def solution(mesh):
    return jax.shard_map(
        shards,
        mesh=mesh,
        in_specs=(
            P("row", "col", None, None, None),
            P(),
            P("row", "col", None, None, None, None),
            P(),
        ),
        out_specs=P("row", "col"),
        check_vma=False,
    )
```
